256 devices in a mesh: gx: 16 (over y, z_hi), gy: 16 (over x, z_lo, core).
Axes of the slice: x: 4, y: 4, z: 8 (z_hi: 4, z_lo: 2; z = z_hi * 2 + z_lo), core: 2. Of those that a mesh axis runs over, the one named last changes fastest.
Arguments:
- charges: float32 [512, 512, 256], P('gx', 'gy'), may hold values from -6 to 6
- kernel_taps: float32 [3, 3, 21], replicated, may hold values from -1.08 to 1.08
Outputs:
- potential: float32 [512, 512, 256], P('gx', 'gy')
The draws below stay inside these ranges and needn't reach their ends.
All inputs are finite; a program needn't handle non-finite values.
Results may differ from the reference program's by a relative error of at most 0.035.
Values sent between devices are 32-bit elements; how exact they have to be, the bound alone decides.
No kernel may reach another device: no remote copies, remote signals or barrier semaphores. Data moves between devices by JAX's collectives and lax.ppermute only.
A program may use at most 128 MiB of HBM per device.

```python
import jax
import jax.numpy as jnp
from jax import lax

NZ = 256
TERMS = 3
LEVELS = 3
NX = 512
NY = 512
TAPS = 21


def shard_levels(key, shape, pieces, least, high):
    factor_of = 1.0
    for position, shards_of in pieces:
        heights = jax.random.uniform(jax.random.fold_in(jax.random.fold_in(key, 6), position), (shards_of,), jnp.float32, least / len(pieces), high / len(pieces))
        factor_of = factor_of * jnp.repeat(jnp.exp(heights), shape[position] // shards_of).reshape((-1,) + (1,) * (len(shape) - 1 - position))
    return factor_of


def bell_draw(key, dims, scale, bound, cuts=(), held_as=jnp.bfloat16):
    values = scale * jax.random.normal(key, dims, jnp.float32)
    if cuts:
        values = values * shard_levels(key, dims, cuts, -0.22, 0.18)
    return jnp.clip(values, -bound, bound).astype(held_as)


def setup_inputs(seed: int = 0) -> dict:
    key_of = jax.random.split(jax.random.key(seed), 3)
    charges = bell_draw(key_of[0], (NX, NY, NZ), 1.0, 6.0, ((0, 16), (1, 16)), jnp.float32)
    kernel_taps = bell_draw(key_of[1], (LEVELS, TERMS, TAPS), 0.18, 1.08, (), jnp.float32)
    return dict(charges=charges, kernel_taps=kernel_taps)


SPLINE = (0.125, 0.5, 0.75, 0.5, 0.125)


def correlate(values, taps, along):
    length = values.shape[along]
    tap_count = taps.shape[0]
    radius = tap_count // 2
    wrapped = (jnp.arange(tap_count, dtype=jnp.int32) - radius) % length
    onehot = (wrapped[:, None] == jnp.arange(length, dtype=jnp.int32)[None, :]).astype(jnp.float32)
    profile = jnp.dot(taps, onehot, preferred_element_type=jnp.float32, precision=lax.Precision.HIGHEST)
    shaped = [1] * values.ndim
    shaped[along] = -1
    spectrum = jnp.fft.rfft(values, axis=along) * jnp.conj(jnp.fft.rfft(profile)).reshape(shaped)
    return jnp.fft.irfft(spectrum, n=length, axis=along)


def convolve(values, taps):
    summed = jnp.zeros(values.shape, jnp.float32)
    for member in range(taps.shape[0]):
        sectioned = correlate(values, taps[member], 0)
        sectioned = correlate(sectioned, taps[member], 1)
        summed = summed + correlate(sectioned, taps[member], 2)
    return summed


def restrict(values, along):
    length = values.shape[along]
    summed = jnp.zeros(values.shape, jnp.float32)
    for shift_by in range(-2, 3):
        summed = summed + SPLINE[shift_by + 2] * jnp.roll(values, -shift_by, along)
    return lax.slice_in_dim(summed, 0, length, 2, along)


def prolong(values, along):
    blank = jnp.zeros(values.shape, jnp.float32)
    shaped = list(values.shape)
    shaped[along] = 2 * shaped[along]
    spread = jnp.stack([values, blank], axis=along + 1).reshape(shaped)
    summed = jnp.zeros(spread.shape, jnp.float32)
    for shift_by in range(-2, 3):
        summed = summed + SPLINE[shift_by + 2] * jnp.roll(spread, shift_by, along)
    return summed


def restrict_grid(values):
    return restrict(restrict(restrict(values, 0), 1), 2)


def prolong_grid(values):
    return prolong(prolong(prolong(values, 0), 1), 2)


def reference(charges, kernel_taps):
    coarse = restrict_grid(charges)
    summit = restrict_grid(coarse)
    top_field = convolve(summit, kernel_taps[2])
    middle = convolve(coarse, kernel_taps[1]) + prolong_grid(top_field)
    return convolve(charges, kernel_taps[0]) + prolong_grid(middle)
```

```python
import jax
import jax.numpy as jnp
from jax import lax
from jax.sharding import PartitionSpec as P

SPLINE = (0.125, 0.5, 0.75, 0.5, 0.125)


def padded_2(x, sides, width):
    for axis, dim in sides:
        peers, length = (lax.axis_size(axis), x.shape[dim])
        up = [(i, (i + 1) % peers) for i in range(peers)]
        down = [(j, i) for i, j in up]
        last = lax.slice_in_dim(x, length - width, length, axis=dim)
        first = lax.slice_in_dim(x, 0, width, axis=dim)
        before = lax.ppermute(last, axis, up)
        after = lax.ppermute(first, axis, down)
        x = jnp.concatenate([before, x, after], axis=dim)
    return x


def from_everyone(x, axis):
    peers = lax.axis_size(axis)
    return lax.all_to_all(jnp.broadcast_to(x[None], (peers, *x.shape)), axis, 0, 0, tiled=True)


def in_order(pieces, dim):
    shape = list(pieces.shape[1:])
    shape[dim] *= pieces.shape[0]
    return jnp.moveaxis(pieces, 0, dim).reshape(shape)


def gathered_copies(x, axis, dim):
    pieces = from_everyone(x, axis)
    return in_order(pieces, dim)


def contract(formula, left, right):
    return jnp.einsum(formula, left, right, precision=lax.Precision.HIGHEST)


def grid_ids(count_rows, count_cols):
    row_ids = lax.broadcasted_iota(jnp.int32, (count_rows, count_cols), 0)
    col_ids = lax.broadcasted_iota(jnp.int32, (count_rows, count_cols), 1)
    return (row_ids, col_ids)


def spline_table(offsets):
    table = jnp.zeros(offsets.shape, jnp.float32)
    for position in range(5):
        table = table + SPLINE[position] * (offsets == position).astype(jnp.float32)
    return table


def band_taps(taps, count_rows, count_cols):
    row_ids, col_ids = grid_ids(count_rows, count_cols)
    offsets = col_ids - row_ids
    tap_count = taps.shape[1]
    table = jnp.zeros((taps.shape[0], count_rows, count_cols), jnp.float32)
    for k in range(tap_count):
        table = jnp.where((offsets == k)[None], taps[:, k, None, None], table)
    return table


def cycle_taps(taps, length):
    tap_count = taps.shape[1]
    radius = tap_count // 2
    row_ids, col_ids = grid_ids(length, length)
    offsets = (col_ids - row_ids + radius) % length
    table = jnp.zeros((taps.shape[0], length, length), jnp.float32)
    for k in range(tap_count):
        table = jnp.where((offsets == k % length)[None], taps[:, k, None, None], table)
    return table


def restrict_band(count_rows, count_cols, margin):
    row_ids, col_ids = grid_ids(count_rows, count_cols)
    return spline_table(col_ids - margin - 2 * row_ids + 2)


def restrict_cycle(length):
    row_ids, col_ids = grid_ids(length // 2, length)
    return spline_table((col_ids - 2 * row_ids + 2) % length)


def prolong_band(count_rows, count_cols):
    row_ids, col_ids = grid_ids(count_rows, count_cols)
    return spline_table(row_ids - 2 * col_ids + 4)


def prolong_cycle(count_rows, coarse_len, offset):
    row_ids, col_ids = grid_ids(count_rows, coarse_len)
    return spline_table((offset + row_ids - 2 * col_ids + 2) % (2 * coarse_len))


def body(charges, kernel_taps):
    radius = kernel_taps.shape[2] // 2
    margin = radius + 1
    term_count = kernel_taps.shape[1]
    rows_x, rows_y, cells_z = charges.shape
    half_x, half_y, half_z = (rows_x // 2, rows_y // 2, cells_z // 2)
    quarter_x, quarter_z = (rows_x // 4, cells_z // 4)
    count_x = lax.axis_size("gx")
    count_y = lax.axis_size("gy")
    wide_y = rows_y * count_y
    quarter_y = wide_y // 4
    taps_fine, taps_middle, taps_top = (kernel_taps[0], kernel_taps[1], kernel_taps[2])
    padded = padded_2(charges, (("gx", 0), ("gy", 1)), radius)
    across_x = band_taps(taps_fine, rows_x, rows_x + 2 * radius)
    across_y = band_taps(taps_fine, rows_y, rows_y + 2 * radius)
    across_z = cycle_taps(taps_fine, cells_z)
    direct_fine = jnp.zeros(charges.shape, jnp.float32)
    for member in range(term_count):
        sectioned = contract("mc,cyz->myz", across_x[member], padded)
        sectioned = contract("nc,mcz->mnz", across_y[member], sectioned)
        direct_fine = direct_fine + contract("mnz,wz->mnw", sectioned, across_z[member])
    coarse = contract("mc,cyz->myz", restrict_band(half_x, rows_x + 2 * radius, radius), padded)
    coarse = contract("nc,mcz->mnz", restrict_band(half_y, rows_y + 2 * radius, radius), coarse)
    coarse = contract("mnz,wz->mnw", coarse, restrict_cycle(cells_z))
    middle_x = band_taps(taps_middle, half_x + 2, half_x + 2 * margin)
    middle_z = cycle_taps(taps_middle, half_z)
    down_x = restrict_band(quarter_x, half_x + 2 * margin, margin)
    down_z = restrict_cycle(half_z)
    up_z = prolong_cycle(half_z, quarter_z, 0)
    rimmed = padded_2(coarse, (("gx", 0), ("gy", 1)), margin)
    middle_y = band_taps(taps_middle, half_y + 2, half_y + 2 * margin)
    direct_middle = jnp.zeros((half_x + 2, half_y + 2, half_z), jnp.float32)
    for member in range(term_count):
        sectioned = contract("mc,cyz->myz", middle_x[member], rimmed)
        sectioned = contract("nc,mcz->mnz", middle_y[member], sectioned)
        direct_middle = direct_middle + contract("mnz,wz->mnw", sectioned, middle_z[member])
    summit = contract("mc,cyz->myz", down_x, rimmed)
    summit = contract(
        "nc,mcz->mnz", restrict_band(half_y // 2, half_y + 2 * margin, margin), summit
    )
    summit = contract("mnz,wz->mnw", summit, down_z)
    lift_y = prolong_cycle(half_y + 2, quarter_y, lax.axis_index("gy") * half_y - 1)
    spread_y = prolong_band(rows_y, half_y + 2)
    top_y = cycle_taps(taps_top, quarter_y)
    top_z = cycle_taps(taps_top, quarter_z)
    full_x = quarter_x * count_x
    top_x = cycle_taps(taps_top, full_x)
    along_z = jnp.stack(
        [contract("mnz,wz->mnw", summit, top_z[member]) for member in range(term_count)]
    )
    portion = lax.all_to_all(along_z, "gy", split_axis=3, concat_axis=2, tiled=True)
    turned_yz = jnp.stack(
        [contract("nc,mcw->mnw", top_y[member], portion[member]) for member in range(term_count)]
    )
    up_x = prolong_cycle(2 * full_x, full_x, 0)
    portion = lax.all_to_all(turned_yz, "gx", split_axis=2, concat_axis=1, tiled=True)
    result = jnp.zeros(portion.shape[1:], jnp.float32)
    for member in range(term_count):
        result = result + contract("mc,cnw->mnw", top_x[member], portion[member])
    refined = contract("jm,mnw->jnw", up_x, result)
    rest_shape = refined.shape[1:]
    blocks = refined.reshape((count_x, half_x) + rest_shape)
    leading = jnp.roll(refined, 1, 0).reshape((count_x, half_x) + rest_shape)[:, :1]
    trailing = jnp.roll(refined, -1, 0).reshape((count_x, half_x) + rest_shape)[:, -1:]
    windows = jnp.concatenate([leading, blocks, trailing], axis=1)
    back_rows = lax.all_to_all(windows, "gx", split_axis=0, concat_axis=2, tiled=True)[0]
    returned = gathered_copies(back_rows, "gy", 2)
    lifted = contract("jn,mnw->mjw", lift_y, returned)
    lifted = contract("mjz,wz->mjw", lifted, up_z)
    middle = direct_middle + lifted
    refined = contract("jm,myz->jyz", prolong_band(rows_x, half_x + 2), middle)
    refined = contract("jn,mnz->mjz", spread_y, refined)
    refined = contract("mjz,wz->mjw", refined, prolong_cycle(cells_z, half_z, 0))
    return direct_fine + refined


def solution(mesh):
    return jax.shard_map(
        body,
        mesh=mesh,
        in_specs=(P("gx", "gy", None), P()),
        out_specs=P("gx", "gy", None),
        check_vma=False,
    )
```

```python
import functools

import jax
import jax.numpy as jnp
import numpy as np
from jax import lax
from jax.experimental import pallas as pl
from jax.experimental.pallas import tpu as pltpu
from jax.sharding import PartitionSpec as P

SPLINE = (0.125, 0.5, 0.75, 0.5, 0.125)
RADIUS = 10
TAPS = 21
BF = jnp.bfloat16
F32 = jnp.float32
VMEM_LIMIT = 48 * 1024 * 1024


def weight(offset):
    return SPLINE[offset + 2] if -2 <= offset <= 2 else 0.0


def restrict_table(coarse, fine):
    return np.array([[weight(f - 2 * c) for f in fine] for c in coarse], np.float32)


def prolong_cyclic(coarse_len):
    table = np.zeros((coarse_len, 2 * coarse_len), np.float32)
    for c in range(coarse_len):
        for k in range(-2, 3):
            table[c, (2 * c + k) % (2 * coarse_len)] += weight(k)
    return table


def tap_basis(rows, positions):
    basis = np.zeros((TAPS, len(rows), len(positions)), np.float32)
    for r, row in enumerate(rows):
        for c, position in enumerate(positions):
            if position is not None and 0 <= position - row + RADIUS < TAPS:
                basis[position - row + RADIUS, r, c] = 1.0
    return basis


def tables():
    ry = np.zeros((24, 32), np.float32)
    ry[:18] = restrict_table(range(-1, 17), range(32))
    rz = prolong_cyclic(128).T
    ry2 = np.zeros((16, 24), np.float32)
    ry2[:11, :18] = restrict_table(range(-1, 10), range(-1, 17))
    half = prolong_cyclic(64).T
    rz2 = np.zeros((256, 128), np.float32)
    rz2[:128, :64] = half
    rz2[128:, 64:] = half
    none = [None] * 6
    place0 = list(range(32)) + list(range(-10, 0)) + none + list(range(32, 42)) + none
    offsets0 = np.full((32, 64), -1, np.int32)
    for n in range(32):
        for c, position in enumerate(place0):
            if position is not None:
                offsets0[n, c] = position - n + RADIUS
    offsets0 = np.tile(offsets0, (1, 3))
    place1 = list(range(-11, 1)) + list(range(-1, 17)) + list(range(15, 27)) + none
    lift1 = restrict_table(range(-1, 17), range(32)).T
    basis1 = np.einsum("nm,dmc->dnc", lift1, tap_basis(range(-1, 17), place1))
    place2 = (
        list(range(-1, 10)) + [None] * 5 + list(range(-9, 2)) + list(range(7, 18))
        + list(range(-11, -6)) + list(range(15, 20))
    )
    lift2 = lift1 @ restrict_table(range(-1, 10), range(-1, 17)).T
    basis2 = np.einsum("nm,dmc->dnc", lift2, tap_basis(range(-1, 10), place2))
    basis1 = np.tile(basis1, (1, 1, 3))
    basis2 = np.tile(basis2, (1, 1, 3))
    up2 = prolong_cyclic(64)
    up1 = prolong_cyclic(128)
    return ry, rz, ry2, rz2, offsets0, basis1, basis2, up2, up1


def halves(x):
    high = x.astype(BF)
    return high, (x - high.astype(F32)).astype(BF)


def dot(a, b):
    return jnp.dot(a, b, preferred_element_type=F32)


def spline_sum(read, center, low, high):
    total = None
    for k in range(-2, 3):
        if low <= 2 * center + k <= high:
            term = SPLINE[k + 2] * read(2 * center + k)
            total = term if total is None else total + term
    return total


def matrices_kernel(taps, offsets0, basis1, basis2, up2, y0, y1, y2, z0h, z0l, z1h, z1l, z2h, z2l):
    def cycle(level, member, length):
        rows = lax.broadcasted_iota(jnp.int32, (length, length), 0)
        cols = lax.broadcasted_iota(jnp.int32, (length, length), 1)
        offsets = (rows - cols + RADIUS) & (length - 1)
        table = jnp.zeros((length, length), F32)
        for k in range(TAPS):
            table = jnp.where(offsets == k, taps[level, member * TAPS + k], table)
        return table

    for member in range(3):
        rows = pl.ds(32 * member, 32)
        table = jnp.zeros((32, 192), F32)
        for k in range(TAPS):
            table = jnp.where(offsets0[...] == k, taps[0, member * TAPS + k], table)
        high, low = halves(table)
        lanes = lax.broadcasted_iota(jnp.int32, (32, 192), 1)
        y0[rows] = jnp.where(lanes < 128, high.astype(F32), low.astype(F32)).astype(BF)
        lanes = lax.broadcasted_iota(jnp.int32, (32, 144), 1)
        for level, basis, out in ((1, basis1, y1), (2, basis2, y2)):
            table = jnp.zeros((32, 144), F32)
            for k in range(TAPS):
                table = table + taps[level, member * TAPS + k] * basis[k]
            high, low = halves(table)
            out[rows] = jnp.where(lanes < 96, high.astype(F32), low.astype(F32)).astype(BF)
        high, low = halves(cycle(0, member, 256))
        z0h[pl.ds(256 * member, 256)] = high
        z0l[pl.ds(256 * member, 256)] = low
        high, low = halves(cycle(1, member, 128))
        z1h[pl.ds(128 * member, 128)] = high
        z1l[pl.ds(128 * member, 128)] = low
        high, low = halves(cycle(2, member, 64))
        table = dot(high, up2[...]) + dot(low, up2[...])
        high, low = halves(table)
        z2h[pl.ds(128 * member, 64)] = high
        z2l[pl.ds(128 * member, 64)] = low
        z2h[pl.ds(128 * member + 64, 64)] = jnp.zeros((64, 128), BF)
        z2l[pl.ds(128 * member + 64, 64)] = jnp.zeros((64, 128), BF)


def restrict_kernel(c, ry, rz, ry2, rz2, l1, l2, up1, down1, two, s1, s2):
    for i in range(-1, 17):
        high, low = halves(spline_sum(lambda r: c[r], i, 0, 31))
        s1[i + 1] = dot(ry[...], high) + dot(ry[...], low)
    high, low = halves(s1[...].reshape(18 * 24, 256))
    l1[...] = (dot(high, rz[...]) + dot(low, rz[...])).reshape(18, 24, 128)
    for i in range(-1, 10):
        high, low = halves(spline_sum(lambda r: l1[r + 1], i, -1, 16))
        s2[i + 1] = dot(ry2[...], high) + dot(ry2[...], low)
    s2[11] = jnp.zeros((16, 128), F32)
    first = s2[pl.ds(0, 6)].reshape(96, 128)
    second = s2[pl.ds(6, 6)].reshape(96, 128)
    total = jnp.zeros((96, 128), F32)
    for part, rows in ((first, pl.ds(0, 128)), (second, pl.ds(128, 128))):
        high, low = halves(part)
        total = total + dot(high, rz2[rows]) + dot(low, rz2[rows])
    total = total.reshape(6, 16, 128)
    l2[...] = total
    up1[pl.ds(64, 8)] = jnp.zeros((8, 128), F32)
    down1[pl.ds(64, 8)] = jnp.zeros((8, 128), F32)
    two[pl.ds(48, 8)] = jnp.zeros((8, 128), F32)
    for j in range(6):
        up1[pl.ds(11 * j, 11)] = total[j, :11]
        down1[pl.ds(11 * j, 11)] = total[j, :11]
        if j < 5:
            two[pl.ds(11 * j, 11)] = total[j, :11]
    for r in range(12):
        up1[pl.ds(72 + 18 * r, 18)] = l1[6 + r, :18]
        down1[pl.ds(72 + 18 * r, 18)] = l1[r, :18]


def face_kernel(c, before, after, up, down):
    for i in range(52):
        read = before if i < 10 else c if i < 42 else after
        row = i if i < 10 else i - 10 if i < 42 else i - 42
        up[pl.ds(10 * i, 10)] = read[row, 22:32]
        down[pl.ds(10 * i, 10)] = read[row, 0:10]
    up[pl.ds(520, 8)] = jnp.zeros((8, 256), F32)
    down[pl.ds(520, 8)] = jnp.zeros((8, 256), F32)


def gather_x_kernel(l1, l2, left, right, left2, right2, l1x, l2x, up1, down1, up2, down2):
    for i in range(38):
        if i < 12:
            l1x[i, :18] = left[pl.ds(72 + 18 * i, 18)]
            l1x[i, pl.ds(18, 6)] = jnp.zeros((6, 128), F32)
        elif i >= 26:
            l1x[i, :18] = right[pl.ds(72 + 18 * (i - 26), 18)]
            l1x[i, pl.ds(18, 6)] = jnp.zeros((6, 128), F32)
        if 10 <= i < 12 or 26 <= i < 28:
            l1x[i] = l1x[i] + l1[i - 10]
        elif 12 <= i < 26:
            l1x[i] = l1[i - 10]
    lanes = lax.broadcasted_iota(jnp.int32, (11, 128), 1)
    lower = lanes < 64
    rolled = lambda x: pltpu.roll(x, 64, 1)
    for j in range(16):
        low = []
        high = []
        if j < 5:
            low.append(rolled(left2[pl.ds(11 * j, 11)]))
        if 2 <= j < 8:
            low.append(left[pl.ds(11 * (j - 2), 11)])
        if 8 <= j < 13:
            low.append(rolled(left[pl.ds(11 * (j - 8), 11)]))
        if j >= 10:
            low.append(l2[j - 10, :11])
        if j < 5:
            high.append(l2[j, :11])
        if 2 <= j < 8:
            high.append(rolled(right[pl.ds(11 * (j - 2), 11)]))
        if 8 <= j < 13:
            high.append(right[pl.ds(11 * (j - 8), 11)])
        if 10 <= j < 15:
            high.append(rolled(right2[pl.ds(11 * (j - 10), 11)]))
        row = jnp.where(lower, sum(low, jnp.zeros((11, 128), F32)), sum(high, jnp.zeros((11, 128), F32)))
        l2x[j, :11] = row
        l2x[j, pl.ds(11, 5)] = jnp.zeros((5, 128), F32)
        up1[pl.ds(11 * j, 11)] = row
        down1[pl.ds(11 * j, 11)] = row
        up2[pl.ds(5 * j, 5)] = row[6:11]
        down2[pl.ds(5 * j, 5)] = row[0:5]
    for i in range(38):
        up1[pl.ds(176 + 12 * i, 12)] = l1x[i, 6:18]
        down1[pl.ds(176 + 12 * i, 12)] = l1x[i, 0:12]


def upper_kernel(taps, l1x, l2x, left, right, left2, right2, y1, y2, z1h, z1l, z2h, z2l, out,
                 f1, f2, v1, v2, w1, w2, mid):
    for i in range(38):
        f1[i, pl.ds(0, 12)] = left[pl.ds(176 + 12 * i, 12)]
        f1[i, pl.ds(12, 18)] = l1x[i, :18]
        f1[i, pl.ds(30, 12)] = right[pl.ds(176 + 12 * i, 12)]
        f1[i, pl.ds(42, 6)] = jnp.zeros((6, 128), F32)
    for j in range(16):
        f2[j, pl.ds(0, 16)] = l2x[j]
        f2[j, pl.ds(16, 11)] = left[pl.ds(11 * j, 11)]
        f2[j, pl.ds(27, 11)] = right[pl.ds(11 * j, 11)]
        f2[j, pl.ds(38, 5)] = left2[pl.ds(5 * j, 5)]
        f2[j, pl.ds(43, 5)] = right2[pl.ds(5 * j, 5)]

    @pl.loop(0, 38, unroll=2)
    def _(i):
        high, low = halves(f1[i])
        v1[i] = dot(y1[...], jnp.concatenate([high, low, high], 0))

    @pl.loop(0, 16, unroll=2)
    def _(j):
        high, low = halves(f2[j])
        v = dot(y2[...], jnp.concatenate([high, low, high], 0))
        v2[j] = v
        v2[16 + j] = pltpu.roll(v, 64, 1)

    def correlate_x(level, v, w, count, g):
        member = g // 4
        rows = pl.ds(pl.multiple_of(8 * g, 8), 8)
        scale = [taps[level, member * TAPS + k] for k in range(TAPS)]
        for base in range(0, count, 9 if count == 18 else 11):
            many = 9 if count == 18 else 11
            sums = [None] * many
            for i in range(base, base + many + TAPS - 1):
                value = v[i, rows]
                for m in range(many):
                    k = i - base - m
                    if 0 <= k < TAPS:
                        term = scale[k] * value
                        sums[m] = term if sums[m] is None else sums[m] + term
            for m in range(many):
                w[base + m, rows] = sums[m]

    @pl.loop(0, 12)
    def _(g):
        correlate_x(1, v1, w1, 18, g)
        correlate_x(2, v2, w2, 11, g)

    def correlate_z(w, count, high_table, low_table):
        total = jnp.zeros((count * 32, 128), F32)
        for member in range(3):
            high, low = halves(w[:, pl.ds(32 * member, 32)].reshape(count * 32, 128))
            rows = pl.ds(128 * member, 128)
            total = total + dot(high, high_table[rows]) + dot(low, high_table[rows]) + dot(high, low_table[rows])
        return total.reshape(count, 32, 128)

    v2[pl.ds(0, 11), pl.ds(0, 32)] = correlate_z(w2, 11, z2h, z2l)
    mid[...] = correlate_z(w1, 18, z1h, z1l)
    top = lambda i: v2[i + 1, pl.ds(0, 32)]
    for a in range(-1, 9):
        if a >= 0:
            mid[2 * a + 1] = mid[2 * a + 1] + (0.75 * top(a) + 0.125 * (top(a - 1) + top(a + 1)))
        if a < 8:
            mid[2 * a + 2] = mid[2 * a + 2] + 0.5 * (top(a) + top(a + 1))
    for a in range(16):
        out[2 * a] = 0.75 * mid[a + 1] + 0.125 * (mid[a] + mid[a + 2])
        out[2 * a + 1] = 0.5 * (mid[a + 1] + mid[a + 2])


def finest_kernel(taps, c, before, after, left, right, middle, y0, z0h, z0l, up1, out, v, wh, wl):
    def section(own, i, base, at):
        b = left[pl.ds(base, 48)][10 * at:10 * at + 16]
        a = right[pl.ds(base, 48)][10 * at:10 * at + 16]
        high, low = halves(jnp.concatenate([own, b, a], 0))
        v[i] = dot(y0[...], jnp.concatenate([high, low, high], 0))

    for i in range(10):
        section(before[i], i, 40 * (i // 4), i % 4)
    for i in (10, 11):
        section(c[i - 10], i, 40 * (i // 4), i % 4)

    @pl.loop(3, 10)
    def _(q):
        base = pl.multiple_of(40 * q, 8)
        for at in range(4):
            i = 4 * q + at
            section(c[i - 10], i, base, at)

    for i in (40, 41):
        section(c[i - 10], i, 40 * (i // 4), i % 4)
    for i in range(42, 52):
        section(after[i - 42], i, 40 * (i // 4), i % 4)

    @pl.loop(0, 4)
    def _(g):
        for member in range(3):
            rows = pl.ds(pl.multiple_of(32 * member + 8 * g, 8), 8)
            scale = [taps[0, member * TAPS + k] for k in range(TAPS)]
            for h in range(2):
                lanes = pl.ds(128 * h, 128)
                for base in range(0, 32, 8):
                    sums = [None] * 8
                    for i in range(base, base + 8 + TAPS - 1):
                        value = v[i, rows, lanes]
                        for m in range(8):
                            k = i - base - m
                            if 0 <= k < TAPS:
                                term = scale[k] * value
                                sums[m] = term if sums[m] is None else sums[m] + term
                    for m in range(0, 8, 2):
                        high, low = halves(jnp.concatenate([sums[m], sums[m + 1]], 0))
                        at = (pl.ds(8 * (base + m), 16), pl.ds(256 * member + 128 * h, 128))
                        wh[at] = high
                        wl[at] = low
        cols = pl.ds(pl.multiple_of(8 * g, 8), 8)
        total = dot(wh[...], z0h[...]) + dot(wl[...], z0h[...]) + dot(wh[...], z0l[...])
        high, low = halves(middle[:, cols].reshape(256, 128))
        total = total + dot(high, up1[...]) + dot(low, up1[...])
        out[:, cols] = total.reshape(32, 8, 256)


def call(kernel, outs, scratch=(), scalars=0, count=0, flops=0, moved=0, name=None):
    vmem = pl.BlockSpec(memory_space=pltpu.VMEM)
    smem = pl.BlockSpec(memory_space=pltpu.SMEM)
    shapes = [jax.ShapeDtypeStruct(*o) for o in outs]
    return pl.pallas_call(
        kernel,
        out_shape=shapes,
        in_specs=[smem] * scalars + [vmem] * (count - scalars),
        out_specs=[vmem] * len(shapes),
        scratch_shapes=[pltpu.VMEM(*s) for s in scratch],
        compiler_params=pltpu.CompilerParams(vmem_limit_bytes=VMEM_LIMIT),
        cost_estimate=pl.CostEstimate(flops=flops, bytes_accessed=moved, transcendentals=0),
        name=name,
    )


def shift(x, axis, by):
    n = lax.axis_size(axis)
    return lax.ppermute(x, axis, [(i, (i + by) % n) for i in range(n)])


def body(charges, kernel_taps):
    ry, rz, ry2, rz2, offsets0, basis1, basis2, up2, up1 = tables()
    taps = kernel_taps.reshape(3, 63)
    b16 = lambda x: jnp.asarray(x, BF)
    before = shift(charges[22:], "gx", 1)
    after = shift(charges[:10], "gx", -1)
    l1, l2, s_up, s_down, s_two = call(
        restrict_kernel,
        [((18, 24, 128), F32), ((6, 16, 128), F32), ((288, 128), F32), ((288, 128), F32), ((56, 128), F32)],
        [((18, 24, 256), F32), ((12, 16, 128), F32)], 0, 5, 10**8, 2 * 10**6, name="restrict",
    )(charges, b16(ry), b16(rz), b16(ry2), b16(rz2))
    x_left = shift(s_up, "gx", 1)
    x_right = shift(s_down, "gx", -1)
    x_left2 = shift(s_two, "gx", 2)
    x_right2 = shift(s_two, "gx", -2)
    y0, y1, y2, z0h, z0l, z1h, z1l, z2h, z2l = call(
        matrices_kernel,
        [((96, 192), BF), ((96, 144), BF), ((96, 144), BF), ((768, 256), BF), ((768, 256), BF),
         ((384, 128), BF), ((384, 128), BF), ((384, 128), BF), ((384, 128), BF)],
        [], 1, 5, 10**8, 4 * 10**6, name="matrices",
    )(taps, jnp.asarray(offsets0), jnp.asarray(basis1), jnp.asarray(basis2), b16(up2))
    l1x, l2x, t_up, t_down, t_up2, t_down2 = call(
        gather_x_kernel,
        [((38, 24, 128), F32), ((16, 16, 128), F32), ((632, 128), F32), ((632, 128), F32),
         ((80, 128), F32), ((80, 128), F32)],
        [], 0, 6, 10**6, 2 * 10**6, name="gather_x",
    )(l1, l2, x_left, x_right, x_left2, x_right2)
    f_up, f_down = call(
        face_kernel, [((528, 256), F32), ((528, 256), F32)], [], 0, 3, 10**6, 3 * 10**6, name="faces",
    )(charges, before, after)
    left = shift(f_up, "gy", 1)
    right = shift(f_down, "gy", -1)
    y_left = shift(t_up, "gy", 1)
    y_right = shift(t_down, "gy", -1)
    y_left2 = shift(t_up2, "gy", 2)
    y_right2 = shift(t_down2, "gy", -2)
    middle, = call(
        upper_kernel, [((32, 32, 128), F32)],
        [((38, 48, 128), F32), ((16, 48, 128), F32), ((38, 96, 128), F32), ((32, 96, 128), F32),
         ((18, 96, 128), F32), ((11, 96, 128), F32), ((18, 32, 128), F32)],
        1, 13, 4 * 10**8, 4 * 10**6, name="upper",
    )(taps, l1x, l2x, y_left, y_right, y_left2, y_right2, y1, y2, z1h, z1l, z2h, z2l)
    result, = call(
        finest_kernel, [((32, 32, 256), F32)],
        [((52, 96, 256), F32), ((256, 768), BF), ((256, 768), BF)],
        1, 11, 2 * 10**9, 6 * 10**6, name="finest",
    )(taps, charges, before, after, left, right, middle, y0, z0h, z0l, b16(up1))
    return result


def solution(mesh):
    return jax.shard_map(
        body,
        mesh=mesh,
        in_specs=(P("gx", "gy", None), P()),
        out_specs=P("gx", "gy", None),
        check_vma=False,
    )
```

```python
import functools

import jax
import jax.numpy as jnp
import numpy as np
from jax import lax
from jax.experimental import pallas as pl
from jax.experimental.pallas import tpu as pltpu
from jax.sharding import PartitionSpec as P

SPLINE = (0.125, 0.5, 0.75, 0.5, 0.125)
RADIUS = 10
TAPS = 21
BF = jnp.bfloat16
F32 = jnp.float32
VMEM_LIMIT = 48 * 1024 * 1024


def weight(offset):
    return SPLINE[offset + 2] if -2 <= offset <= 2 else 0.0


def restrict_table(coarse, fine):
    return np.array([[weight(f - 2 * c) for f in fine] for c in coarse], np.float32)


def prolong_cyclic(coarse_len):
    table = np.zeros((coarse_len, 2 * coarse_len), np.float32)
    for c in range(coarse_len):
        for k in range(-2, 3):
            table[c, (2 * c + k) % (2 * coarse_len)] += weight(k)
    return table


def tap_basis(rows, positions):
    basis = np.zeros((TAPS, len(rows), len(positions)), np.float32)
    for r, row in enumerate(rows):
        for c, position in enumerate(positions):
            if position is not None and 0 <= position - row + RADIUS < TAPS:
                basis[position - row + RADIUS, r, c] = 1.0
    return basis


def tables():
    none = [None] * 6
    place0 = list(range(32)) + list(range(-10, 0)) + none + list(range(32, 42)) + none
    offsets0 = np.full((32, 64), -1, np.int32)
    for n in range(32):
        for c, position in enumerate(place0):
            if position is not None:
                offsets0[n, c] = position - n + RADIUS
    offsets0 = np.tile(offsets0, (1, 3))
    place1 = list(range(-11, 1)) + list(range(-1, 17)) + list(range(15, 27)) + none
    lift1 = restrict_table(range(-1, 17), range(32)).T
    basis1 = np.einsum("nm,dmc->dnc", lift1, tap_basis(range(-1, 17), place1))
    place2 = (
        list(range(-1, 10)) + [None] * 5 + list(range(-9, 2)) + list(range(7, 18))
        + list(range(-11, -6)) + list(range(15, 20))
    )
    lift2 = lift1 @ restrict_table(range(-1, 10), range(-1, 17)).T
    basis2 = np.einsum("nm,dmc->dnc", lift2, tap_basis(range(-1, 10), place2))
    basis1 = np.tile(basis1, (1, 1, 3))
    basis2 = np.tile(basis2, (1, 1, 3))
    up2 = prolong_cyclic(64)
    up1 = prolong_cyclic(128)
    return offsets0, basis1, basis2, up2, up1


def halves(x):
    high = x.astype(BF)
    return high, (x - high.astype(F32)).astype(BF)


def dot(a, b):
    return jnp.dot(a, b, preferred_element_type=F32)


def spline_sum(read, center, low, high):
    total = None
    for k in range(-2, 3):
        if low <= 2 * center + k <= high:
            term = SPLINE[k + 2] * read(2 * center + k)
            total = term if total is None else total + term
    return total


def matrices_kernel(taps, offsets0, basis1, basis2, up2, y0, y1, y2, z0h, z0l, z1h, z1l, z2h, z2l):
    def cycle(level, member, length):
        rows = lax.broadcasted_iota(jnp.int32, (length, length), 0)
        cols = lax.broadcasted_iota(jnp.int32, (length, length), 1)
        offsets = (rows - cols + RADIUS) & (length - 1)
        table = jnp.zeros((length, length), F32)
        for k in range(TAPS):
            table = jnp.where(offsets == k, taps[level, member * TAPS + k], table)
        return table

    for member in range(3):
        rows = pl.ds(32 * member, 32)
        table = jnp.zeros((32, 192), F32)
        for k in range(TAPS):
            table = jnp.where(offsets0[...] == k, taps[0, member * TAPS + k], table)
        high, low = halves(table)
        lanes = lax.broadcasted_iota(jnp.int32, (32, 192), 1)
        y0[rows] = jnp.where(lanes < 128, high.astype(F32), low.astype(F32)).astype(BF)
        lanes = lax.broadcasted_iota(jnp.int32, (32, 144), 1)
        for level, basis, out in ((1, basis1, y1), (2, basis2, y2)):
            table = jnp.zeros((32, 144), F32)
            for k in range(TAPS):
                table = table + taps[level, member * TAPS + k] * basis[k]
            high, low = halves(table)
            out[rows] = jnp.where(lanes < 96, high.astype(F32), low.astype(F32)).astype(BF)
        high, low = halves(cycle(0, member, 256))
        z0h[pl.ds(256 * member, 256)] = high
        z0l[pl.ds(256 * member, 256)] = low
        high, low = halves(cycle(1, member, 128))
        z1h[pl.ds(128 * member, 128)] = high
        z1l[pl.ds(128 * member, 128)] = low
        high, low = halves(cycle(2, member, 64))
        table = dot(high, up2[...]) + dot(low, up2[...])
        high, low = halves(table)
        z2h[pl.ds(128 * member, 64)] = high
        z2l[pl.ds(128 * member, 64)] = low
        z2h[pl.ds(128 * member + 64, 64)] = jnp.zeros((64, 128), BF)
        z2l[pl.ds(128 * member + 64, 64)] = jnp.zeros((64, 128), BF)


def spline_iota(shape, offset, coarse_dim, fine_dim, keep=None):
    fine = lax.broadcasted_iota(jnp.int32, shape, fine_dim)
    coarse = lax.broadcasted_iota(jnp.int32, shape, coarse_dim)
    delta = fine - 2 * coarse + offset
    if keep is not None:
        delta = jnp.where(coarse < keep, delta, 99)
    return spline_of(delta)


def spline_of(delta):
    far = jnp.abs(delta)
    return jnp.where(far == 0, 0.75, jnp.where(far == 1, 0.5, jnp.where(far == 2, 0.125, 0.0)))


def cyclic_iota(shape, coarse_dim, fine_dim, fine_len):
    fine = lax.broadcasted_iota(jnp.int32, shape, fine_dim)
    coarse = lax.broadcasted_iota(jnp.int32, shape, coarse_dim)
    return spline_of(((fine - 2 * coarse + 2) & (fine_len - 1)) - 2)


def restrict_kernel(c, l1, l2, up1, down1, face_up, face_down, s1, s2):
    for i in range(32):
        face_up[pl.ds(10 * i, 10)] = c[i, 22:32]
        face_down[pl.ds(10 * i, 10)] = c[i, 0:10]
    face_up[pl.ds(320, 8)] = jnp.zeros((8, 256), F32)
    face_down[pl.ds(320, 8)] = jnp.zeros((8, 256), F32)
    ry = spline_iota((24, 32), 2, 0, 1, 18).astype(BF)
    for i in range(-1, 17):
        high, low = halves(spline_sum(lambda r: c[r], i, 0, 31))
        s1[i + 1] = dot(ry, high) + dot(ry, low)
    rz = cyclic_iota((256, 128), 1, 0, 256).astype(BF)
    high, low = halves(s1[...].reshape(18 * 24, 256))
    l1[...] = (dot(high, rz) + dot(low, rz)).reshape(18, 24, 128)
    ry2 = spline_iota((16, 24), 1, 0, 1, 11).astype(BF)
    for i in range(-1, 10):
        high, low = halves(spline_sum(lambda r: l1[r + 1], i, -1, 16))
        s2[i + 1] = dot(ry2, high) + dot(ry2, low)
    s2[11] = jnp.zeros((16, 128), F32)
    near = s2[pl.ds(0, 6)].reshape(96, 128)
    far = s2[pl.ds(6, 6)].reshape(96, 128)
    lanes = lax.broadcasted_iota(jnp.int32, (128, 128), 1)
    both = spline_of(((lax.broadcasted_iota(jnp.int32, (128, 128), 0) - 2 * (lanes & 63) + 2) & 127) - 2)
    total = jnp.zeros((96, 128), F32)
    for part, upper in ((near, False), (far, True)):
        weights = jnp.where((lanes >= 64) == upper, both, 0.0).astype(BF)
        high, low = halves(part)
        total = total + dot(high, weights) + dot(low, weights)
    total = total.reshape(6, 16, 128)
    l2[...] = total
    up1[pl.ds(64, 8)] = jnp.zeros((8, 128), F32)
    down1[pl.ds(64, 8)] = jnp.zeros((8, 128), F32)
    for j in range(6):
        up1[pl.ds(11 * j, 11)] = total[j, :11]
        down1[pl.ds(11 * j, 11)] = total[j, :11]
    for r in range(12):
        up1[pl.ds(72 + 18 * r, 18)] = l1[6 + r, :18]
        down1[pl.ds(72 + 18 * r, 18)] = l1[r, :18]


def paired(base, count, j):
    return (pl.ds(base + count * (j // 2), count), pl.ds(128 * (j % 2), 128))


def face_x_kernel(c, left, right, up, down):
    for r in range(10):
        up[pl.ds(32 * r, 32)] = c[22 + r]
        down[pl.ds(32 * r, 32)] = c[r]
    for j in range(5):
        up[paired(320, 11, j)] = left[pl.ds(11 * j, 11)]
        down[paired(320, 11, j)] = right[pl.ds(11 * j, 11)]


def gather_x_kernel(before, after, l1, l2, left, right, l1x, l2x, up, down):
    for i in range(20):
        row = before[pl.ds(32 * i, 32)] if i < 10 else after[pl.ds(32 * (i - 10), 32)]
        up[pl.ds(10 * i, 10)] = row[22:32]
        down[pl.ds(10 * i, 10)] = row[0:10]
    up[pl.ds(200, 8)] = jnp.zeros((8, 256), F32)
    down[pl.ds(200, 8)] = jnp.zeros((8, 256), F32)
    for i in range(38):
        if i < 12:
            l1x[i, :18] = left[pl.ds(72 + 18 * i, 18)]
            l1x[i, pl.ds(18, 6)] = jnp.zeros((6, 128), F32)
        elif i >= 26:
            l1x[i, :18] = right[pl.ds(72 + 18 * (i - 26), 18)]
            l1x[i, pl.ds(18, 6)] = jnp.zeros((6, 128), F32)
        if 10 <= i < 12 or 26 <= i < 28:
            l1x[i] = l1x[i] + l1[i - 10]
        elif 12 <= i < 26:
            l1x[i] = l1[i - 10]
    lanes = lax.broadcasted_iota(jnp.int32, (11, 128), 1)
    lower = lanes < 64
    rolled = lambda x: pltpu.roll(x, 64, 1)
    for j in range(16):
        low = []
        high = []
        if j < 5:
            low.append(rolled(before[paired(320, 11, j)]))
        if 2 <= j < 8:
            low.append(left[pl.ds(11 * (j - 2), 11)])
        if 8 <= j < 13:
            low.append(rolled(left[pl.ds(11 * (j - 8), 11)]))
        if j >= 10:
            low.append(l2[j - 10, :11])
        if j < 5:
            high.append(l2[j, :11])
        if 2 <= j < 8:
            high.append(rolled(right[pl.ds(11 * (j - 2), 11)]))
        if 8 <= j < 13:
            high.append(right[pl.ds(11 * (j - 8), 11)])
        if 10 <= j < 15:
            high.append(rolled(after[paired(320, 11, j - 10)]))
        row = jnp.where(lower, sum(low, jnp.zeros((11, 128), F32)), sum(high, jnp.zeros((11, 128), F32)))
        l2x[j, :11] = row
        l2x[j, pl.ds(11, 5)] = jnp.zeros((5, 128), F32)
        up[paired(208, 11, j)] = row
        down[paired(208, 11, j)] = row
    for i in range(38):
        up[paired(296, 12, i)] = l1x[i, 6:18]
        down[paired(296, 12, i)] = l1x[i, 0:12]


def second_kernel(left, right, up, down):
    for j in range(16):
        rows, lanes = paired(208, 11, j)
        up[pl.ds(5 * j, 5)] = left[pl.ds(rows.start + 6, 5), lanes]
        down[pl.ds(5 * j, 5)] = right[pl.ds(rows.start, 5), lanes]


def upper_kernel(taps, l1x, l2x, left, right, left2, right2, y1, y2, z1h, z1l, z2h, z2l, up1, direct,
                 out, f1, f2, v1, v2, w1, w2, mid, fine):
    for i in range(38):
        f1[i, pl.ds(0, 12)] = left[paired(296, 12, i)]
        f1[i, pl.ds(12, 18)] = l1x[i, :18]
        f1[i, pl.ds(30, 12)] = right[paired(296, 12, i)]
        f1[i, pl.ds(42, 6)] = jnp.zeros((6, 128), F32)
    for j in range(16):
        f2[j, pl.ds(0, 16)] = l2x[j]
        f2[j, pl.ds(16, 11)] = left[paired(208, 11, j)]
        f2[j, pl.ds(27, 11)] = right[paired(208, 11, j)]
        f2[j, pl.ds(38, 5)] = left2[pl.ds(5 * j, 5)]
        f2[j, pl.ds(43, 5)] = right2[pl.ds(5 * j, 5)]

    @pl.loop(0, 38, unroll=2)
    def _(i):
        high, low = halves(f1[i])
        v1[i] = dot(y1[...], jnp.concatenate([high, low, high], 0))

    @pl.loop(0, 16, unroll=2)
    def _(j):
        high, low = halves(f2[j])
        v = dot(y2[...], jnp.concatenate([high, low, high], 0))
        v2[j] = v
        v2[16 + j] = pltpu.roll(v, 64, 1)

    def correlate_x(level, v, w, count, g):
        member = g // 4
        rows = pl.ds(pl.multiple_of(8 * g, 8), 8)
        scale = [taps[level, member * TAPS + k] for k in range(TAPS)]
        for base in range(0, count, 9 if count == 18 else 11):
            many = 9 if count == 18 else 11
            sums = [None] * many
            for i in range(base, base + many + TAPS - 1):
                value = v[i, rows]
                for m in range(many):
                    k = i - base - m
                    if 0 <= k < TAPS:
                        term = scale[k] * value
                        sums[m] = term if sums[m] is None else sums[m] + term
            for m in range(many):
                w[base + m, rows] = sums[m]

    @pl.loop(0, 12)
    def _(g):
        correlate_x(1, v1, w1, 18, g)
        correlate_x(2, v2, w2, 11, g)

    def correlate_z(w, count, high_table, low_table):
        total = jnp.zeros((count * 32, 128), F32)
        for member in range(3):
            high, low = halves(w[:, pl.ds(32 * member, 32)].reshape(count * 32, 128))
            rows = pl.ds(128 * member, 128)
            total = total + dot(high, high_table[rows]) + dot(low, high_table[rows]) + dot(high, low_table[rows])
        return total.reshape(count, 32, 128)

    v2[pl.ds(0, 11), pl.ds(0, 32)] = correlate_z(w2, 11, z2h, z2l)
    mid[...] = correlate_z(w1, 18, z1h, z1l)
    top = lambda i: v2[i + 1, pl.ds(0, 32)]
    for a in range(-1, 9):
        if a >= 0:
            mid[2 * a + 1] = mid[2 * a + 1] + (0.75 * top(a) + 0.125 * (top(a - 1) + top(a + 1)))
        if a < 8:
            mid[2 * a + 2] = mid[2 * a + 2] + 0.5 * (top(a) + top(a + 1))
    for a in range(16):
        fine[2 * a] = 0.75 * mid[a + 1] + 0.125 * (mid[a] + mid[a + 2])
        fine[2 * a + 1] = 0.5 * (mid[a + 1] + mid[a + 2])
    for q in range(4):
        rows = pl.ds(8 * q, 8)
        high, low = halves(fine[rows].reshape(256, 128))
        out[rows] = direct[rows] + (dot(high, up1[...]) + dot(low, up1[...])).reshape(8, 32, 256)


def section(table, own, left, right, base, at):
    b = left[pl.ds(base, 48)][10 * at:10 * at + 16]
    a = right[pl.ds(base, 48)][10 * at:10 * at + 16]
    high, low = halves(jnp.concatenate([own, b, a], 0))
    return dot(table[...], jnp.concatenate([high, low, high], 0))


def inner_kernel(taps, c, left, right, y0, w, v):
    @pl.loop(0, 8)
    def _(q):
        base = pl.multiple_of(40 * q, 8)
        for at in range(4):
            i = 4 * q + at
            v[i] = section(y0, c[i], left, right, base, at)

    @pl.loop(0, 4)
    def _(g):
        for member in range(3):
            rows = pl.ds(pl.multiple_of(32 * member + 8 * g, 8), 8)
            scale = [taps[0, member * TAPS + k] for k in range(TAPS)]
            for h in range(2):
                lanes = pl.ds(128 * h, 128)
                for base in range(0, 32, 8):
                    sums = [None] * 8
                    for i in range(max(base - RADIUS, 0), min(base + 8 + RADIUS, 32)):
                        value = v[i, rows, lanes]
                        for m in range(8):
                            k = i - base - m + RADIUS
                            if 0 <= k < TAPS:
                                term = scale[k] * value
                                sums[m] = term if sums[m] is None else sums[m] + term
                    for m in range(8):
                        w[base + m, rows, lanes] = sums[m]


def finest_kernel(taps, before, after, left, right, y0, z0h, z0l, w, out, v, wh, wl):
    for i in range(20):
        own = before[pl.ds(32 * i, 32)] if i < 10 else after[pl.ds(32 * (i - 10), 32)]
        b = left[pl.ds(10 * i, 16)]
        a = right[pl.ds(10 * i, 16)]
        high, low = halves(jnp.concatenate([own, b, a], 0))
        v[i] = dot(y0[...], jnp.concatenate([high, low, high], 0))

    @pl.loop(0, 4)
    def _(g):
        for member in range(3):
            rows = pl.ds(pl.multiple_of(32 * member + 8 * g, 8), 8)
            scale = [taps[0, member * TAPS + k] for k in range(TAPS)]
            for h in range(2):
                lanes = pl.ds(128 * h, 128)
                for base in range(0, 32, 2):
                    sums = []
                    for m in (base, base + 1):
                        total = w[m, rows, lanes]
                        for r in range(10):
                            if r >= m:
                                total = total + scale[r - m] * v[r, rows, lanes]
                            if r <= m - 22:
                                total = total + scale[42 + r - m] * v[10 + r, rows, lanes]
                        sums.append(total)
                    high, low = halves(jnp.concatenate(sums, 0))
                    at = (pl.ds(8 * base, 16), pl.ds(256 * member + 128 * h, 128))
                    wh[at] = high
                    wl[at] = low
        cols = pl.ds(pl.multiple_of(8 * g, 8), 8)
        total = dot(wh[...], z0h[...]) + dot(wl[...], z0h[...]) + dot(wh[...], z0l[...])
        out[:, cols] = total.reshape(32, 8, 256)


def call(kernel, outs, scratch=(), scalars=0, count=0, flops=0, moved=0, name=None):
    vmem = pl.BlockSpec(memory_space=pltpu.VMEM)
    smem = pl.BlockSpec(memory_space=pltpu.SMEM)
    shapes = [jax.ShapeDtypeStruct(*o) for o in outs]
    return pl.pallas_call(
        kernel,
        out_shape=shapes,
        in_specs=[smem] * scalars + [vmem] * (count - scalars),
        out_specs=[vmem] * len(shapes),
        scratch_shapes=[pltpu.VMEM(*s) for s in scratch],
        compiler_params=pltpu.CompilerParams(vmem_limit_bytes=VMEM_LIMIT),
        cost_estimate=pl.CostEstimate(flops=flops, bytes_accessed=moved, transcendentals=0),
        name=name,
    )


def shift(x, axis, by):
    n = lax.axis_size(axis)
    return lax.ppermute(x, axis, [(i, (i + by) % n) for i in range(n)])


def body(charges, kernel_taps):
    offsets0, basis1, basis2, up2, up1 = tables()
    taps = kernel_taps.reshape(3, 63)
    b16 = lambda x: jnp.asarray(x, BF)
    l1, l2, s_up, s_down, o_up, o_down = call(
        restrict_kernel,
        [((18, 24, 128), F32), ((6, 16, 128), F32), ((288, 128), F32), ((288, 128), F32),
         ((328, 256), F32), ((328, 256), F32)],
        [((18, 24, 256), F32), ((12, 16, 128), F32)], 0, 1, 10**8, 2 * 10**6, name="restrict",
    )(charges)
    x_left = shift(s_up, "gx", 1)
    x_right = shift(s_down, "gx", -1)
    own_left = shift(o_up, "gy", 1)
    own_right = shift(o_down, "gy", -1)
    taps, l1 = lax.optimization_barrier((taps, l1))
    y0, y1, y2, z0h, z0l, z1h, z1l, z2h, z2l = call(
        matrices_kernel,
        [((96, 192), BF), ((96, 144), BF), ((96, 144), BF), ((768, 256), BF), ((768, 256), BF),
         ((384, 128), BF), ((384, 128), BF), ((384, 128), BF), ((384, 128), BF)],
        [], 1, 5, 10**8, 4 * 10**6, name="matrices",
    )(taps, jnp.asarray(offsets0), jnp.asarray(basis1), jnp.asarray(basis2), b16(up2))
    x_left, x_right, y0 = lax.optimization_barrier((x_left, x_right, y0))
    c_up, c_down = call(
        face_x_kernel, [((360, 256), F32), ((360, 256), F32)], [], 0, 3, 10**6, 2 * 10**6, name="face_x",
    )(charges, x_left, x_right)
    before = shift(c_up, "gx", 1)
    after = shift(c_down, "gx", -1)
    y0, c_up, c_down = lax.optimization_barrier((y0, c_up, c_down))
    inner, = call(
        inner_kernel, [((32, 96, 256), F32)], [((32, 96, 256), F32)], 1, 5, 10**9, 6 * 10**6, name="inner",
    )(taps, charges, own_left, own_right, y0)
    before, after, inner = lax.optimization_barrier((before, after, inner))
    l1x, l2x, f_up, f_down = call(
        gather_x_kernel,
        [((38, 24, 128), F32), ((16, 16, 128), F32), ((528, 256), F32), ((528, 256), F32)],
        [], 0, 6, 10**6, 5 * 10**6, name="gather_x",
    )(before, after, l1, l2, x_left, x_right)
    left = shift(f_up, "gy", 1)
    right = shift(f_down, "gy", -1)
    t_up, t_down = call(
        second_kernel, [((80, 128), F32), ((80, 128), F32)], [], 0, 2, 10**5, 10**6, name="second",
    )(left, right)
    left2 = shift(t_up, "gy", 1)
    right2 = shift(t_down, "gy", -1)
    y0, t_up, t_down = lax.optimization_barrier((y0, t_up, t_down))
    direct, = call(
        finest_kernel, [((32, 32, 256), F32)],
        [((20, 96, 256), F32), ((256, 768), BF), ((256, 768), BF)],
        1, 9, 2 * 10**9, 6 * 10**6, name="finest",
    )(taps, before, after, left, right, y0, z0h, z0l, inner)
    result, = call(
        upper_kernel, [((32, 32, 256), F32)],
        [((38, 48, 128), F32), ((16, 48, 128), F32), ((38, 96, 128), F32), ((32, 96, 128), F32),
         ((18, 96, 128), F32), ((11, 96, 128), F32), ((18, 32, 128), F32), ((32, 32, 128), F32)],
        1, 15, 4 * 10**8, 4 * 10**6, name="upper",
    )(taps, l1x, l2x, left, right, left2, right2, y1, y2, z1h, z1l, z2h, z2l, b16(up1), direct)
    return result


def solution(mesh):
    return jax.shard_map(
        body,
        mesh=mesh,
        in_specs=(P("gx", "gy", None), P()),
        out_specs=P("gx", "gy", None),
        check_vma=False,
    )
```

```python
import jax
import jax.numpy as jnp
from jax import lax
from jax.experimental import pallas as pl
from jax.experimental.pallas import tpu as pltpu
from jax.sharding import PartitionSpec as P

SPLINE = (0.125, 0.5, 0.75, 0.5, 0.125)
RADIUS = 10
TAPS = 21
BF = jnp.bfloat16
F32 = jnp.float32
VMEM_LIMIT = 48 * 1024 * 1024


def halves(x):
    high = x.astype(BF)
    return high, (x - high.astype(F32)).astype(BF)


def dot(a, b):
    return jnp.dot(a, b, preferred_element_type=F32)


def spline_sum(read, center, low, high):
    total = None
    for k in range(-2, 3):
        if low <= 2 * center + k <= high:
            term = SPLINE[k + 2] * read(2 * center + k)
            total = term if total is None else total + term
    return total


def matrices_kernel(taps, y0, y1, y2, z0h, z0l, z1h, z1l, z2h, z2l, up1):
    def iota(shape, dim):
        return lax.broadcasted_iota(jnp.int32, shape, dim)

    def pick(level, member, offsets):
        table = jnp.zeros(offsets.shape, F32)
        for k in range(TAPS):
            table = jnp.where(offsets == k, taps[level, member, k], table)
        return table

    def cycle(level, member, length):
        offsets = (iota((length, length), 0) - iota((length, length), 1) + RADIUS) & (length - 1)
        return pick(level, member, offsets)

    def spread(lanes, width, pieces):
        cols = lanes
        for _ in range(2):
            cols = jnp.where(cols >= width, cols - width, cols)
        place = jnp.full(lanes.shape, -99, jnp.int32)
        for begin, end, position in pieces:
            place = jnp.where((cols >= begin) & (cols < end), cols - begin + position, place)
        return place

    def put(out, rows, table, width):
        high, low = halves(table)
        out[rows] = jnp.where(iota(table.shape, 1) < 2 * width, high.astype(F32), low.astype(F32)).astype(BF)

    def product(weights, table):
        high, low = halves(table)
        return dot(weights, high) + dot(weights, low)

    place0 = spread(iota((32, 192), 1), 64, ((0, 32, 0), (32, 42, -10), (48, 58, 32))) - iota((32, 192), 0) + RADIUS
    place1 = spread(iota((32, 144), 1), 48, ((0, 12, -11), (12, 30, -1), (30, 42, 15)))
    place1 = place1 - (iota((32, 144), 0) - 1) + RADIUS
    place2 = spread(iota((32, 144), 1), 48, ((0, 11, -1), (16, 27, -9), (27, 38, 7), (38, 43, -11), (43, 48, 15)))
    place2 = place2 - (iota((32, 144), 0) - 1) + RADIUS
    columns = iota((32, 32), 1) - 1
    lift1 = jnp.where(columns < 17, spline_of(iota((32, 32), 0) - 2 * columns), 0.0).astype(BF)
    lift2 = jnp.where(columns < 10, spline_of(iota((32, 32), 0) - 1 - 2 * columns), 0.0).astype(BF)
    lift2 = dot(lift1, lift2).astype(BF)
    up2 = cyclic_iota((64, 128), 0, 1, 128).astype(BF)
    up1[...] = cyclic_iota((128, 256), 0, 1, 256).astype(BF)
    for member in range(3):
        rows = pl.ds(32 * member, 32)
        put(y0, rows, pick(0, member, place0), 64)
        put(y1, rows, product(lift1, pick(1, member, place1)), 48)
        put(y2, rows, product(lift2, pick(2, member, place2)), 48)
        high, low = halves(cycle(0, member, 256))
        z0h[pl.ds(256 * member, 256)] = high
        z0l[pl.ds(256 * member, 256)] = low
        high, low = halves(cycle(1, member, 128))
        z1h[pl.ds(128 * member, 128)] = high
        z1l[pl.ds(128 * member, 128)] = low
        high, low = halves(cycle(2, member, 64))
        table = dot(high, up2) + dot(low, up2)
        high, low = halves(table)
        z2h[pl.ds(128 * member, 64)] = high
        z2l[pl.ds(128 * member, 64)] = low
        z2h[pl.ds(128 * member + 64, 64)] = jnp.zeros((64, 128), BF)
        z2l[pl.ds(128 * member + 64, 64)] = jnp.zeros((64, 128), BF)


def spline_iota(shape, offset, coarse_dim, fine_dim, keep=None):
    fine = lax.broadcasted_iota(jnp.int32, shape, fine_dim)
    coarse = lax.broadcasted_iota(jnp.int32, shape, coarse_dim)
    delta = fine - 2 * coarse + offset
    if keep is not None:
        delta = jnp.where(coarse < keep, delta, 99)
    return spline_of(delta)


def spline_of(delta):
    far = jnp.abs(delta)
    return jnp.where(far == 0, 0.75, jnp.where(far == 1, 0.5, jnp.where(far == 2, 0.125, 0.0)))


def cyclic_iota(shape, coarse_dim, fine_dim, fine_len):
    fine = lax.broadcasted_iota(jnp.int32, shape, fine_dim)
    coarse = lax.broadcasted_iota(jnp.int32, shape, coarse_dim)
    return spline_of(((fine - 2 * coarse + 2) & (fine_len - 1)) - 2)


def restrict_kernel(c, l1, l2, up1, down1, face_up, face_down, last, first, s1, s2):
    for r in range(10):
        last[pl.ds(32 * r, 32)] = c[22 + r]
        first[pl.ds(32 * r, 32)] = c[r]
    for i in range(32):
        face_up[pl.ds(10 * i, 10)] = c[i, 22:32]
        face_down[pl.ds(10 * i, 10)] = c[i, 0:10]
    face_up[pl.ds(320, 8)] = jnp.zeros((8, 256), F32)
    face_down[pl.ds(320, 8)] = jnp.zeros((8, 256), F32)
    ry = spline_iota((24, 32), 2, 0, 1, 18).astype(BF)
    for i in range(-1, 17):
        high, low = halves(spline_sum(lambda r: c[r], i, 0, 31))
        s1[i + 1] = dot(ry, high) + dot(ry, low)
    rz = cyclic_iota((256, 128), 1, 0, 256).astype(BF)
    high, low = halves(s1[...].reshape(18 * 24, 256))
    l1[...] = (dot(high, rz) + dot(low, rz)).reshape(18, 24, 128)
    ry2 = spline_iota((16, 24), 1, 0, 1, 11).astype(BF)
    for i in range(-1, 10):
        high, low = halves(spline_sum(lambda r: l1[r + 1], i, -1, 16))
        s2[i + 1] = dot(ry2, high) + dot(ry2, low)
    s2[11] = jnp.zeros((16, 128), F32)
    near = s2[pl.ds(0, 6)].reshape(96, 128)
    far = s2[pl.ds(6, 6)].reshape(96, 128)
    lanes = lax.broadcasted_iota(jnp.int32, (128, 128), 1)
    both = spline_of(((lax.broadcasted_iota(jnp.int32, (128, 128), 0) - 2 * (lanes & 63) + 2) & 127) - 2)
    total = jnp.zeros((96, 128), F32)
    for part, upper in ((near, False), (far, True)):
        weights = jnp.where((lanes >= 64) == upper, both, 0.0).astype(BF)
        high, low = halves(part)
        total = total + dot(high, weights) + dot(low, weights)
    total = total.reshape(6, 16, 128)
    l2[...] = total
    up1[pl.ds(64, 8)] = jnp.zeros((8, 128), F32)
    down1[pl.ds(64, 8)] = jnp.zeros((8, 128), F32)
    for j in range(6):
        up1[pl.ds(11 * j, 11)] = total[j, :11]
        down1[pl.ds(11 * j, 11)] = total[j, :11]
    for r in range(12):
        up1[pl.ds(72 + 18 * r, 18)] = l1[6 + r, :18]
        down1[pl.ds(72 + 18 * r, 18)] = l1[r, :18]


def paired(base, count, j):
    return (pl.ds(base + count * (j // 2), count), pl.ds(128 * (j % 2), 128))


def face_x_kernel(last, first, left, right, up, down):
    up[pl.ds(0, 320)] = last[...]
    down[pl.ds(0, 320)] = first[...]
    lower = lax.broadcasted_iota(jnp.int32, (11, 128), 1) < 64
    for p in range(3):
        even = 2 * p
        odd = min(even + 1, 4)
        a = left[pl.ds(11 * even, 11)]
        b = left[pl.ds(11 * odd, 11)]
        up[paired(320, 11, p)] = jnp.where(lower, pltpu.roll(a, 64, 1), b)
        a = right[pl.ds(11 * even, 11)]
        b = right[pl.ds(11 * odd, 11)]
        down[paired(320, 11, p)] = jnp.where(lower, a, pltpu.roll(b, 64, 1))


def gather_fine_kernel(l1, left, right, l1x, up, down):
    for i in range(38):
        if i < 12:
            l1x[i, :18] = left[pl.ds(72 + 18 * i, 18)]
            l1x[i, pl.ds(18, 6)] = jnp.zeros((6, 128), F32)
        elif i >= 26:
            l1x[i, :18] = right[pl.ds(72 + 18 * (i - 26), 18)]
            l1x[i, pl.ds(18, 6)] = jnp.zeros((6, 128), F32)
        if 10 <= i < 12 or 26 <= i < 28:
            l1x[i] = l1x[i] + l1[i - 10]
        elif 12 <= i < 26:
            l1x[i] = l1[i - 10]
    for i in range(38):
        up[pl.ds(12 * i, 12)] = l1x[i, 6:18]
        down[pl.ds(12 * i, 12)] = l1x[i, 0:12]


def gather_top_kernel(before, after, l2, left, right, l2x, up, down):
    for i in range(20):
        row = before[pl.ds(32 * i, 32)] if i < 10 else after[pl.ds(32 * (i - 10), 32)]
        up[pl.ds(10 * i, 10)] = row[22:32]
        down[pl.ds(10 * i, 10)] = row[0:10]
    up[pl.ds(200, 8)] = jnp.zeros((8, 256), F32)
    down[pl.ds(200, 8)] = jnp.zeros((8, 256), F32)
    lanes = lax.broadcasted_iota(jnp.int32, (11, 128), 1)
    lower = lanes < 64
    rolled = lambda x: pltpu.roll(x, 64, 1)
    for j in range(16):
        low = []
        high = []
        if j < 5:
            slab = before[paired(320, 11, j // 2)]
            low.append(slab if j % 2 == 0 else rolled(slab))
        if 2 <= j < 8:
            low.append(left[pl.ds(11 * (j - 2), 11)])
        if 8 <= j < 13:
            low.append(rolled(left[pl.ds(11 * (j - 8), 11)]))
        if j >= 10:
            low.append(l2[j - 10, :11])
        if j < 5:
            high.append(l2[j, :11])
        if 2 <= j < 8:
            high.append(rolled(right[pl.ds(11 * (j - 2), 11)]))
        if 8 <= j < 13:
            high.append(right[pl.ds(11 * (j - 8), 11)])
        if 10 <= j < 15:
            slab = after[paired(320, 11, (j - 10) // 2)]
            high.append(rolled(slab) if j % 2 == 0 else slab)
        row = jnp.where(lower, sum(low, jnp.zeros((11, 128), F32)), sum(high, jnp.zeros((11, 128), F32)))
        l2x[j, :11] = row
        l2x[j, pl.ds(11, 5)] = jnp.zeros((5, 128), F32)
        up[paired(208, 11, j)] = row
        down[paired(208, 11, j)] = row


def second_kernel(left, right, up, down):
    for j in range(16):
        rows, lanes = paired(208, 11, j)
        up[pl.ds(5 * j, 5)] = left[pl.ds(rows.start + 6, 5), lanes]
        down[pl.ds(5 * j, 5)] = right[pl.ds(rows.start, 5), lanes]


def correlate_x(taps, level, v, w, count, many):
    @pl.loop(0, 12)
    def _(g):
        member = g // 4
        rows = pl.ds(pl.multiple_of(8 * g, 8), 8)
        scale = [taps[level, member, k] for k in range(TAPS)]
        for base in range(0, count, many):
            sums = [None] * many
            for i in range(base, base + many + TAPS - 1):
                value = v[i, rows]
                for m in range(many):
                    k = i - base - m
                    if 0 <= k < TAPS:
                        term = scale[k] * value
                        sums[m] = term if sums[m] is None else sums[m] + term
            for m in range(many):
                w[base + m, rows] = sums[m]


def correlate_z(w, count, high_table, low_table):
    total = jnp.zeros((count * 32, 128), F32)
    for member in range(3):
        high, low = halves(w[:, pl.ds(32 * member, 32)].reshape(count * 32, 128))
        rows = pl.ds(128 * member, 128)
        total = total + dot(high, high_table[rows]) + dot(low, high_table[rows]) + dot(high, low_table[rows])
    return total.reshape(count, 32, 128)


def fine_level_kernel(taps, l1x, left, right, y1, z1h, z1l, mid, f1, v1, w1):
    for i in range(38):
        f1[i, pl.ds(0, 12)] = left[pl.ds(12 * i, 12)]
        f1[i, pl.ds(12, 18)] = l1x[i, :18]
        f1[i, pl.ds(30, 12)] = right[pl.ds(12 * i, 12)]
        f1[i, pl.ds(42, 6)] = jnp.zeros((6, 128), F32)

    @pl.loop(0, 38, unroll=2)
    def _(i):
        high, low = halves(f1[i])
        v1[i] = dot(y1[...], jnp.concatenate([high, low, high], 0))

    correlate_x(taps, 1, v1, w1, 18, 9)
    mid[...] = correlate_z(w1, 18, z1h, z1l)


def upper_kernel(taps, l2x, left, right, left2, right2, y2, z2h, z2l, up1, mid_in, direct, out,
                 f2, v2, w2, mid, fine):
    for j in range(16):
        f2[j, pl.ds(0, 16)] = l2x[j]
        f2[j, pl.ds(16, 11)] = left[paired(208, 11, j)]
        f2[j, pl.ds(27, 11)] = right[paired(208, 11, j)]
        f2[j, pl.ds(38, 5)] = left2[pl.ds(5 * j, 5)]
        f2[j, pl.ds(43, 5)] = right2[pl.ds(5 * j, 5)]

    @pl.loop(0, 16, unroll=2)
    def _(j):
        high, low = halves(f2[j])
        v = dot(y2[...], jnp.concatenate([high, low, high], 0))
        v2[j] = v
        v2[16 + j] = pltpu.roll(v, 64, 1)

    correlate_x(taps, 2, v2, w2, 11, 11)
    v2[pl.ds(0, 11), pl.ds(0, 32)] = correlate_z(w2, 11, z2h, z2l)
    top = lambda i: v2[i + 1, pl.ds(0, 32)]
    for a in range(-1, 9):
        if a >= 0:
            mid[2 * a + 1] = mid_in[2 * a + 1] + (0.75 * top(a) + 0.125 * (top(a - 1) + top(a + 1)))
        if a < 8:
            mid[2 * a + 2] = mid_in[2 * a + 2] + 0.5 * (top(a) + top(a + 1))
    for a in range(16):
        fine[2 * a] = 0.75 * mid[a + 1] + 0.125 * (mid[a] + mid[a + 2])
        fine[2 * a + 1] = 0.5 * (mid[a + 1] + mid[a + 2])
    for q in range(4):
        rows = pl.ds(8 * q, 8)
        high, low = halves(fine[rows].reshape(256, 128))
        out[rows] = direct[rows] + (dot(high, up1[...]) + dot(low, up1[...])).reshape(8, 32, 256)


def section(table, own, left, right, base, at):
    b = left[pl.ds(base, 48)][10 * at:10 * at + 16]
    a = right[pl.ds(base, 48)][10 * at:10 * at + 16]
    high, low = halves(jnp.concatenate([own, b, a], 0))
    return dot(table[...], jnp.concatenate([high, low, high], 0))


def inner_kernel(taps, c, left, right, y0, w, v):
    @pl.loop(0, 8)
    def _(q):
        base = pl.multiple_of(40 * q, 8)
        for at in range(4):
            i = 4 * q + at
            v[i] = section(y0, c[i], left, right, base, at)

    @pl.loop(0, 4)
    def _(g):
        for member in range(3):
            rows = pl.ds(pl.multiple_of(32 * member + 8 * g, 8), 8)
            scale = [taps[0, member, k] for k in range(TAPS)]
            for h in range(2):
                lanes = pl.ds(128 * h, 128)
                for base in range(0, 32, 8):
                    sums = [None] * 8
                    for i in range(max(base - RADIUS, 0), min(base + 8 + RADIUS, 32)):
                        value = v[i, rows, lanes]
                        for m in range(8):
                            k = i - base - m + RADIUS
                            if 0 <= k < TAPS:
                                term = scale[k] * value
                                sums[m] = term if sums[m] is None else sums[m] + term
                    for m in range(8):
                        w[base + m, rows, lanes] = sums[m]


def finest_kernel(taps, before, after, left, right, y0, z0h, z0l, w, out, v, wh, wl):
    for i in range(20):
        own = before[pl.ds(32 * i, 32)] if i < 10 else after[pl.ds(32 * (i - 10), 32)]
        b = left[pl.ds(10 * i, 16)]
        a = right[pl.ds(10 * i, 16)]
        high, low = halves(jnp.concatenate([own, b, a], 0))
        v[i] = dot(y0[...], jnp.concatenate([high, low, high], 0))

    @pl.loop(0, 4)
    def _(g):
        for member in range(3):
            rows = pl.ds(pl.multiple_of(32 * member + 8 * g, 8), 8)
            scale = [taps[0, member, k] for k in range(TAPS)]
            for h in range(2):
                lanes = pl.ds(128 * h, 128)
                for base in range(0, 32, 2):
                    sums = []
                    for m in (base, base + 1):
                        total = w[m, rows, lanes]
                        for r in range(10):
                            if r >= m:
                                total = total + scale[r - m] * v[r, rows, lanes]
                            if r <= m - 22:
                                total = total + scale[42 + r - m] * v[10 + r, rows, lanes]
                        sums.append(total)
                    high, low = halves(jnp.concatenate(sums, 0))
                    at = (pl.ds(8 * base, 16), pl.ds(256 * member + 128 * h, 128))
                    wh[at] = high
                    wl[at] = low
        cols = pl.ds(pl.multiple_of(8 * g, 8), 8)
        total = dot(wh[...], z0h[...]) + dot(wl[...], z0h[...]) + dot(wh[...], z0l[...])
        out[:, cols] = total.reshape(32, 8, 256)


def call(kernel, outs, scratch=(), scalars=0, count=0, flops=0, moved=0, name=None):
    vmem = pl.BlockSpec(memory_space=pltpu.VMEM)
    smem = pl.BlockSpec(memory_space=pltpu.SMEM)
    shapes = [jax.ShapeDtypeStruct(*o) for o in outs]
    return pl.pallas_call(
        kernel,
        out_shape=shapes,
        in_specs=[smem] * scalars + [vmem] * (count - scalars),
        out_specs=[vmem] * len(shapes),
        scratch_shapes=[pltpu.VMEM(*s) for s in scratch],
        compiler_params=pltpu.CompilerParams(vmem_limit_bytes=VMEM_LIMIT),
        cost_estimate=pl.CostEstimate(flops=flops, bytes_accessed=moved, transcendentals=0),
        name=name,
    )


def shift(x, axis, by):
    n = lax.axis_size(axis)
    return lax.ppermute(x, axis, [(i, (i + by) % n) for i in range(n)])


def body(charges, kernel_taps):
    taps = kernel_taps
    l1, l2, s_up, s_down, o_up, o_down, last, first = call(
        restrict_kernel,
        [((18, 24, 128), F32), ((6, 16, 128), F32), ((288, 128), F32), ((288, 128), F32),
         ((328, 256), F32), ((328, 256), F32), ((320, 256), F32), ((320, 256), F32)],
        [((18, 24, 256), F32), ((12, 16, 128), F32)], 0, 1, 10**8, 2 * 10**6, name="restrict",
    )(charges)
    x_left = shift(s_up, "gx", 1)
    x_right = shift(s_down, "gx", -1)
    own_left = shift(o_up, "gy", 1)
    own_right = shift(o_down, "gy", -1)
    taps, l1 = lax.optimization_barrier((taps, l1))
    y0, y1, y2, z0h, z0l, z1h, z1l, z2h, z2l, up1 = call(
        matrices_kernel,
        [((96, 192), BF), ((96, 144), BF), ((96, 144), BF), ((768, 256), BF), ((768, 256), BF),
         ((384, 128), BF), ((384, 128), BF), ((384, 128), BF), ((384, 128), BF), ((128, 256), BF)],
        [], 1, 1, 10**8, 4 * 10**6, name="matrices",
    )(taps)
    x_left, x_right, y0 = lax.optimization_barrier((x_left, x_right, y0))
    c_up, c_down = call(
        face_x_kernel, [((344, 256), F32), ((344, 256), F32)], [], 0, 4, 10**6, 2 * 10**6, name="face_x",
    )(last, first, x_left, x_right)
    before = shift(c_up, "gx", 1)
    after = shift(c_down, "gx", -1)
    x_left, x_right, c_up = lax.optimization_barrier((x_left, x_right, c_up))
    l1x, g_up, g_down = call(
        gather_fine_kernel, [((38, 24, 128), F32), ((456, 128), F32), ((456, 128), F32)],
        [], 0, 3, 10**6, 2 * 10**6, name="gather_fine",
    )(l1, x_left, x_right)
    fine_left = shift(g_up, "gy", 1)
    fine_right = shift(g_down, "gy", -1)
    y0, g_up, g_down = lax.optimization_barrier((y0, g_up, g_down))
    inner, = call(
        inner_kernel, [((32, 96, 256), F32)], [((32, 96, 256), F32)], 1, 5, 10**9, 6 * 10**6, name="inner",
    )(taps, charges, own_left, own_right, y0)
    before, after, inner, fine_left, fine_right = lax.optimization_barrier(
        (before, after, inner, fine_left, fine_right)
    )
    l2x, f_up, f_down = call(
        gather_top_kernel,
        [((16, 16, 128), F32), ((296, 256), F32), ((296, 256), F32)],
        [], 0, 5, 10**6, 5 * 10**6, name="gather_top",
    )(before, after, l2, x_left, x_right)
    left = shift(f_up, "gy", 1)
    right = shift(f_down, "gy", -1)
    l1x, f_up, f_down = lax.optimization_barrier((l1x, f_up, f_down))
    mid, = call(
        fine_level_kernel, [((18, 32, 128), F32)],
        [((38, 48, 128), F32), ((38, 96, 128), F32), ((18, 96, 128), F32)],
        1, 7, 4 * 10**8, 4 * 10**6, name="fine_level",
    )(taps, l1x, fine_left, fine_right, y1, z1h, z1l)
    left, right, mid = lax.optimization_barrier((left, right, mid))
    t_up, t_down = call(
        second_kernel, [((80, 128), F32), ((80, 128), F32)], [], 0, 2, 10**5, 10**6, name="second",
    )(left, right)
    left2 = shift(t_up, "gy", 1)
    right2 = shift(t_down, "gy", -1)
    y0, t_up, t_down = lax.optimization_barrier((y0, t_up, t_down))
    direct, = call(
        finest_kernel, [((32, 32, 256), F32)],
        [((20, 96, 256), F32), ((256, 768), BF), ((256, 768), BF)],
        1, 9, 2 * 10**9, 6 * 10**6, name="finest",
    )(taps, before, after, left, right, y0, z0h, z0l, inner)
    result, = call(
        upper_kernel, [((32, 32, 256), F32)],
        [((16, 48, 128), F32), ((32, 96, 128), F32), ((11, 96, 128), F32), ((18, 32, 128), F32),
         ((32, 32, 128), F32)],
        1, 12, 4 * 10**8, 4 * 10**6, name="upper",
    )(taps, l2x, left, right, left2, right2, y2, z2h, z2l, up1, mid, direct)
    return result


def solution(mesh):
    return jax.shard_map(
        body,
        mesh=mesh,
        in_specs=(P("gx", "gy", None), P()),
        out_specs=P("gx", "gy", None),
        check_vma=False,
    )
```

```python
import jax
import jax.numpy as jnp
from jax import lax
from jax.experimental import pallas as pl
from jax.experimental.pallas import tpu as pltpu
from jax.sharding import PartitionSpec as P

SPLINE = (0.125, 0.5, 0.75, 0.5, 0.125)
RADIUS = 10
TAPS = 21
BF = jnp.bfloat16
F32 = jnp.float32
VMEM_LIMIT = 48 * 1024 * 1024
HINT = 2 * 10**10


def halves(x):
    high = x.astype(BF)
    return high, (x - high.astype(F32)).astype(BF)


def dot(a, b):
    return jnp.dot(a, b, preferred_element_type=F32)


def spline_sum(read, center, low, high):
    total = None
    for k in range(-2, 3):
        if low <= 2 * center + k <= high:
            term = SPLINE[k + 2] * read(2 * center + k)
            total = term if total is None else total + term
    return total


def matrices_kernel(taps, y0, y1, y2, z0h, z0l, z1, z2, up1):
    def iota(shape, dim):
        return lax.broadcasted_iota(jnp.int32, shape, dim)

    def pick(level, member, offsets):
        table = jnp.zeros(offsets.shape, F32)
        for k in range(TAPS):
            table = jnp.where(offsets == k, taps[level, member, k], table)
        return table

    def cycle(level, member, length):
        offsets = (iota((length, length), 0) - iota((length, length), 1) + RADIUS) & (length - 1)
        return pick(level, member, offsets)

    def spread(lanes, width, pieces):
        cols = lanes
        for _ in range(2):
            cols = jnp.where(cols >= width, cols - width, cols)
        place = jnp.full(lanes.shape, -99, jnp.int32)
        for begin, end, position in pieces:
            place = jnp.where((cols >= begin) & (cols < end), cols - begin + position, place)
        return place

    def put(out, rows, table, width):
        high, low = halves(table)
        out[rows] = jnp.where(iota(table.shape, 1) < 2 * width, high.astype(F32), low.astype(F32)).astype(BF)

    def block(out, base, table, count):
        high, low = halves(table)
        zero = jnp.zeros((128, 128), BF)
        if count < 128:
            for at in (base, base + 128):
                out[pl.ds(at + count, 128 - count)] = jnp.zeros((128 - count, 256), BF)
        out[pl.ds(base, count), pl.ds(0, 128)] = high
        out[pl.ds(base, count), pl.ds(128, 128)] = low
        out[pl.ds(base + 128, count), pl.ds(0, 128)] = high
        out[pl.ds(base + 128, count), pl.ds(128, 128)] = zero[:count]

    def product(weights, table):
        high, low = halves(table)
        return dot(weights, high) + dot(weights, low)

    place0 = spread(iota((32, 192), 1), 64, ((0, 32, 0), (32, 42, -10), (48, 58, 32))) - iota((32, 192), 0) + RADIUS
    place1 = spread(iota((32, 144), 1), 48, ((0, 12, -11), (12, 30, -1), (30, 42, 15)))
    place1 = place1 - (iota((32, 144), 0) - 1) + RADIUS
    place2 = spread(iota((32, 144), 1), 48, ((0, 11, -1), (16, 27, -9), (27, 38, 7), (38, 43, -11), (43, 48, 15)))
    place2 = place2 - (iota((32, 144), 0) - 1) + RADIUS
    columns = iota((32, 32), 1) - 1
    lift1 = jnp.where(columns < 17, spline_of(iota((32, 32), 0) - 2 * columns), 0.0).astype(BF)
    lift2 = jnp.where(columns < 10, spline_of(iota((32, 32), 0) - 1 - 2 * columns), 0.0).astype(BF)
    lift2 = dot(lift1, lift2).astype(BF)
    up2 = cyclic_iota((64, 128), 0, 1, 128).astype(BF)
    up1[pl.ds(0, 128)] = cyclic_iota((128, 256), 0, 1, 256).astype(BF)
    up1[pl.ds(128, 128)] = cyclic_iota((128, 256), 0, 1, 256).astype(BF)
    for member in range(3):
        rows = pl.ds(32 * member, 32)
        put(y0, rows, pick(0, member, place0), 64)
        put(y1, rows, product(lift1, pick(1, member, place1)), 48)
        put(y2, rows, product(lift2, pick(2, member, place2)), 48)
        high, low = halves(cycle(0, member, 256))
        z0h[pl.ds(256 * member, 256)] = high
        z0l[pl.ds(256 * member, 256)] = low
        block(z1, 256 * member, cycle(1, member, 128), 128)
        high, low = halves(cycle(2, member, 64))
        block(z2, 256 * member, dot(high, up2) + dot(low, up2), 64)


def spline_iota(shape, offset, coarse_dim, fine_dim, keep=None):
    fine = lax.broadcasted_iota(jnp.int32, shape, fine_dim)
    coarse = lax.broadcasted_iota(jnp.int32, shape, coarse_dim)
    delta = fine - 2 * coarse + offset
    if keep is not None:
        delta = jnp.where(coarse < keep, delta, 99)
    return spline_of(delta)


def spline_of(delta):
    far = jnp.abs(delta)
    return jnp.where(far == 0, 0.75, jnp.where(far == 1, 0.5, jnp.where(far == 2, 0.125, 0.0)))


def cyclic_iota(shape, coarse_dim, fine_dim, fine_len):
    fine = lax.broadcasted_iota(jnp.int32, shape, fine_dim)
    coarse = lax.broadcasted_iota(jnp.int32, shape, coarse_dim)
    return spline_of(((fine - 2 * coarse + 2) & (fine_len - 1)) - 2)


def restrict_kernel(c, l1, l2, up1, down1, last, first, face_up, face_down, s1, s2):
    for i in range(32):
        face_up[pl.ds(10 * i, 10)] = c[i, 22:32]
        face_down[pl.ds(10 * i, 10)] = c[i, 0:10]
    face_up[pl.ds(320, 8)] = jnp.zeros((8, 256), F32)
    face_down[pl.ds(320, 8)] = jnp.zeros((8, 256), F32)
    for r in range(10):
        last[pl.ds(32 * r, 32)] = c[22 + r]
        first[pl.ds(32 * r, 32)] = c[r]
    ry = spline_iota((24, 32), 2, 0, 1, 18).astype(BF)
    for i in range(-1, 17):
        high, low = halves(spline_sum(lambda r: c[r], i, 0, 31))
        s1[i + 1] = dot(ry, high) + dot(ry, low)
    rz = cyclic_iota((256, 128), 1, 0, 256).astype(BF)
    high, low = halves(s1[...].reshape(18 * 24, 256))
    l1[...] = (dot(high, rz) + dot(low, rz)).reshape(18, 24, 128)
    ry2 = spline_iota((16, 24), 1, 0, 1, 11).astype(BF)
    for i in range(-1, 10):
        high, low = halves(spline_sum(lambda r: l1[r + 1], i, -1, 16))
        s2[i + 1] = dot(ry2, high) + dot(ry2, low)
    s2[11] = jnp.zeros((16, 128), F32)
    near = s2[pl.ds(0, 6)].reshape(96, 128)
    far = s2[pl.ds(6, 6)].reshape(96, 128)
    lanes = lax.broadcasted_iota(jnp.int32, (128, 128), 1)
    both = spline_of(((lax.broadcasted_iota(jnp.int32, (128, 128), 0) - 2 * (lanes & 63) + 2) & 127) - 2)
    total = jnp.zeros((96, 128), F32)
    for part, upper in ((near, False), (far, True)):
        weights = jnp.where((lanes >= 64) == upper, both, 0.0).astype(BF)
        high, low = halves(part)
        total = total + dot(high, weights) + dot(low, weights)
    total = total.reshape(6, 16, 128)
    l2[...] = total
    up1[pl.ds(64, 8)] = jnp.zeros((8, 128), F32)
    down1[pl.ds(64, 8)] = jnp.zeros((8, 128), F32)
    for j in range(6):
        up1[pl.ds(11 * j, 11)] = total[j, :11]
        down1[pl.ds(11 * j, 11)] = total[j, :11]
    for r in range(12):
        up1[pl.ds(72 + 18 * r, 18)] = l1[6 + r, :18]
        down1[pl.ds(72 + 18 * r, 18)] = l1[r, :18]


def paired(base, count, j):
    return (pl.ds(base + count * (j // 2), count), pl.ds(128 * (j % 2), 128))


def forward_kernel(left, right, up, down):
    lower = lax.broadcasted_iota(jnp.int32, (11, 128), 1) < 64
    for p in range(3):
        even = 2 * p
        odd = min(even + 1, 4)
        rows = pl.ds(11 * p, 11)
        a = left[pl.ds(11 * even, 11)]
        b = left[pl.ds(11 * odd, 11)]
        up[rows] = jnp.where(lower, pltpu.roll(a, 64, 1), b)
        a = right[pl.ds(11 * even, 11)]
        b = right[pl.ds(11 * odd, 11)]
        down[rows] = jnp.where(lower, a, pltpu.roll(b, 64, 1))


def gather_kernel(l1, l2, left, right, left2, right2, l1x, l2x, up, down):
    for i in range(38):
        if i < 12:
            l1x[i, :18] = left[pl.ds(72 + 18 * i, 18)]
            l1x[i, pl.ds(18, 6)] = jnp.zeros((6, 128), F32)
        elif i >= 26:
            l1x[i, :18] = right[pl.ds(72 + 18 * (i - 26), 18)]
            l1x[i, pl.ds(18, 6)] = jnp.zeros((6, 128), F32)
        if 10 <= i < 12 or 26 <= i < 28:
            l1x[i] = l1x[i] + l1[i - 10]
        elif 12 <= i < 26:
            l1x[i] = l1[i - 10]
    for i in range(38):
        up[paired(0, 12, i)] = l1x[i, 6:18]
        down[paired(0, 12, i)] = l1x[i, 0:12]
    lanes = lax.broadcasted_iota(jnp.int32, (11, 128), 1)
    lower = lanes < 64
    rolled = lambda x: pltpu.roll(x, 64, 1)
    for j in range(16):
        low = []
        high = []
        if j < 5:
            slab = left2[pl.ds(11 * (j // 2), 11)]
            low.append(slab if j % 2 == 0 else rolled(slab))
        if 2 <= j < 8:
            low.append(left[pl.ds(11 * (j - 2), 11)])
        if 8 <= j < 13:
            low.append(rolled(left[pl.ds(11 * (j - 8), 11)]))
        if j >= 10:
            low.append(l2[j - 10, :11])
        if j < 5:
            high.append(l2[j, :11])
        if 2 <= j < 8:
            high.append(rolled(right[pl.ds(11 * (j - 2), 11)]))
        if 8 <= j < 13:
            high.append(right[pl.ds(11 * (j - 8), 11)])
        if 10 <= j < 15:
            slab = right2[pl.ds(11 * ((j - 10) // 2), 11)]
            high.append(rolled(slab) if j % 2 == 0 else slab)
        row = jnp.where(lower, sum(low, jnp.zeros((11, 128), F32)), sum(high, jnp.zeros((11, 128), F32)))
        l2x[j, :11] = row
        l2x[j, pl.ds(11, 5)] = jnp.zeros((5, 128), F32)
        up[paired(228, 11, j)] = row
        down[paired(228, 11, j)] = row


def corner_kernel(before, after, up, down):
    for i in range(20):
        row = before[pl.ds(32 * i, 32)] if i < 10 else after[pl.ds(32 * (i - 10), 32)]
        up[pl.ds(10 * i, 10)] = row[22:32]
        down[pl.ds(10 * i, 10)] = row[0:10]
    up[pl.ds(200, 8)] = jnp.zeros((8, 256), F32)
    down[pl.ds(200, 8)] = jnp.zeros((8, 256), F32)


def second_kernel(left, right, up, down):
    for j in range(16):
        rows, lanes = paired(228, 11, j)
        up[pl.ds(5 * j, 5)] = left[pl.ds(rows.start + 6, 5), lanes]
        down[pl.ds(5 * j, 5)] = right[pl.ds(rows.start, 5), lanes]


def correlate_x(taps, level, v, w, count, many):
    @pl.loop(0, 12)
    def _(g):
        member = g // 4
        rows = pl.ds(pl.multiple_of(8 * g, 8), 8)
        scale = [taps[level, member, k] for k in range(TAPS)]
        for base in range(0, count, many):
            sums = [None] * many
            for i in range(base, base + many + TAPS - 1):
                value = v[i, rows]
                for m in range(many):
                    k = i - base - m
                    if 0 <= k < TAPS:
                        term = scale[k] * value
                        sums[m] = term if sums[m] is None else sums[m] + term
            for m in range(many):
                w[base + m, rows] = sums[m]


def correlate_z(w, count, table):
    total = jnp.zeros((count * 32, 256), F32)
    for member in range(3):
        high, low = halves(w[:, pl.ds(32 * member, 32)].reshape(count * 32, 128))
        total = total + dot(jnp.concatenate([high, low], 1), table[pl.ds(256 * member, 256)])
    return (total[:, :128] + total[:, 128:]).reshape(count, 32, 128)


def fine_level_kernel(taps, l1x, left, right, y1, z1, mid, f1, v1, w1):
    for i in range(38):
        f1[i, pl.ds(0, 12)] = left[paired(0, 12, i)]
        f1[i, pl.ds(12, 18)] = l1x[i, :18]
        f1[i, pl.ds(30, 12)] = right[paired(0, 12, i)]
        f1[i, pl.ds(42, 6)] = jnp.zeros((6, 128), F32)

    @pl.loop(0, 38, unroll=19)
    def _(i):
        high, low = halves(f1[i])
        v1[i] = dot(y1[...], jnp.concatenate([high, low, high], 0))

    correlate_x(taps, 1, v1, w1, 18, 9)
    mid[...] = correlate_z(w1, 18, z1)


def upper_kernel(taps, l2x, left, right, left2, right2, y2, z2, up1, mid_in, direct, out,
                 f2, v2, w2, mid, fine):
    for j in range(16):
        f2[j, pl.ds(0, 16)] = l2x[j]
        f2[j, pl.ds(16, 11)] = left[paired(228, 11, j)]
        f2[j, pl.ds(27, 11)] = right[paired(228, 11, j)]
        f2[j, pl.ds(38, 5)] = left2[pl.ds(5 * j, 5)]
        f2[j, pl.ds(43, 5)] = right2[pl.ds(5 * j, 5)]

    @pl.loop(0, 16, unroll=16)
    def _(j):
        high, low = halves(f2[j])
        v = dot(y2[...], jnp.concatenate([high, low, high], 0))
        v2[j] = v
        v2[16 + j] = pltpu.roll(v, 64, 1)

    correlate_x(taps, 2, v2, w2, 11, 11)
    v2[pl.ds(0, 11), pl.ds(0, 32)] = correlate_z(w2, 11, z2)
    top = lambda i: v2[i + 1, pl.ds(0, 32)]
    for a in range(-1, 9):
        if a >= 0:
            mid[2 * a + 1] = mid_in[2 * a + 1] + (0.75 * top(a) + 0.125 * (top(a - 1) + top(a + 1)))
        if a < 8:
            mid[2 * a + 2] = mid_in[2 * a + 2] + 0.5 * (top(a) + top(a + 1))
    for a in range(16):
        fine[2 * a] = 0.75 * mid[a + 1] + 0.125 * (mid[a] + mid[a + 2])
        fine[2 * a + 1] = 0.5 * (mid[a + 1] + mid[a + 2])
    for q in range(4):
        rows = pl.ds(8 * q, 8)
        high, low = halves(fine[rows].reshape(256, 128))
        out[rows] = direct[rows] + dot(jnp.concatenate([high, low], 1), up1[...]).reshape(8, 32, 256)


def section(table, own, left, right, base, at):
    b = left[pl.ds(base, 48)][10 * at:10 * at + 16]
    a = right[pl.ds(base, 48)][10 * at:10 * at + 16]
    high, low = halves(jnp.concatenate([own, b, a], 0))
    return dot(table[...], jnp.concatenate([high, low, high], 0))


def inner_kernel(taps, c, left, right, y0, z0h, z0l, out, v, wh, wl):
    @pl.loop(0, 8, unroll=4)
    def _(q):
        base = pl.multiple_of(40 * q, 8)
        for at in range(4):
            i = 4 * q + at
            v[i] = section(y0, c[i], left, right, base, at)

    @pl.loop(0, 4)
    def _(g):
        for member in range(3):
            rows = pl.ds(pl.multiple_of(32 * member + 8 * g, 8), 8)
            scale = [taps[0, member, k] for k in range(TAPS)]
            for h in range(2):
                lanes = pl.ds(128 * h, 128)
                for base in range(0, 32, 8):
                    sums = [None] * 8
                    for i in range(max(base - RADIUS, 0), min(base + 8 + RADIUS, 32)):
                        value = v[i, rows, lanes]
                        for m in range(8):
                            k = i - base - m + RADIUS
                            if 0 <= k < TAPS:
                                term = scale[k] * value
                                sums[m] = term if sums[m] is None else sums[m] + term
                    for m in range(0, 8, 2):
                        high, low = halves(jnp.concatenate([sums[m], sums[m + 1]], 0))
                        at = (pl.ds(8 * (base + m), 16), pl.ds(256 * member + 128 * h, 128))
                        wh[at] = high
                        wl[at] = low
        cols = pl.ds(pl.multiple_of(8 * g, 8), 8)
        total = dot(wh[...], z0h[...]) + dot(wl[...], z0h[...]) + dot(wh[...], z0l[...])
        out[:, cols] = total.reshape(32, 8, 256)


def finest_kernel(taps, before, after, left, right, y0, z0h, z0l, inner, out, v, wh, wl):
    for i in range(20):
        own = before[pl.ds(32 * i, 32)] if i < 10 else after[pl.ds(32 * (i - 10), 32)]
        b = left[pl.ds(10 * i, 16)]
        a = right[pl.ds(10 * i, 16)]
        high, low = halves(jnp.concatenate([own, b, a], 0))
        v[i] = dot(y0[...], jnp.concatenate([high, low, high], 0))

    @pl.loop(0, 4)
    def _(g):
        for member in range(3):
            rows = pl.ds(pl.multiple_of(32 * member + 8 * g, 8), 8)
            scale = [taps[0, member, k] for k in range(TAPS)]
            for h in range(2):
                lanes = pl.ds(128 * h, 128)
                sums = [None] * 20
                for r in range(20):
                    value = v[r, rows, lanes]
                    for m in range(10):
                        k = r - m if r < 10 else 20 + r - 10 - m
                        at = m if r < 10 else 10 + m
                        if r < 10 and m > r or r >= 10 and m < r - 10:
                            continue
                        term = scale[k] * value
                        sums[at] = term if sums[at] is None else sums[at] + term
                for m in range(0, 20, 2):
                    high, low = halves(jnp.concatenate([sums[m], sums[m + 1]], 0))
                    at = (pl.ds(8 * m, 16), pl.ds(256 * member + 128 * h, 128))
                    wh[at] = high
                    wl[at] = low
        cols = pl.ds(pl.multiple_of(8 * g, 8), 8)
        total = dot(wh[...], z0h[...]) + dot(wl[...], z0h[...]) + dot(wh[...], z0l[...])
        total = total.reshape(20, 8, 256)
        out[pl.ds(0, 10), cols] = inner[pl.ds(0, 10), cols] + total[:10]
        out[pl.ds(10, 12), cols] = inner[pl.ds(10, 12), cols]
        out[pl.ds(22, 10), cols] = inner[pl.ds(22, 10), cols] + total[10:]


def call(kernel, outs, scratch=(), scalars=0, count=0, flops=0, moved=0, name=None):
    vmem = pl.BlockSpec(memory_space=pltpu.VMEM)
    smem = pl.BlockSpec(memory_space=pltpu.SMEM)
    shapes = [jax.ShapeDtypeStruct(*o) for o in outs]
    return pl.pallas_call(
        kernel,
        out_shape=shapes,
        in_specs=[smem] * scalars + [vmem] * (count - scalars),
        out_specs=[vmem] * len(shapes),
        scratch_shapes=[pltpu.VMEM(*s) for s in scratch],
        compiler_params=pltpu.CompilerParams(vmem_limit_bytes=VMEM_LIMIT),
        cost_estimate=pl.CostEstimate(flops=flops, bytes_accessed=moved, transcendentals=0),
        name=name,
    )


def shift(x, axis, by):
    n = lax.axis_size(axis)
    return lax.ppermute(x, axis, [(i, (i + by) % n) for i in range(n)])


def body(charges, kernel_taps):
    taps = kernel_taps
    l1, l2, s_up, s_down, last, first, o_up, o_down = call(
        restrict_kernel,
        [((18, 24, 128), F32), ((6, 16, 128), F32), ((288, 128), F32), ((288, 128), F32),
         ((320, 256), F32), ((320, 256), F32), ((328, 256), F32), ((328, 256), F32)],
        [((18, 24, 256), F32), ((12, 16, 128), F32)], 0, 1, 10**8, 2 * 10**6, name="restrict",
    )(charges)
    x_left = shift(s_up, "gx", 1)
    x_right = shift(s_down, "gx", -1)
    own_left = shift(o_up, "gy", 1)
    own_right = shift(o_down, "gy", -1)
    taps, l1 = lax.optimization_barrier((taps, l1))
    y0, y1, y2, z0h, z0l, z1, z2, up1 = call(
        matrices_kernel,
        [((96, 192), BF), ((96, 144), BF), ((96, 144), BF), ((768, 256), BF), ((768, 256), BF),
         ((768, 256), BF), ((768, 256), BF), ((256, 256), BF)],
        [], 1, 1, 10**8, 4 * 10**6, name="matrices",
    )(taps)
    x_left, x_right, y0 = lax.optimization_barrier((x_left, x_right, y0))
    c_up, c_down = call(
        forward_kernel, [((40, 128), F32), ((40, 128), F32)], [], 0, 2, HINT, 0, name="forward",
    )(x_left, x_right)
    x_left2 = shift(c_up, "gx", 1)
    x_right2 = shift(c_down, "gx", -1)

    l1x, l2x, g_up, g_down = call(
        gather_kernel,
        [((38, 24, 128), F32), ((16, 16, 128), F32), ((316, 256), F32), ((316, 256), F32)],
        [], 0, 6, 0, 0, name="gather",
    )(l1, l2, x_left, x_right, x_left2, x_right2)
    left = shift(g_up, "gy", 1)
    right = shift(g_down, "gy", -1)
    last, first, g_up, g_down = lax.optimization_barrier((last, first, g_up, g_down))
    before = shift(last, "gx", 1)
    after = shift(first, "gx", -1)
    y0, g_up, g_down = lax.optimization_barrier((y0, g_up, g_down))
    inner, = call(
        inner_kernel, [((32, 32, 256), F32)],
        [((32, 96, 256), F32), ((256, 768), BF), ((256, 768), BF)], 1, 7, 2 * 10**9, 6 * 10**6, name="inner",
    )(taps, charges, own_left, own_right, y0, z0h, z0l)
    left, right, inner = lax.optimization_barrier((left, right, inner))
    t_up, t_down = call(
        second_kernel, [((80, 128), F32), ((80, 128), F32)], [], 0, 2, 10**5, 10**6, name="second",
    )(left, right)
    left2 = shift(t_up, "gy", 1)
    right2 = shift(t_down, "gy", -1)
    before, after, t_up, t_down = lax.optimization_barrier((before, after, t_up, t_down))
    f_up, f_down = call(
        corner_kernel, [((208, 256), F32), ((208, 256), F32)], [], 0, 2, 10**6, 10**6, name="corner",
    )(before, after)
    corner_left = shift(f_up, "gy", 1)
    corner_right = shift(f_down, "gy", -1)
    l1x, f_up, f_down = lax.optimization_barrier((l1x, f_up, f_down))
    mid, = call(
        fine_level_kernel, [((18, 32, 128), F32)],
        [((38, 48, 128), F32), ((38, 96, 128), F32), ((18, 96, 128), F32)],
        1, 6, 4 * 10**8, 4 * 10**6, name="fine_level",
    )(taps, l1x, left, right, y1, z1)
    partial, = call(
        upper_kernel, [((32, 32, 256), F32)],
        [((16, 48, 128), F32), ((32, 96, 128), F32), ((11, 96, 128), F32), ((18, 32, 128), F32),
         ((32, 32, 128), F32)],
        1, 11, 4 * 10**8, 4 * 10**6, name="upper",
    )(taps, l2x, left, right, left2, right2, y2, z2, up1, mid, inner)
    corner_left, corner_right, partial = lax.optimization_barrier((corner_left, corner_right, partial))
    result, = call(
        finest_kernel, [((32, 32, 256), F32)],
        [((20, 96, 256), F32), ((160, 768), BF), ((160, 768), BF)],
        1, 9, 2 * 10**9, 6 * 10**6, name="finest",
    )(taps, before, after, corner_left, corner_right, y0, z0h, z0l, partial)
    return result


def solution(mesh):
    return jax.shard_map(
        body,
        mesh=mesh,
        in_specs=(P("gx", "gy", None), P()),
        out_specs=P("gx", "gy", None),
        check_vma=False,
    )
```

```python
import jax
import jax.numpy as jnp
from jax import lax
from jax.experimental import pallas as pl
from jax.experimental.pallas import tpu as pltpu
from jax.sharding import PartitionSpec as P

SPLINE = (0.125, 0.5, 0.75, 0.5, 0.125)
RADIUS = 10
TAPS = 21
BF = jnp.bfloat16
F32 = jnp.float32
VMEM_LIMIT = 48 * 1024 * 1024


def halves(x):
    high = x.astype(BF)
    return high, (x - high.astype(F32)).astype(BF)


def dot(a, b):
    return jnp.dot(a, b, preferred_element_type=F32)


def spline_sum(read, center, low, high):
    total = None
    for k in range(-2, 3):
        if low <= 2 * center + k <= high:
            term = SPLINE[k + 2] * read(2 * center + k)
            total = term if total is None else total + term
    return total


def matrices_kernel(taps, y0, y1, y2, z0h, z0l, z1, z2, up1):
    def iota(shape, dim):
        return lax.broadcasted_iota(jnp.int32, shape, dim)

    def pick(level, member, offsets):
        table = jnp.zeros(offsets.shape, F32)
        for k in range(TAPS):
            table = jnp.where(offsets == k, taps[level, member, k], table)
        return table

    def cycle(level, member, length):
        offsets = (iota((length, length), 0) - iota((length, length), 1) + RADIUS) & (length - 1)
        return pick(level, member, offsets)

    def spread(lanes, width, pieces):
        cols = lanes
        for _ in range(2):
            cols = jnp.where(cols >= width, cols - width, cols)
        place = jnp.full(lanes.shape, -99, jnp.int32)
        for begin, end, position in pieces:
            place = jnp.where((cols >= begin) & (cols < end), cols - begin + position, place)
        return place

    def put(out, rows, table, width):
        high, low = halves(table)
        out[rows] = jnp.where(iota(table.shape, 1) < 2 * width, high.astype(F32), low.astype(F32)).astype(BF)

    def block(out, base, table, count):
        high, low = halves(table)
        zero = jnp.zeros((128, 128), BF)
        if count < 128:
            for at in (base, base + 128):
                out[pl.ds(at + count, 128 - count)] = jnp.zeros((128 - count, 256), BF)
        out[pl.ds(base, count), pl.ds(0, 128)] = high
        out[pl.ds(base, count), pl.ds(128, 128)] = low
        out[pl.ds(base + 128, count), pl.ds(0, 128)] = high
        out[pl.ds(base + 128, count), pl.ds(128, 128)] = zero[:count]

    def product(weights, table):
        high, low = halves(table)
        return dot(weights, high) + dot(weights, low)

    place0 = spread(iota((32, 192), 1), 64, ((0, 32, 0), (32, 42, -10), (48, 58, 32))) - iota((32, 192), 0) + RADIUS
    place1 = spread(iota((32, 144), 1), 48, ((0, 12, -11), (12, 30, -1), (30, 42, 15)))
    place1 = place1 - (iota((32, 144), 0) - 1) + RADIUS
    place2 = spread(iota((32, 144), 1), 48, ((0, 11, -1), (16, 27, -9), (27, 38, 7), (38, 43, -11), (43, 48, 15)))
    place2 = place2 - (iota((32, 144), 0) - 1) + RADIUS
    columns = iota((32, 32), 1) - 1
    lift1 = jnp.where(columns < 17, spline_of(iota((32, 32), 0) - 2 * columns), 0.0).astype(BF)
    lift2 = jnp.where(columns < 10, spline_of(iota((32, 32), 0) - 1 - 2 * columns), 0.0).astype(BF)
    lift2 = dot(lift1, lift2).astype(BF)
    up2 = cyclic_iota((64, 128), 0, 1, 128).astype(BF)
    up1[pl.ds(0, 128)] = cyclic_iota((128, 256), 0, 1, 256).astype(BF)
    up1[pl.ds(128, 128)] = cyclic_iota((128, 256), 0, 1, 256).astype(BF)
    for member in range(3):
        rows = pl.ds(32 * member, 32)
        put(y0, rows, pick(0, member, place0), 64)
        put(y1, rows, product(lift1, pick(1, member, place1)), 48)
        put(y2, rows, product(lift2, pick(2, member, place2)), 48)
        high, low = halves(cycle(0, member, 256))
        z0h[pl.ds(256 * member, 256)] = high
        z0l[pl.ds(256 * member, 256)] = low
        block(z1, 256 * member, cycle(1, member, 128), 128)
        high, low = halves(cycle(2, member, 64))
        block(z2, 256 * member, dot(high, up2) + dot(low, up2), 64)


def spline_iota(shape, offset, coarse_dim, fine_dim, keep=None):
    fine = lax.broadcasted_iota(jnp.int32, shape, fine_dim)
    coarse = lax.broadcasted_iota(jnp.int32, shape, coarse_dim)
    delta = fine - 2 * coarse + offset
    if keep is not None:
        delta = jnp.where(coarse < keep, delta, 99)
    return spline_of(delta)


def spline_of(delta):
    far = jnp.abs(delta)
    return jnp.where(far == 0, 0.75, jnp.where(far == 1, 0.5, jnp.where(far == 2, 0.125, 0.0)))


def cyclic_iota(shape, coarse_dim, fine_dim, fine_len):
    fine = lax.broadcasted_iota(jnp.int32, shape, fine_dim)
    coarse = lax.broadcasted_iota(jnp.int32, shape, coarse_dim)
    return spline_of(((fine - 2 * coarse + 2) & (fine_len - 1)) - 2)


def restrict_kernel(c, l1, l2, up1, down1, last, first, face_up, face_down, s1, s2):
    ry = spline_iota((24, 32), 2, 0, 1, 18).astype(BF)
    for i in range(-1, 17):
        high, low = halves(spline_sum(lambda r: c[r], i, 0, 31))
        s1[i + 1] = dot(ry, high) + dot(ry, low)
    for i in range(32):
        face_up[pl.ds(10 * i, 10)] = c[i, 22:32]
        face_down[pl.ds(10 * i, 10)] = c[i, 0:10]
    face_up[pl.ds(320, 8)] = jnp.zeros((8, 256), F32)
    face_down[pl.ds(320, 8)] = jnp.zeros((8, 256), F32)
    for r in range(10):
        last[pl.ds(32 * r, 32)] = c[22 + r]
        first[pl.ds(32 * r, 32)] = c[r]
    rz = cyclic_iota((256, 128), 1, 0, 256).astype(BF)
    high, low = halves(s1[...].reshape(18 * 24, 256))
    l1[...] = (dot(high, rz) + dot(low, rz)).reshape(18, 24, 128)
    ry2 = spline_iota((16, 24), 1, 0, 1, 11).astype(BF)
    for i in range(-1, 10):
        high, low = halves(spline_sum(lambda r: l1[r + 1], i, -1, 16))
        s2[i + 1] = dot(ry2, high) + dot(ry2, low)
    s2[11] = jnp.zeros((16, 128), F32)
    near = s2[pl.ds(0, 6)].reshape(96, 128)
    far = s2[pl.ds(6, 6)].reshape(96, 128)
    lanes = lax.broadcasted_iota(jnp.int32, (128, 128), 1)
    both = spline_of(((lax.broadcasted_iota(jnp.int32, (128, 128), 0) - 2 * (lanes & 63) + 2) & 127) - 2)
    total = jnp.zeros((96, 128), F32)
    for part, upper in ((near, False), (far, True)):
        weights = jnp.where((lanes >= 64) == upper, both, 0.0).astype(BF)
        high, low = halves(part)
        total = total + dot(high, weights) + dot(low, weights)
    total = total.reshape(6, 16, 128)
    l2[...] = total
    up1[pl.ds(64, 8)] = jnp.zeros((8, 128), F32)
    down1[pl.ds(64, 8)] = jnp.zeros((8, 128), F32)
    for j in range(6):
        up1[pl.ds(11 * j, 11)] = total[j, :11]
        down1[pl.ds(11 * j, 11)] = total[j, :11]
    for r in range(12):
        up1[pl.ds(72 + 18 * r, 18)] = l1[6 + r, :18]
        down1[pl.ds(72 + 18 * r, 18)] = l1[r, :18]


def paired(base, count, j):
    return (pl.ds(base + count * (j // 2), count), pl.ds(128 * (j % 2), 128))


def face_x_kernel(last, first, left, right, up, down):
    up[pl.ds(0, 320)] = last[...]
    down[pl.ds(0, 320)] = first[...]
    lower = lax.broadcasted_iota(jnp.int32, (11, 128), 1) < 64
    for p in range(3):
        even = 2 * p
        odd = min(even + 1, 4)
        a = left[pl.ds(11 * even, 11)]
        b = left[pl.ds(11 * odd, 11)]
        up[paired(320, 11, p)] = jnp.where(lower, pltpu.roll(a, 64, 1), b)
        a = right[pl.ds(11 * even, 11)]
        b = right[pl.ds(11 * odd, 11)]
        down[paired(320, 11, p)] = jnp.where(lower, a, pltpu.roll(b, 64, 1))


def gather_fine_kernel(l1, left, right, l1x, up, down):
    for i in range(38):
        if i < 12:
            l1x[i, :18] = left[pl.ds(72 + 18 * i, 18)]
            l1x[i, pl.ds(18, 6)] = jnp.zeros((6, 128), F32)
        elif i >= 26:
            l1x[i, :18] = right[pl.ds(72 + 18 * (i - 26), 18)]
            l1x[i, pl.ds(18, 6)] = jnp.zeros((6, 128), F32)
        if 10 <= i < 12 or 26 <= i < 28:
            l1x[i] = l1x[i] + l1[i - 10]
        elif 12 <= i < 26:
            l1x[i] = l1[i - 10]
    for i in range(38):
        up[pl.ds(12 * i, 12)] = l1x[i, 6:18]
        down[pl.ds(12 * i, 12)] = l1x[i, 0:12]


def gather_top_kernel(before, after, l2, left, right, l2x, up, down, up2, down2):
    for i in range(20):
        row = before[pl.ds(32 * i, 32)] if i < 10 else after[pl.ds(32 * (i - 10), 32)]
        up[pl.ds(10 * i, 10)] = row[22:32]
        down[pl.ds(10 * i, 10)] = row[0:10]
    up[pl.ds(200, 8)] = jnp.zeros((8, 256), F32)
    down[pl.ds(200, 8)] = jnp.zeros((8, 256), F32)
    lanes = lax.broadcasted_iota(jnp.int32, (11, 128), 1)
    lower = lanes < 64
    rolled = lambda x: pltpu.roll(x, 64, 1)
    for j in range(16):
        low = []
        high = []
        if j < 5:
            slab = before[paired(320, 11, j // 2)]
            low.append(slab if j % 2 == 0 else rolled(slab))
        if 2 <= j < 8:
            low.append(left[pl.ds(11 * (j - 2), 11)])
        if 8 <= j < 13:
            low.append(rolled(left[pl.ds(11 * (j - 8), 11)]))
        if j >= 10:
            low.append(l2[j - 10, :11])
        if j < 5:
            high.append(l2[j, :11])
        if 2 <= j < 8:
            high.append(rolled(right[pl.ds(11 * (j - 2), 11)]))
        if 8 <= j < 13:
            high.append(right[pl.ds(11 * (j - 8), 11)])
        if 10 <= j < 15:
            slab = after[paired(320, 11, (j - 10) // 2)]
            high.append(rolled(slab) if j % 2 == 0 else slab)
        row = jnp.where(lower, sum(low, jnp.zeros((11, 128), F32)), sum(high, jnp.zeros((11, 128), F32)))
        l2x[j, :11] = row
        l2x[j, pl.ds(11, 5)] = jnp.zeros((5, 128), F32)
        up[paired(208, 11, j)] = row
        down[paired(208, 11, j)] = row
        up2[pl.ds(5 * j, 5)] = row[6:11]
        down2[pl.ds(5 * j, 5)] = row[0:5]


def correlate_x(taps, level, v, w, count, many):
    @pl.loop(0, 12)
    def _(g):
        member = g // 4
        rows = pl.ds(pl.multiple_of(8 * g, 8), 8)
        scale = [taps[level, member, k] for k in range(TAPS)]
        for base in range(0, count, many):
            sums = [None] * many
            for i in range(base, base + many + TAPS - 1):
                value = v[i, rows]
                for m in range(many):
                    k = i - base - m
                    if 0 <= k < TAPS:
                        term = scale[k] * value
                        sums[m] = term if sums[m] is None else sums[m] + term
            for m in range(many):
                w[base + m, rows] = sums[m]


def correlate_z(w, count, table):
    total = jnp.zeros((count * 32, 256), F32)
    for member in range(3):
        high, low = halves(w[:, pl.ds(32 * member, 32)].reshape(count * 32, 128))
        total = total + dot(jnp.concatenate([high, low], 1), table[pl.ds(256 * member, 256)])
    return (total[:, :128] + total[:, 128:]).reshape(count, 32, 128)


def fine_level_kernel(taps, l1x, left, right, y1, z1, mid, f1, v1, w1):
    for i in range(38):
        f1[i, pl.ds(0, 12)] = left[pl.ds(12 * i, 12)]
        f1[i, pl.ds(12, 18)] = l1x[i, :18]
        f1[i, pl.ds(30, 12)] = right[pl.ds(12 * i, 12)]
        f1[i, pl.ds(42, 6)] = jnp.zeros((6, 128), F32)

    @pl.loop(0, 38, unroll=19)
    def _(i):
        high, low = halves(f1[i])
        v1[i] = dot(y1[...], jnp.concatenate([high, low, high], 0))

    correlate_x(taps, 1, v1, w1, 18, 9)
    mid[...] = correlate_z(w1, 18, z1)


def upper_kernel(taps, l2x, left, right, left2, right2, y2, z2, up1, mid_in, direct, out,
                 f2, v2, w2, mid, fine, done, sems):
    for j in range(16):
        f2[j, pl.ds(0, 16)] = l2x[j]
        f2[j, pl.ds(16, 11)] = left[paired(208, 11, j)]
        f2[j, pl.ds(27, 11)] = right[paired(208, 11, j)]
        f2[j, pl.ds(38, 5)] = left2[pl.ds(5 * j, 5)]
        f2[j, pl.ds(43, 5)] = right2[pl.ds(5 * j, 5)]

    @pl.loop(0, 16, unroll=16)
    def _(j):
        high, low = halves(f2[j])
        v = dot(y2[...], jnp.concatenate([high, low, high], 0))
        v2[j] = v
        v2[16 + j] = pltpu.roll(v, 64, 1)

    correlate_x(taps, 2, v2, w2, 11, 11)
    v2[pl.ds(0, 11), pl.ds(0, 32)] = correlate_z(w2, 11, z2)
    top = lambda i: v2[i + 1, pl.ds(0, 32)]
    for a in range(-1, 9):
        if a >= 0:
            mid[2 * a + 1] = mid_in[2 * a + 1] + (0.75 * top(a) + 0.125 * (top(a - 1) + top(a + 1)))
        if a < 8:
            mid[2 * a + 2] = mid_in[2 * a + 2] + 0.5 * (top(a) + top(a + 1))
    for a in range(16):
        fine[2 * a] = 0.75 * mid[a + 1] + 0.125 * (mid[a] + mid[a + 2])
        fine[2 * a + 1] = 0.5 * (mid[a + 1] + mid[a + 2])
    copies = []
    for q in range(4):
        rows = pl.ds(8 * q, 8)
        high, low = halves(fine[rows].reshape(256, 128))
        done[rows] = direct[rows] + dot(jnp.concatenate([high, low], 1), up1[...]).reshape(8, 32, 256)
        copies.append(pltpu.make_async_copy(done.at[rows], out.at[rows], sems.at[q]))
        copies[q].start()
    for copy in copies:
        copy.wait()


def section(table, own, left, right, base, at):
    b = left[pl.ds(base, 48)][10 * at:10 * at + 16]
    a = right[pl.ds(base, 48)][10 * at:10 * at + 16]
    high, low = halves(jnp.concatenate([own, b, a], 0))
    return dot(table[...], jnp.concatenate([high, low, high], 0))


def inner_kernel(taps, c, left, right, y0, z0h, z0l, out, v, wh, wl):
    @pl.loop(0, 8, unroll=4)
    def _(q):
        base = pl.multiple_of(40 * q, 8)
        for at in range(4):
            i = 4 * q + at
            v[i] = section(y0, c[i], left, right, base, at)

    @pl.loop(0, 4)
    def _(g):
        for member in range(3):
            rows = pl.ds(pl.multiple_of(32 * member + 8 * g, 8), 8)
            scale = [taps[0, member, k] for k in range(TAPS)]
            for h in range(2):
                lanes = pl.ds(128 * h, 128)
                for base in range(0, 32, 8):
                    sums = [None] * 8
                    for i in range(max(base - RADIUS, 0), min(base + 8 + RADIUS, 32)):
                        value = v[i, rows, lanes]
                        for m in range(8):
                            k = i - base - m + RADIUS
                            if 0 <= k < TAPS:
                                term = scale[k] * value
                                sums[m] = term if sums[m] is None else sums[m] + term
                    for m in range(0, 8, 2):
                        high, low = halves(jnp.concatenate([sums[m], sums[m + 1]], 0))
                        at = (pl.ds(8 * (base + m), 16), pl.ds(256 * member + 128 * h, 128))
                        wh[at] = high
                        wl[at] = low
        cols = pl.ds(pl.multiple_of(8 * g, 8), 8)
        total = dot(wh[...], z0h[...]) + dot(wl[...], z0h[...]) + dot(wh[...], z0l[...])
        out[:, cols] = total.reshape(32, 8, 256)


def finest_kernel(taps, before, after, left, right, y0, z0h, z0l, inner, out, v, wh, wl):
    for i in range(20):
        own = before[pl.ds(32 * i, 32)] if i < 10 else after[pl.ds(32 * (i - 10), 32)]
        b = left[pl.ds(10 * i, 16)]
        a = right[pl.ds(10 * i, 16)]
        high, low = halves(jnp.concatenate([own, b, a], 0))
        v[i] = dot(y0[...], jnp.concatenate([high, low, high], 0))

    @pl.loop(0, 4)
    def _(g):
        for member in range(3):
            rows = pl.ds(pl.multiple_of(32 * member + 8 * g, 8), 8)
            scale = [taps[0, member, k] for k in range(TAPS)]
            for h in range(2):
                lanes = pl.ds(128 * h, 128)
                sums = [None] * 20
                for r in range(20):
                    value = v[r, rows, lanes]
                    for m in range(10):
                        k = r - m if r < 10 else 20 + r - 10 - m
                        at = m if r < 10 else 10 + m
                        if r < 10 and m > r or r >= 10 and m < r - 10:
                            continue
                        term = scale[k] * value
                        sums[at] = term if sums[at] is None else sums[at] + term
                for m in range(0, 20, 2):
                    high, low = halves(jnp.concatenate([sums[m], sums[m + 1]], 0))
                    at = (pl.ds(8 * m, 16), pl.ds(256 * member + 128 * h, 128))
                    wh[at] = high
                    wl[at] = low
        cols = pl.ds(pl.multiple_of(8 * g, 8), 8)
        total = dot(wh[...], z0h[...]) + dot(wl[...], z0h[...]) + dot(wh[...], z0l[...])
        total = total.reshape(20, 8, 256)
        out[pl.ds(0, 10), cols] = inner[pl.ds(0, 10), cols] + total[:10]
        out[pl.ds(10, 12), cols] = inner[pl.ds(10, 12), cols]
        out[pl.ds(22, 10), cols] = inner[pl.ds(22, 10), cols] + total[10:]


def call(kernel, outs, scratch=(), scalars=0, count=0, flops=0, moved=0, name=None, sems=0, far=False):
    vmem = pl.BlockSpec(memory_space=pltpu.VMEM)
    smem = pl.BlockSpec(memory_space=pltpu.SMEM)
    hbm = pl.BlockSpec(memory_space=pltpu.HBM)
    shapes = [jax.ShapeDtypeStruct(*o) for o in outs]
    return pl.pallas_call(
        kernel,
        out_shape=shapes,
        in_specs=[smem] * scalars + [vmem] * (count - scalars),
        out_specs=[hbm if far else vmem] * len(shapes),
        scratch_shapes=[pltpu.VMEM(*s) for s in scratch] + [pltpu.SemaphoreType.DMA((sems,))] * (sems > 0),
        compiler_params=pltpu.CompilerParams(vmem_limit_bytes=VMEM_LIMIT),
        cost_estimate=pl.CostEstimate(flops=flops, bytes_accessed=moved, transcendentals=0),
        name=name,
    )


def shift(x, axis, by):
    n = lax.axis_size(axis)
    return lax.ppermute(x, axis, [(i, (i + by) % n) for i in range(n)])


def body(charges, kernel_taps):
    taps = kernel_taps
    l1, l2, s_up, s_down, last, first, o_up, o_down = call(
        restrict_kernel,
        [((18, 24, 128), F32), ((6, 16, 128), F32), ((288, 128), F32), ((288, 128), F32),
         ((320, 256), F32), ((320, 256), F32), ((328, 256), F32), ((328, 256), F32)],
        [((18, 24, 256), F32), ((12, 16, 128), F32)], 0, 1, 10**8, 2 * 10**6, name="restrict",
    )(charges)
    x_left = shift(s_up, "gx", 1)
    x_right = shift(s_down, "gx", -1)
    taps, l1 = lax.optimization_barrier((taps, l1))
    y0, y1, y2, z0h, z0l, z1, z2, up1 = call(
        matrices_kernel,
        [((96, 192), BF), ((96, 144), BF), ((96, 144), BF), ((768, 256), BF), ((768, 256), BF),
         ((768, 256), BF), ((768, 256), BF), ((256, 256), BF)],
        [], 1, 1, 10**8, 4 * 10**6, name="matrices",
    )(taps)
    own_left = shift(o_up, "gy", 1)
    own_right = shift(o_down, "gy", -1)
    x_left, x_right, y0 = lax.optimization_barrier((x_left, x_right, y0))
    c_up, c_down = call(
        face_x_kernel, [((344, 256), F32), ((344, 256), F32)], [], 0, 4, 2 * 10**10, 2 * 10**6, name="face_x",
    )(last, first, x_left, x_right)
    before = shift(c_up, "gx", 1)
    after = shift(c_down, "gx", -1)
    x_left, x_right, c_up = lax.optimization_barrier((x_left, x_right, c_up))
    l1x, g_up, g_down = call(
        gather_fine_kernel, [((38, 24, 128), F32), ((456, 128), F32), ((456, 128), F32)],
        [], 0, 3, 2 * 10**10, 2 * 10**6, name="gather_fine",
    )(l1, x_left, x_right)
    fine_left = shift(g_up, "gy", 1)
    fine_right = shift(g_down, "gy", -1)
    y0, g_up, g_down = lax.optimization_barrier((y0, g_up, g_down))
    inner, = call(
        inner_kernel, [((32, 32, 256), F32)],
        [((32, 96, 256), F32), ((256, 768), BF), ((256, 768), BF)], 1, 7, 2 * 10**9, 6 * 10**6, name="inner",
    )(taps, charges, own_left, own_right, y0, z0h, z0l)
    before, after, inner, fine_left, fine_right = lax.optimization_barrier(
        (before, after, inner, fine_left, fine_right)
    )
    l2x, f_up, f_down, t_up, t_down = call(
        gather_top_kernel,
        [((16, 16, 128), F32), ((296, 256), F32), ((296, 256), F32), ((80, 128), F32), ((80, 128), F32)],
        [], 0, 5, 10**6, 5 * 10**6, name="gather_top",
    )(before, after, l2, x_left, x_right)
    left = shift(f_up, "gy", 1)
    right = shift(f_down, "gy", -1)
    left2 = shift(t_up, "gy", 2)
    right2 = shift(t_down, "gy", -2)
    l1x, f_up, f_down = lax.optimization_barrier((l1x, f_up, f_down))
    mid, = call(
        fine_level_kernel, [((18, 32, 128), F32)],
        [((38, 48, 128), F32), ((38, 96, 128), F32), ((18, 96, 128), F32)],
        1, 6, 4 * 10**8, 4 * 10**6, name="fine_level",
    )(taps, l1x, fine_left, fine_right, y1, z1)
    left, right, mid = lax.optimization_barrier((left, right, mid))
    direct, = call(
        finest_kernel, [((32, 32, 256), F32)],
        [((20, 96, 256), F32), ((160, 768), BF), ((160, 768), BF)],
        1, 9, 2 * 10**9, 6 * 10**6, name="finest",
    )(taps, before, after, left, right, y0, z0h, z0l, inner)
    result, = call(
        upper_kernel, [((32, 32, 256), F32)],
        [((16, 48, 128), F32), ((32, 96, 128), F32), ((11, 96, 128), F32), ((18, 32, 128), F32),
         ((32, 32, 128), F32), ((32, 32, 256), F32)],
        1, 11, 4 * 10**8, 4 * 10**6, name="upper", sems=4, far=True,
    )(taps, l2x, left, right, left2, right2, y2, z2, up1, mid, direct)
    return result


def solution(mesh):
    return jax.shard_map(
        body,
        mesh=mesh,
        in_specs=(P("gx", "gy", None), P()),
        out_specs=P("gx", "gy", None),
        check_vma=False,
    )
```

```python
import jax
import jax.numpy as jnp
from jax import lax
from jax.experimental import pallas as pl
from jax.experimental.pallas import tpu as pltpu
from jax.sharding import PartitionSpec as P

SPLINE = (0.125, 0.5, 0.75, 0.5, 0.125)
RADIUS = 10
TAPS = 21
BF = jnp.bfloat16
F32 = jnp.float32
VMEM_LIMIT = 48 * 1024 * 1024
HINT = 2 * 10**10


def halves(x):
    high = x.astype(BF)
    return high, (x - high.astype(F32)).astype(BF)


def dot(a, b):
    return jnp.dot(a, b, preferred_element_type=F32)


def spline_sum(read, center, low, high):
    total = None
    for k in range(-2, 3):
        if low <= 2 * center + k <= high:
            term = SPLINE[k + 2] * read(2 * center + k)
            total = term if total is None else total + term
    return total


def matrices_kernel(taps, y0, y1, y2, z0h, z0l, z1, z2, up1):
    def iota(shape, dim):
        return lax.broadcasted_iota(jnp.int32, shape, dim)

    def pick(level, member, offsets):
        table = jnp.zeros(offsets.shape, F32)
        for k in range(TAPS):
            table = jnp.where(offsets == k, taps[level, member, k], table)
        return table

    def cycle(level, member, length):
        offsets = (iota((length, length), 0) - iota((length, length), 1) + RADIUS) & (length - 1)
        return pick(level, member, offsets)

    def spread(lanes, width, pieces):
        cols = lanes
        for _ in range(2):
            cols = jnp.where(cols >= width, cols - width, cols)
        place = jnp.full(lanes.shape, -99, jnp.int32)
        for begin, end, position in pieces:
            place = jnp.where((cols >= begin) & (cols < end), cols - begin + position, place)
        return place

    def put(out, rows, table, width):
        high, low = halves(table)
        out[rows] = jnp.where(iota(table.shape, 1) < 2 * width, high.astype(F32), low.astype(F32)).astype(BF)

    def block(out, base, table, count):
        high, low = halves(table)
        zero = jnp.zeros((128, 128), BF)
        if count < 128:
            for at in (base, base + 128):
                out[pl.ds(at + count, 128 - count)] = jnp.zeros((128 - count, 256), BF)
        out[pl.ds(base, count), pl.ds(0, 128)] = high
        out[pl.ds(base, count), pl.ds(128, 128)] = low
        out[pl.ds(base + 128, count), pl.ds(0, 128)] = high
        out[pl.ds(base + 128, count), pl.ds(128, 128)] = zero[:count]

    def product(weights, table):
        high, low = halves(table)
        return dot(weights, high) + dot(weights, low)

    place0 = spread(iota((32, 192), 1), 64, ((0, 32, 0), (32, 42, -10), (48, 58, 32))) - iota((32, 192), 0) + RADIUS
    place1 = spread(iota((32, 144), 1), 48, ((0, 12, -11), (12, 30, -1), (30, 42, 15)))
    place1 = place1 - (iota((32, 144), 0) - 1) + RADIUS
    place2 = spread(iota((32, 144), 1), 48, ((0, 11, -1), (16, 27, -9), (27, 38, 7), (38, 43, -11), (43, 48, 15)))
    place2 = place2 - (iota((32, 144), 0) - 1) + RADIUS
    columns = iota((32, 32), 1) - 1
    lift1 = jnp.where(columns < 17, spline_of(iota((32, 32), 0) - 2 * columns), 0.0).astype(BF)
    lift2 = jnp.where(columns < 10, spline_of(iota((32, 32), 0) - 1 - 2 * columns), 0.0).astype(BF)
    lift2 = dot(lift1, lift2).astype(BF)
    up2 = cyclic_iota((64, 128), 0, 1, 128).astype(BF)
    up1[pl.ds(0, 128)] = cyclic_iota((128, 256), 0, 1, 256).astype(BF)
    up1[pl.ds(128, 128)] = cyclic_iota((128, 256), 0, 1, 256).astype(BF)
    for member in range(3):
        rows = pl.ds(32 * member, 32)
        put(y0, rows, pick(0, member, place0), 64)
        put(y1, rows, product(lift1, pick(1, member, place1)), 48)
        put(y2, rows, product(lift2, pick(2, member, place2)), 48)
        high, low = halves(cycle(0, member, 256))
        z0h[pl.ds(256 * member, 256)] = high
        z0l[pl.ds(256 * member, 256)] = low
        block(z1, 256 * member, cycle(1, member, 128), 128)
        high, low = halves(cycle(2, member, 64))
        block(z2, 256 * member, dot(high, up2) + dot(low, up2), 64)


def spline_iota(shape, offset, coarse_dim, fine_dim, keep=None):
    fine = lax.broadcasted_iota(jnp.int32, shape, fine_dim)
    coarse = lax.broadcasted_iota(jnp.int32, shape, coarse_dim)
    delta = fine - 2 * coarse + offset
    if keep is not None:
        delta = jnp.where(coarse < keep, delta, 99)
    return spline_of(delta)


def spline_of(delta):
    far = jnp.abs(delta)
    return jnp.where(far == 0, 0.75, jnp.where(far == 1, 0.5, jnp.where(far == 2, 0.125, 0.0)))


def cyclic_iota(shape, coarse_dim, fine_dim, fine_len):
    fine = lax.broadcasted_iota(jnp.int32, shape, fine_dim)
    coarse = lax.broadcasted_iota(jnp.int32, shape, coarse_dim)
    return spline_of(((fine - 2 * coarse + 2) & (fine_len - 1)) - 2)


def restrict_kernel(c, l1, l2, up1, down1, last, first, face_up, face_down, s1, s2):
    for i in range(32):
        face_up[pl.ds(10 * i, 10)] = c[i, 22:32]
        face_down[pl.ds(10 * i, 10)] = c[i, 0:10]
    face_up[pl.ds(320, 8)] = jnp.zeros((8, 256), F32)
    face_down[pl.ds(320, 8)] = jnp.zeros((8, 256), F32)
    for r in range(10):
        last[pl.ds(32 * r, 32)] = c[22 + r]
        first[pl.ds(32 * r, 32)] = c[r]
    ry = spline_iota((24, 32), 2, 0, 1, 18).astype(BF)
    for i in range(-1, 17):
        high, low = halves(spline_sum(lambda r: c[r], i, 0, 31))
        s1[i + 1] = dot(ry, high) + dot(ry, low)
    rz = cyclic_iota((256, 128), 1, 0, 256).astype(BF)
    high, low = halves(s1[...].reshape(18 * 24, 256))
    l1[...] = (dot(high, rz) + dot(low, rz)).reshape(18, 24, 128)
    ry2 = spline_iota((16, 24), 1, 0, 1, 11).astype(BF)
    for i in range(-1, 10):
        high, low = halves(spline_sum(lambda r: l1[r + 1], i, -1, 16))
        s2[i + 1] = dot(ry2, high) + dot(ry2, low)
    s2[11] = jnp.zeros((16, 128), F32)
    near = s2[pl.ds(0, 6)].reshape(96, 128)
    far = s2[pl.ds(6, 6)].reshape(96, 128)
    lanes = lax.broadcasted_iota(jnp.int32, (128, 128), 1)
    both = spline_of(((lax.broadcasted_iota(jnp.int32, (128, 128), 0) - 2 * (lanes & 63) + 2) & 127) - 2)
    total = jnp.zeros((96, 128), F32)
    for part, upper in ((near, False), (far, True)):
        weights = jnp.where((lanes >= 64) == upper, both, 0.0).astype(BF)
        high, low = halves(part)
        total = total + dot(high, weights) + dot(low, weights)
    total = total.reshape(6, 16, 128)
    l2[...] = total
    up1[pl.ds(64, 8)] = jnp.zeros((8, 128), F32)
    down1[pl.ds(64, 8)] = jnp.zeros((8, 128), F32)
    for j in range(6):
        up1[pl.ds(11 * j, 11)] = total[j, :11]
        down1[pl.ds(11 * j, 11)] = total[j, :11]
    for r in range(12):
        up1[pl.ds(72 + 18 * r, 18)] = l1[6 + r, :18]
        down1[pl.ds(72 + 18 * r, 18)] = l1[r, :18]


def paired(base, count, j):
    return (pl.ds(base + count * (j // 2), count), pl.ds(128 * (j % 2), 128))


def forward_kernel(left, right, up, down):
    lower = lax.broadcasted_iota(jnp.int32, (11, 128), 1) < 64
    for p in range(3):
        even = 2 * p
        odd = min(even + 1, 4)
        rows = pl.ds(11 * p, 11)
        a = left[pl.ds(11 * even, 11)]
        b = left[pl.ds(11 * odd, 11)]
        up[rows] = jnp.where(lower, pltpu.roll(a, 64, 1), b)
        a = right[pl.ds(11 * even, 11)]
        b = right[pl.ds(11 * odd, 11)]
        down[rows] = jnp.where(lower, a, pltpu.roll(b, 64, 1))


def gather_kernel(l1, l2, left, right, left2, right2, l1x, l2x, up, down, up2, down2):
    for i in range(38):
        if i < 12:
            l1x[i, :18] = left[pl.ds(72 + 18 * i, 18)]
            l1x[i, pl.ds(18, 6)] = jnp.zeros((6, 128), F32)
        elif i >= 26:
            l1x[i, :18] = right[pl.ds(72 + 18 * (i - 26), 18)]
            l1x[i, pl.ds(18, 6)] = jnp.zeros((6, 128), F32)
        if 10 <= i < 12 or 26 <= i < 28:
            l1x[i] = l1x[i] + l1[i - 10]
        elif 12 <= i < 26:
            l1x[i] = l1[i - 10]
    for i in range(38):
        up[paired(0, 12, i)] = l1x[i, 6:18]
        down[paired(0, 12, i)] = l1x[i, 0:12]
    lanes = lax.broadcasted_iota(jnp.int32, (11, 128), 1)
    lower = lanes < 64
    rolled = lambda x: pltpu.roll(x, 64, 1)
    for j in range(16):
        low = []
        high = []
        if j < 5:
            slab = left2[pl.ds(11 * (j // 2), 11)]
            low.append(slab if j % 2 == 0 else rolled(slab))
        if 2 <= j < 8:
            low.append(left[pl.ds(11 * (j - 2), 11)])
        if 8 <= j < 13:
            low.append(rolled(left[pl.ds(11 * (j - 8), 11)]))
        if j >= 10:
            low.append(l2[j - 10, :11])
        if j < 5:
            high.append(l2[j, :11])
        if 2 <= j < 8:
            high.append(rolled(right[pl.ds(11 * (j - 2), 11)]))
        if 8 <= j < 13:
            high.append(right[pl.ds(11 * (j - 8), 11)])
        if 10 <= j < 15:
            slab = right2[pl.ds(11 * ((j - 10) // 2), 11)]
            high.append(rolled(slab) if j % 2 == 0 else slab)
        row = jnp.where(lower, sum(low, jnp.zeros((11, 128), F32)), sum(high, jnp.zeros((11, 128), F32)))
        l2x[j, :11] = row
        l2x[j, pl.ds(11, 5)] = jnp.zeros((5, 128), F32)
        up[paired(228, 11, j)] = row
        down[paired(228, 11, j)] = row
        up2[pl.ds(5 * j, 5)] = row[6:11]
        down2[pl.ds(5 * j, 5)] = row[0:5]


def corner_kernel(before, after, up, down):
    for i in range(20):
        row = before[pl.ds(32 * i, 32)] if i < 10 else after[pl.ds(32 * (i - 10), 32)]
        up[pl.ds(10 * i, 10)] = row[22:32]
        down[pl.ds(10 * i, 10)] = row[0:10]
    up[pl.ds(200, 8)] = jnp.zeros((8, 256), F32)
    down[pl.ds(200, 8)] = jnp.zeros((8, 256), F32)


def correlate_x(taps, level, v, w, count, many):
    @pl.loop(0, 12)
    def _(g):
        member = g // 4
        rows = pl.ds(pl.multiple_of(8 * g, 8), 8)
        scale = [taps[level, member, k] for k in range(TAPS)]
        for base in range(0, count, many):
            sums = [None] * many
            for i in range(base, base + many + TAPS - 1):
                value = v[i, rows]
                for m in range(many):
                    k = i - base - m
                    if 0 <= k < TAPS:
                        term = scale[k] * value
                        sums[m] = term if sums[m] is None else sums[m] + term
            for m in range(many):
                w[base + m, rows] = sums[m]


def correlate_z(w, count, table):
    total = jnp.zeros((count * 32, 256), F32)
    for member in range(3):
        high, low = halves(w[:, pl.ds(32 * member, 32)].reshape(count * 32, 128))
        total = total + dot(jnp.concatenate([high, low], 1), table[pl.ds(256 * member, 256)])
    return (total[:, :128] + total[:, 128:]).reshape(count, 32, 128)


def fine_level_kernel(taps, l1x, left, right, y1, z1, mid, f1, v1, w1):
    for i in range(38):
        f1[i, pl.ds(0, 12)] = left[paired(0, 12, i)]
        f1[i, pl.ds(12, 18)] = l1x[i, :18]
        f1[i, pl.ds(30, 12)] = right[paired(0, 12, i)]
        f1[i, pl.ds(42, 6)] = jnp.zeros((6, 128), F32)

    @pl.loop(0, 38, unroll=19)
    def _(i):
        high, low = halves(f1[i])
        v1[i] = dot(y1[...], jnp.concatenate([high, low, high], 0))

    correlate_x(taps, 1, v1, w1, 18, 9)
    mid[...] = correlate_z(w1, 18, z1)


def upper_kernel(taps, l2x, left, right, left2, right2, y2, z2, up1, mid_in, direct, out,
                 f2, v2, w2, mid, fine):
    for j in range(16):
        f2[j, pl.ds(0, 16)] = l2x[j]
        f2[j, pl.ds(16, 11)] = left[paired(228, 11, j)]
        f2[j, pl.ds(27, 11)] = right[paired(228, 11, j)]
        f2[j, pl.ds(38, 5)] = left2[pl.ds(5 * j, 5)]
        f2[j, pl.ds(43, 5)] = right2[pl.ds(5 * j, 5)]

    @pl.loop(0, 16, unroll=16)
    def _(j):
        high, low = halves(f2[j])
        v = dot(y2[...], jnp.concatenate([high, low, high], 0))
        v2[j] = v
        v2[16 + j] = pltpu.roll(v, 64, 1)

    correlate_x(taps, 2, v2, w2, 11, 11)
    v2[pl.ds(0, 11), pl.ds(0, 32)] = correlate_z(w2, 11, z2)
    top = lambda i: v2[i + 1, pl.ds(0, 32)]
    for a in range(-1, 9):
        if a >= 0:
            mid[2 * a + 1] = mid_in[2 * a + 1] + (0.75 * top(a) + 0.125 * (top(a - 1) + top(a + 1)))
        if a < 8:
            mid[2 * a + 2] = mid_in[2 * a + 2] + 0.5 * (top(a) + top(a + 1))
    for a in range(16):
        fine[2 * a] = 0.75 * mid[a + 1] + 0.125 * (mid[a] + mid[a + 2])
        fine[2 * a + 1] = 0.5 * (mid[a + 1] + mid[a + 2])
    for q in range(4):
        rows = pl.ds(8 * q, 8)
        high, low = halves(fine[rows].reshape(256, 128))
        out[rows] = direct[rows] + dot(jnp.concatenate([high, low], 1), up1[...]).reshape(8, 32, 256)


def section(table, own, left, right, base, at):
    b = left[pl.ds(base, 48)][10 * at:10 * at + 16]
    a = right[pl.ds(base, 48)][10 * at:10 * at + 16]
    high, low = halves(jnp.concatenate([own, b, a], 0))
    return dot(table[...], jnp.concatenate([high, low, high], 0))


def inner_kernel(taps, c, left, right, y0, z0h, z0l, out, v, wh, wl):
    @pl.loop(0, 8, unroll=4)
    def _(q):
        base = pl.multiple_of(40 * q, 8)
        for at in range(4):
            i = 4 * q + at
            v[i] = section(y0, c[i], left, right, base, at)

    @pl.loop(0, 4)
    def _(g):
        for member in range(3):
            rows = pl.ds(pl.multiple_of(32 * member + 8 * g, 8), 8)
            scale = [taps[0, member, k] for k in range(TAPS)]
            for h in range(2):
                lanes = pl.ds(128 * h, 128)
                for base in range(0, 32, 8):
                    sums = [None] * 8
                    for i in range(max(base - RADIUS, 0), min(base + 8 + RADIUS, 32)):
                        value = v[i, rows, lanes]
                        for m in range(8):
                            k = i - base - m + RADIUS
                            if 0 <= k < TAPS:
                                term = scale[k] * value
                                sums[m] = term if sums[m] is None else sums[m] + term
                    for m in range(0, 8, 2):
                        high, low = halves(jnp.concatenate([sums[m], sums[m + 1]], 0))
                        at = (pl.ds(8 * (base + m), 16), pl.ds(256 * member + 128 * h, 128))
                        wh[at] = high
                        wl[at] = low
        cols = pl.ds(pl.multiple_of(8 * g, 8), 8)
        total = dot(wh[...], z0h[...]) + dot(wl[...], z0h[...]) + dot(wh[...], z0l[...])
        out[:, cols] = total.reshape(32, 8, 256)


def finest_kernel(taps, before, after, left, right, y0, z0h, z0l, inner, out, v, wh, wl, done, sems):
    for i in range(20):
        own = before[pl.ds(32 * i, 32)] if i < 10 else after[pl.ds(32 * (i - 10), 32)]
        b = left[pl.ds(10 * i, 16)]
        a = right[pl.ds(10 * i, 16)]
        high, low = halves(jnp.concatenate([own, b, a], 0))
        v[i] = dot(y0[...], jnp.concatenate([high, low, high], 0))

    @pl.loop(0, 4)
    def _(g):
        for member in range(3):
            rows = pl.ds(pl.multiple_of(32 * member + 8 * g, 8), 8)
            scale = [taps[0, member, k] for k in range(TAPS)]
            for h in range(2):
                lanes = pl.ds(128 * h, 128)
                sums = [None] * 20
                for r in range(20):
                    value = v[r, rows, lanes]
                    for m in range(10):
                        k = r - m if r < 10 else 20 + r - 10 - m
                        at = m if r < 10 else 10 + m
                        if r < 10 and m > r or r >= 10 and m < r - 10:
                            continue
                        term = scale[k] * value
                        sums[at] = term if sums[at] is None else sums[at] + term
                for m in range(0, 20, 2):
                    high, low = halves(jnp.concatenate([sums[m], sums[m + 1]], 0))
                    at = (pl.ds(8 * m, 16), pl.ds(256 * member + 128 * h, 128))
                    wh[at] = high
                    wl[at] = low
        cols = pl.ds(pl.multiple_of(8 * g, 8), 8)
        total = dot(wh[...], z0h[...]) + dot(wl[...], z0h[...]) + dot(wh[...], z0l[...])
        total = total.reshape(20, 8, 256)
        done[pl.ds(0, 10), cols] = inner[pl.ds(0, 10), cols] + total[:10]
        done[pl.ds(10, 12), cols] = inner[pl.ds(10, 12), cols]
        done[pl.ds(22, 10), cols] = inner[pl.ds(22, 10), cols] + total[10:]
        pltpu.make_async_copy(done.at[:, cols], out.at[:, cols], sems.at[g]).start()

    for g in range(4):
        cols = pl.ds(8 * g, 8)
        pltpu.make_async_copy(done.at[:, cols], out.at[:, cols], sems.at[g]).wait()


def call(kernel, outs, scratch=(), scalars=0, count=0, flops=0, moved=0, name=None, sems=0, far=False):
    vmem = pl.BlockSpec(memory_space=pltpu.VMEM)
    smem = pl.BlockSpec(memory_space=pltpu.SMEM)
    hbm = pl.BlockSpec(memory_space=pltpu.HBM)
    shapes = [jax.ShapeDtypeStruct(*o) for o in outs]
    return pl.pallas_call(
        kernel,
        out_shape=shapes,
        in_specs=[smem] * scalars + [vmem] * (count - scalars),
        out_specs=[hbm if far else vmem] * len(shapes),
        scratch_shapes=[pltpu.VMEM(*s) for s in scratch] + [pltpu.SemaphoreType.DMA((sems,))] * (sems > 0),
        compiler_params=pltpu.CompilerParams(vmem_limit_bytes=VMEM_LIMIT),
        cost_estimate=pl.CostEstimate(flops=flops, bytes_accessed=moved, transcendentals=0),
        name=name,
    )


def shift(x, axis, by):
    n = lax.axis_size(axis)
    return lax.ppermute(x, axis, [(i, (i + by) % n) for i in range(n)])


def body(charges, kernel_taps):
    taps = kernel_taps
    l1, l2, s_up, s_down, last, first, o_up, o_down = call(
        restrict_kernel,
        [((18, 24, 128), F32), ((6, 16, 128), F32), ((288, 128), F32), ((288, 128), F32),
         ((320, 256), F32), ((320, 256), F32), ((328, 256), F32), ((328, 256), F32)],
        [((18, 24, 256), F32), ((12, 16, 128), F32)], 0, 1, 10**8, 2 * 10**6, name="restrict",
    )(charges)
    x_left = shift(s_up, "gx", 1)
    x_right = shift(s_down, "gx", -1)
    own_left = shift(o_up, "gy", 1)
    own_right = shift(o_down, "gy", -1)
    taps, l1 = lax.optimization_barrier((taps, l1))
    y0, y1, y2, z0h, z0l, z1, z2, up1 = call(
        matrices_kernel,
        [((96, 192), BF), ((96, 144), BF), ((96, 144), BF), ((768, 256), BF), ((768, 256), BF),
         ((768, 256), BF), ((768, 256), BF), ((256, 256), BF)],
        [], 1, 1, 10**8, 4 * 10**6, name="matrices",
    )(taps)
    x_left, x_right, y0 = lax.optimization_barrier((x_left, x_right, y0))
    c_up, c_down = call(
        forward_kernel, [((40, 128), F32), ((40, 128), F32)], [], 0, 2, HINT, 0, name="forward",
    )(x_left, x_right)
    x_left2 = shift(c_up, "gx", 1)
    x_right2 = shift(c_down, "gx", -1)
    last, first, c_up, c_down = lax.optimization_barrier((last, first, c_up, c_down))
    before = shift(last, "gx", 1)
    after = shift(first, "gx", -1)
    l1x, l2x, g_up, g_down, t_up, t_down = call(
        gather_kernel,
        [((38, 24, 128), F32), ((16, 16, 128), F32), ((316, 256), F32), ((316, 256), F32),
         ((80, 128), F32), ((80, 128), F32)],
        [], 0, 6, 0, 0, name="gather",
    )(l1, l2, x_left, x_right, x_left2, x_right2)
    left = shift(g_up, "gy", 1)
    right = shift(g_down, "gy", -1)
    left2 = shift(t_up, "gy", 2)
    right2 = shift(t_down, "gy", -2)
    y0, g_up, g_down = lax.optimization_barrier((y0, g_up, g_down))
    inner, = call(
        inner_kernel, [((32, 32, 256), F32)],
        [((32, 96, 256), F32), ((256, 768), BF), ((256, 768), BF)], 1, 7, 3 * 10**9, 6 * 10**6, name="inner",
    )(taps, charges, own_left, own_right, y0, z0h, z0l)
    before, after, left2, right2, inner = lax.optimization_barrier((before, after, left2, right2, inner))
    f_up, f_down = call(
        corner_kernel, [((208, 256), F32), ((208, 256), F32)], [], 0, 2, 10**6, 10**6, name="corner",
    )(before, after)
    corner_left = shift(f_up, "gy", 1)
    corner_right = shift(f_down, "gy", -1)
    l1x, f_up, f_down = lax.optimization_barrier((l1x, f_up, f_down))
    mid, = call(
        fine_level_kernel, [((18, 32, 128), F32)],
        [((38, 48, 128), F32), ((38, 96, 128), F32), ((18, 96, 128), F32)],
        1, 6, 4 * 10**8, 4 * 10**6, name="fine_level",
    )(taps, l1x, left, right, y1, z1)
    partial, = call(
        upper_kernel, [((32, 32, 256), F32)],
        [((16, 48, 128), F32), ((32, 96, 128), F32), ((11, 96, 128), F32), ((18, 32, 128), F32),
         ((32, 32, 128), F32)],
        1, 11, 4 * 10**8, 4 * 10**6, name="upper",
    )(taps, l2x, left, right, left2, right2, y2, z2, up1, mid, inner)
    corner_left, corner_right, partial = lax.optimization_barrier((corner_left, corner_right, partial))
    result, = call(
        finest_kernel, [((32, 32, 256), F32)],
        [((20, 96, 256), F32), ((160, 768), BF), ((160, 768), BF), ((32, 32, 256), F32)],
        1, 9, 2 * 10**9, 6 * 10**6, name="finest", sems=4, far=True,
    )(taps, before, after, corner_left, corner_right, y0, z0h, z0l, partial)
    return result


def solution(mesh):
    return jax.shard_map(
        body,
        mesh=mesh,
        in_specs=(P("gx", "gy", None), P()),
        out_specs=P("gx", "gy", None),
        check_vma=False,
    )
```

```python
import jax
import jax.numpy as jnp
from jax import lax
from jax.experimental import pallas as pl
from jax.experimental.pallas import tpu as pltpu
from jax.sharding import PartitionSpec as P

SPLINE = (0.125, 0.5, 0.75, 0.5, 0.125)
RADIUS = 10
TAPS = 21
BF = jnp.bfloat16
F32 = jnp.float32
VMEM_LIMIT = 48 * 1024 * 1024


def halves(x):
    high = x.astype(BF)
    return high, (x - high.astype(F32)).astype(BF)


def dot(a, b):
    return jnp.dot(a, b, preferred_element_type=F32)


def spline_sum(read, center, low, high):
    total = None
    for k in range(-2, 3):
        if low <= 2 * center + k <= high:
            term = SPLINE[k + 2] * read(2 * center + k)
            total = term if total is None else total + term
    return total


def matrices_kernel(taps, y0, y1, y2, z0h, z0l, z1, z2, up1):
    def iota(shape, dim):
        return lax.broadcasted_iota(jnp.int32, shape, dim)

    def pick(level, member, offsets):
        table = jnp.zeros(offsets.shape, F32)
        for k in range(TAPS):
            table = jnp.where(offsets == k, taps[level, member, k], table)
        return table

    def cycle(level, member, length):
        offsets = (iota((length, length), 0) - iota((length, length), 1) + RADIUS) & (length - 1)
        return pick(level, member, offsets)

    def spread(lanes, width, pieces):
        cols = lanes
        for _ in range(2):
            cols = jnp.where(cols >= width, cols - width, cols)
        place = jnp.full(lanes.shape, -99, jnp.int32)
        for begin, end, position in pieces:
            place = jnp.where((cols >= begin) & (cols < end), cols - begin + position, place)
        return place

    def put(out, rows, table, width):
        high, low = halves(table)
        out[rows] = jnp.where(iota(table.shape, 1) < 2 * width, high.astype(F32), low.astype(F32)).astype(BF)

    def block(out, base, table, count):
        high, low = halves(table)
        zero = jnp.zeros((128, 128), BF)
        if count < 128:
            for at in (base, base + 128):
                out[pl.ds(at + count, 128 - count)] = jnp.zeros((128 - count, 256), BF)
        out[pl.ds(base, count), pl.ds(0, 128)] = high
        out[pl.ds(base, count), pl.ds(128, 128)] = low
        out[pl.ds(base + 128, count), pl.ds(0, 128)] = high
        out[pl.ds(base + 128, count), pl.ds(128, 128)] = zero[:count]

    def product(weights, table):
        high, low = halves(table)
        return dot(weights, high) + dot(weights, low)

    place0 = spread(iota((32, 192), 1), 64, ((0, 32, 0), (32, 42, -10), (48, 58, 32))) - iota((32, 192), 0) + RADIUS
    place1 = spread(iota((32, 144), 1), 48, ((0, 12, -11), (12, 30, -1), (30, 42, 15)))
    place1 = place1 - (iota((32, 144), 0) - 1) + RADIUS
    place2 = spread(iota((32, 144), 1), 48, ((0, 11, -1), (16, 27, -9), (27, 38, 7), (38, 43, -11), (43, 48, 15)))
    place2 = place2 - (iota((32, 144), 0) - 1) + RADIUS
    columns = iota((32, 32), 1) - 1
    lift1 = jnp.where(columns < 17, spline_of(iota((32, 32), 0) - 2 * columns), 0.0).astype(BF)
    lift2 = jnp.where(columns < 10, spline_of(iota((32, 32), 0) - 1 - 2 * columns), 0.0).astype(BF)
    lift2 = dot(lift1, lift2).astype(BF)
    up2 = cyclic_iota((64, 128), 0, 1, 128).astype(BF)
    up1[pl.ds(0, 128)] = cyclic_iota((128, 256), 0, 1, 256).astype(BF)
    up1[pl.ds(128, 128)] = cyclic_iota((128, 256), 0, 1, 256).astype(BF)
    for member in range(3):
        rows = pl.ds(32 * member, 32)
        put(y0, rows, pick(0, member, place0), 64)
        put(y1, rows, product(lift1, pick(1, member, place1)), 48)
        put(y2, rows, product(lift2, pick(2, member, place2)), 48)
        high, low = halves(cycle(0, member, 256))
        z0h[pl.ds(256 * member, 256)] = high
        z0l[pl.ds(256 * member, 256)] = low
        block(z1, 256 * member, cycle(1, member, 128), 128)
        high, low = halves(cycle(2, member, 64))
        block(z2, 256 * member, dot(high, up2) + dot(low, up2), 64)


def spline_iota(shape, offset, coarse_dim, fine_dim, keep=None):
    fine = lax.broadcasted_iota(jnp.int32, shape, fine_dim)
    coarse = lax.broadcasted_iota(jnp.int32, shape, coarse_dim)
    delta = fine - 2 * coarse + offset
    if keep is not None:
        delta = jnp.where(coarse < keep, delta, 99)
    return spline_of(delta)


def spline_of(delta):
    far = jnp.abs(delta)
    return jnp.where(far == 0, 0.75, jnp.where(far == 1, 0.5, jnp.where(far == 2, 0.125, 0.0)))


def cyclic_iota(shape, coarse_dim, fine_dim, fine_len):
    fine = lax.broadcasted_iota(jnp.int32, shape, fine_dim)
    coarse = lax.broadcasted_iota(jnp.int32, shape, coarse_dim)
    return spline_of(((fine - 2 * coarse + 2) & (fine_len - 1)) - 2)


def restrict_kernel(c, l1, l2, up1, down1, last, first, face_up, face_down, s1, s2):
    ry = spline_iota((24, 32), 2, 0, 1, 18).astype(BF)
    for i in range(-1, 17):
        high, low = halves(spline_sum(lambda r: c[r], i, 0, 31))
        s1[i + 1] = dot(ry, high) + dot(ry, low)
    for i in range(32):
        face_up[pl.ds(10 * i, 10)] = c[i, 22:32]
        face_down[pl.ds(10 * i, 10)] = c[i, 0:10]
    face_up[pl.ds(320, 8)] = jnp.zeros((8, 256), F32)
    face_down[pl.ds(320, 8)] = jnp.zeros((8, 256), F32)
    for r in range(10):
        last[pl.ds(32 * r, 32)] = c[22 + r]
        first[pl.ds(32 * r, 32)] = c[r]
    rz = cyclic_iota((256, 128), 1, 0, 256).astype(BF)
    high, low = halves(s1[...].reshape(18 * 24, 256))
    l1[...] = (dot(high, rz) + dot(low, rz)).reshape(18, 24, 128)
    ry2 = spline_iota((16, 24), 1, 0, 1, 11).astype(BF)
    for i in range(-1, 10):
        high, low = halves(spline_sum(lambda r: l1[r + 1], i, -1, 16))
        s2[i + 1] = dot(ry2, high) + dot(ry2, low)
    s2[11] = jnp.zeros((16, 128), F32)
    near = s2[pl.ds(0, 6)].reshape(96, 128)
    far = s2[pl.ds(6, 6)].reshape(96, 128)
    lanes = lax.broadcasted_iota(jnp.int32, (128, 128), 1)
    both = spline_of(((lax.broadcasted_iota(jnp.int32, (128, 128), 0) - 2 * (lanes & 63) + 2) & 127) - 2)
    total = jnp.zeros((96, 128), F32)
    for part, upper in ((near, False), (far, True)):
        weights = jnp.where((lanes >= 64) == upper, both, 0.0).astype(BF)
        high, low = halves(part)
        total = total + dot(high, weights) + dot(low, weights)
    total = total.reshape(6, 16, 128)
    l2[...] = total
    up1[pl.ds(64, 8)] = jnp.zeros((8, 128), F32)
    down1[pl.ds(64, 8)] = jnp.zeros((8, 128), F32)
    for j in range(6):
        up1[pl.ds(11 * j, 11)] = total[j, :11]
        down1[pl.ds(11 * j, 11)] = total[j, :11]
    for r in range(12):
        up1[pl.ds(72 + 18 * r, 18)] = l1[6 + r, :18]
        down1[pl.ds(72 + 18 * r, 18)] = l1[r, :18]


def paired(base, count, j):
    return (pl.ds(base + count * (j // 2), count), pl.ds(128 * (j % 2), 128))


def face_x_kernel(last, first, left, right, up, down):
    up[pl.ds(0, 320)] = last[...]
    down[pl.ds(0, 320)] = first[...]
    lower = lax.broadcasted_iota(jnp.int32, (11, 128), 1) < 64
    for p in range(3):
        even = 2 * p
        odd = min(even + 1, 4)
        a = left[pl.ds(11 * even, 11)]
        b = left[pl.ds(11 * odd, 11)]
        up[paired(320, 11, p)] = jnp.where(lower, pltpu.roll(a, 64, 1), b)
        a = right[pl.ds(11 * even, 11)]
        b = right[pl.ds(11 * odd, 11)]
        down[paired(320, 11, p)] = jnp.where(lower, a, pltpu.roll(b, 64, 1))


def gather_fine_kernel(l1, left, right, l1x, up, down):
    for i in range(38):
        if i < 12:
            l1x[i, :18] = left[pl.ds(72 + 18 * i, 18)]
            l1x[i, pl.ds(18, 6)] = jnp.zeros((6, 128), F32)
        elif i >= 26:
            l1x[i, :18] = right[pl.ds(72 + 18 * (i - 26), 18)]
            l1x[i, pl.ds(18, 6)] = jnp.zeros((6, 128), F32)
        if 10 <= i < 12 or 26 <= i < 28:
            l1x[i] = l1x[i] + l1[i - 10]
        elif 12 <= i < 26:
            l1x[i] = l1[i - 10]
    for i in range(38):
        up[pl.ds(12 * i, 12)] = l1x[i, 6:18]
        down[pl.ds(12 * i, 12)] = l1x[i, 0:12]


def gather_top_kernel(before, after, l2, left, right, l2x, up, down, up2, down2):
    for i in range(20):
        row = before[pl.ds(32 * i, 32)] if i < 10 else after[pl.ds(32 * (i - 10), 32)]
        up[pl.ds(10 * i, 10)] = row[22:32]
        down[pl.ds(10 * i, 10)] = row[0:10]
    up[pl.ds(200, 8)] = jnp.zeros((8, 256), F32)
    down[pl.ds(200, 8)] = jnp.zeros((8, 256), F32)
    lanes = lax.broadcasted_iota(jnp.int32, (11, 128), 1)
    lower = lanes < 64
    rolled = lambda x: pltpu.roll(x, 64, 1)
    for j in range(16):
        low = []
        high = []
        if j < 5:
            slab = before[paired(320, 11, j // 2)]
            low.append(slab if j % 2 == 0 else rolled(slab))
        if 2 <= j < 8:
            low.append(left[pl.ds(11 * (j - 2), 11)])
        if 8 <= j < 13:
            low.append(rolled(left[pl.ds(11 * (j - 8), 11)]))
        if j >= 10:
            low.append(l2[j - 10, :11])
        if j < 5:
            high.append(l2[j, :11])
        if 2 <= j < 8:
            high.append(rolled(right[pl.ds(11 * (j - 2), 11)]))
        if 8 <= j < 13:
            high.append(right[pl.ds(11 * (j - 8), 11)])
        if 10 <= j < 15:
            slab = after[paired(320, 11, (j - 10) // 2)]
            high.append(rolled(slab) if j % 2 == 0 else slab)
        row = jnp.where(lower, sum(low, jnp.zeros((11, 128), F32)), sum(high, jnp.zeros((11, 128), F32)))
        l2x[j, :11] = row
        l2x[j, pl.ds(11, 5)] = jnp.zeros((5, 128), F32)
        up[paired(208, 11, j)] = row
        down[paired(208, 11, j)] = row
        up2[pl.ds(5 * j, 5)] = row[6:11]
        down2[pl.ds(5 * j, 5)] = row[0:5]


def correlate_x(taps, level, v, w, count, many):
    @pl.loop(0, 12)
    def _(g):
        member = g // 4
        rows = pl.ds(pl.multiple_of(8 * g, 8), 8)
        scale = [taps[level, member, k] for k in range(TAPS)]
        for base in range(0, count, many):
            sums = [None] * many
            for i in range(base, base + many + TAPS - 1):
                value = v[i, rows]
                for m in range(many):
                    k = i - base - m
                    if 0 <= k < TAPS:
                        term = scale[k] * value
                        sums[m] = term if sums[m] is None else sums[m] + term
            for m in range(many):
                w[base + m, rows] = sums[m]


def correlate_z(w, count, table):
    total = jnp.zeros((count * 32, 256), F32)
    for member in range(3):
        high, low = halves(w[:, pl.ds(32 * member, 32)].reshape(count * 32, 128))
        total = total + dot(jnp.concatenate([high, low], 1), table[pl.ds(256 * member, 256)])
    return (total[:, :128] + total[:, 128:]).reshape(count, 32, 128)


def fine_level_kernel(taps, l1x, left, right, y1, z1, mid, f1, v1, w1):
    for i in range(38):
        f1[i, pl.ds(0, 12)] = left[pl.ds(12 * i, 12)]
        f1[i, pl.ds(12, 18)] = l1x[i, :18]
        f1[i, pl.ds(30, 12)] = right[pl.ds(12 * i, 12)]
        f1[i, pl.ds(42, 6)] = jnp.zeros((6, 128), F32)

    @pl.loop(0, 38, unroll=19)
    def _(i):
        high, low = halves(f1[i])
        v1[i] = dot(y1[...], jnp.concatenate([high, low, high], 0))

    correlate_x(taps, 1, v1, w1, 18, 9)
    mid[...] = correlate_z(w1, 18, z1)


def upper_part(taps, l2x, left, right, left2, right2, y2, z2, up1, mid_in, direct, out,
                 f2, v2, w2, mid, fine, done, sems):
    for j in range(16):
        f2[j, pl.ds(0, 16)] = l2x[j]
        f2[j, pl.ds(16, 11)] = left[paired(208, 11, j)]
        f2[j, pl.ds(27, 11)] = right[paired(208, 11, j)]
        f2[j, pl.ds(38, 5)] = left2[pl.ds(5 * j, 5)]
        f2[j, pl.ds(43, 5)] = right2[pl.ds(5 * j, 5)]

    @pl.loop(0, 16, unroll=16)
    def _(j):
        high, low = halves(f2[j])
        v = dot(y2[...], jnp.concatenate([high, low, high], 0))
        v2[j] = v
        v2[16 + j] = pltpu.roll(v, 64, 1)

    correlate_x(taps, 2, v2, w2, 11, 11)
    v2[pl.ds(0, 11), pl.ds(0, 32)] = correlate_z(w2, 11, z2)
    top = lambda i: v2[i + 1, pl.ds(0, 32)]
    for a in range(-1, 9):
        if a >= 0:
            mid[2 * a + 1] = mid_in[2 * a + 1] + (0.75 * top(a) + 0.125 * (top(a - 1) + top(a + 1)))
        if a < 8:
            mid[2 * a + 2] = mid_in[2 * a + 2] + 0.5 * (top(a) + top(a + 1))
    for a in range(16):
        fine[2 * a] = 0.75 * mid[a + 1] + 0.125 * (mid[a] + mid[a + 2])
        fine[2 * a + 1] = 0.5 * (mid[a + 1] + mid[a + 2])
    copies = []
    for q in range(4):
        rows = pl.ds(8 * q, 8)
        high, low = halves(fine[rows].reshape(256, 128))
        done[rows] = direct[rows] + dot(jnp.concatenate([high, low], 1), up1[...]).reshape(8, 32, 256)
        copies.append(pltpu.make_async_copy(done.at[rows], out.at[rows], sems.at[q]))
        copies[q].start()
    for copy in copies:
        copy.wait()


def section(table, own, left, right, base, at):
    b = left[pl.ds(base, 48)][10 * at:10 * at + 16]
    a = right[pl.ds(base, 48)][10 * at:10 * at + 16]
    high, low = halves(jnp.concatenate([own, b, a], 0))
    return dot(table[...], jnp.concatenate([high, low, high], 0))


def inner_kernel(taps, c, left, right, y0, z0h, z0l, out, v, wh, wl):
    @pl.loop(0, 8, unroll=4)
    def _(q):
        base = pl.multiple_of(40 * q, 8)
        for at in range(4):
            i = 4 * q + at
            v[i] = section(y0, c[i], left, right, base, at)

    @pl.loop(0, 4)
    def _(g):
        for member in range(3):
            rows = pl.ds(pl.multiple_of(32 * member + 8 * g, 8), 8)
            scale = [taps[0, member, k] for k in range(TAPS)]
            for h in range(2):
                lanes = pl.ds(128 * h, 128)
                for base in range(0, 32, 8):
                    sums = [None] * 8
                    for i in range(max(base - RADIUS, 0), min(base + 8 + RADIUS, 32)):
                        value = v[i, rows, lanes]
                        for m in range(8):
                            k = i - base - m + RADIUS
                            if 0 <= k < TAPS:
                                term = scale[k] * value
                                sums[m] = term if sums[m] is None else sums[m] + term
                    for m in range(0, 8, 2):
                        high, low = halves(jnp.concatenate([sums[m], sums[m + 1]], 0))
                        at = (pl.ds(8 * (base + m), 16), pl.ds(256 * member + 128 * h, 128))
                        wh[at] = high
                        wl[at] = low
        cols = pl.ds(pl.multiple_of(8 * g, 8), 8)
        total = dot(wh[...], z0h[...]) + dot(wl[...], z0h[...]) + dot(wh[...], z0l[...])
        out[:, cols] = total.reshape(32, 8, 256)


def finest_part(taps, before, after, left, right, y0, z0h, z0l, inner, out, v, wh, wl):
    for i in range(20):
        own = before[pl.ds(32 * i, 32)] if i < 10 else after[pl.ds(32 * (i - 10), 32)]
        b = left[pl.ds(10 * i, 16)]
        a = right[pl.ds(10 * i, 16)]
        high, low = halves(jnp.concatenate([own, b, a], 0))
        v[i] = dot(y0[...], jnp.concatenate([high, low, high], 0))

    @pl.loop(0, 4)
    def _(g):
        for member in range(3):
            rows = pl.ds(pl.multiple_of(32 * member + 8 * g, 8), 8)
            scale = [taps[0, member, k] for k in range(TAPS)]
            for h in range(2):
                lanes = pl.ds(128 * h, 128)
                sums = [None] * 20
                for r in range(20):
                    value = v[r, rows, lanes]
                    for m in range(10):
                        k = r - m if r < 10 else 20 + r - 10 - m
                        at = m if r < 10 else 10 + m
                        if r < 10 and m > r or r >= 10 and m < r - 10:
                            continue
                        term = scale[k] * value
                        sums[at] = term if sums[at] is None else sums[at] + term
                for m in range(0, 20, 2):
                    high, low = halves(jnp.concatenate([sums[m], sums[m + 1]], 0))
                    at = (pl.ds(pl.multiple_of(160 * g, 32) + 8 * m, 16), pl.ds(256 * member + 128 * h, 128))
                    wh[at] = high
                    wl[at] = low

    total = dot(wh[...], z0h[...]) + dot(wl[...], z0h[...]) + dot(wh[...], z0l[...])
    for g in range(4):
        cols = pl.ds(8 * g, 8)
        piece = total[160 * g:160 * g + 160].reshape(20, 8, 256)
        out[pl.ds(0, 10), cols] = inner[pl.ds(0, 10), cols] + piece[:10]
        out[pl.ds(10, 12), cols] = inner[pl.ds(10, 12), cols]
        out[pl.ds(22, 10), cols] = inner[pl.ds(22, 10), cols] + piece[10:]


def last_kernel(taps, before, after, left, right, y0, z0h, z0l, inner, l2x, left2, right2, y2, z2, up1, mid_in,
                out, v, wh, wl, direct, f2, v2, w2, mid, fine, done, sems):
    finest_part(taps, before, after, left, right, y0, z0h, z0l, inner, direct, v, wh, wl)
    upper_part(taps, l2x, left, right, left2, right2, y2, z2, up1, mid_in, direct, out,
               f2, v2, w2, mid, fine, done, sems)


def call(kernel, outs, scratch=(), scalars=0, count=0, flops=0, moved=0, name=None, sems=0, far=False):
    vmem = pl.BlockSpec(memory_space=pltpu.VMEM)
    smem = pl.BlockSpec(memory_space=pltpu.SMEM)
    hbm = pl.BlockSpec(memory_space=pltpu.HBM)
    shapes = [jax.ShapeDtypeStruct(*o) for o in outs]
    return pl.pallas_call(
        kernel,
        out_shape=shapes,
        in_specs=[smem] * scalars + [vmem] * (count - scalars),
        out_specs=[hbm if far else vmem] * len(shapes),
        scratch_shapes=[pltpu.VMEM(*s) for s in scratch] + [pltpu.SemaphoreType.DMA((sems,))] * (sems > 0),
        compiler_params=pltpu.CompilerParams(vmem_limit_bytes=VMEM_LIMIT),
        cost_estimate=pl.CostEstimate(flops=flops, bytes_accessed=moved, transcendentals=0),
        name=name,
    )


def shift(x, axis, by):
    n = lax.axis_size(axis)
    return lax.ppermute(x, axis, [(i, (i + by) % n) for i in range(n)])


def body(charges, kernel_taps):
    taps = kernel_taps
    l1, l2, s_up, s_down, last, first, o_up, o_down = call(
        restrict_kernel,
        [((18, 24, 128), F32), ((6, 16, 128), F32), ((288, 128), F32), ((288, 128), F32),
         ((320, 256), F32), ((320, 256), F32), ((328, 256), F32), ((328, 256), F32)],
        [((18, 24, 256), F32), ((12, 16, 128), F32)], 0, 1, 10**8, 2 * 10**6, name="restrict",
    )(charges)
    x_left = shift(s_up, "gx", 1)
    x_right = shift(s_down, "gx", -1)
    taps, l1 = lax.optimization_barrier((taps, l1))
    y0, y1, y2, z0h, z0l, z1, z2, up1 = call(
        matrices_kernel,
        [((96, 192), BF), ((96, 144), BF), ((96, 144), BF), ((768, 256), BF), ((768, 256), BF),
         ((768, 256), BF), ((768, 256), BF), ((256, 256), BF)],
        [], 1, 1, 10**8, 4 * 10**6, name="matrices",
    )(taps)
    own_left = shift(o_up, "gy", 1)
    own_right = shift(o_down, "gy", -1)
    x_left, x_right, y0 = lax.optimization_barrier((x_left, x_right, y0))
    c_up, c_down = call(
        face_x_kernel, [((344, 256), F32), ((344, 256), F32)], [], 0, 4, 2 * 10**10, 2 * 10**6, name="face_x",
    )(last, first, x_left, x_right)
    before = shift(c_up, "gx", 1)
    after = shift(c_down, "gx", -1)
    x_left, x_right, c_up = lax.optimization_barrier((x_left, x_right, c_up))
    l1x, g_up, g_down = call(
        gather_fine_kernel, [((38, 24, 128), F32), ((456, 128), F32), ((456, 128), F32)],
        [], 0, 3, 2 * 10**10, 2 * 10**6, name="gather_fine",
    )(l1, x_left, x_right)
    fine_left = shift(g_up, "gy", 1)
    fine_right = shift(g_down, "gy", -1)
    y0, g_up, g_down = lax.optimization_barrier((y0, g_up, g_down))
    inner, = call(
        inner_kernel, [((32, 32, 256), F32)],
        [((32, 96, 256), F32), ((256, 768), BF), ((256, 768), BF)], 1, 7, 2 * 10**9, 6 * 10**6, name="inner",
    )(taps, charges, own_left, own_right, y0, z0h, z0l)
    before, after, inner, fine_left, fine_right = lax.optimization_barrier(
        (before, after, inner, fine_left, fine_right)
    )
    l2x, f_up, f_down, t_up, t_down = call(
        gather_top_kernel,
        [((16, 16, 128), F32), ((296, 256), F32), ((296, 256), F32), ((80, 128), F32), ((80, 128), F32)],
        [], 0, 5, 10**6, 5 * 10**6, name="gather_top",
    )(before, after, l2, x_left, x_right)
    left = shift(f_up, "gy", 1)
    right = shift(f_down, "gy", -1)
    left2 = shift(t_up, "gy", 2)
    right2 = shift(t_down, "gy", -2)
    l1x, f_up, f_down = lax.optimization_barrier((l1x, f_up, f_down))
    mid, = call(
        fine_level_kernel, [((18, 32, 128), F32)],
        [((38, 48, 128), F32), ((38, 96, 128), F32), ((18, 96, 128), F32)],
        1, 6, 4 * 10**8, 4 * 10**6, name="fine_level",
    )(taps, l1x, fine_left, fine_right, y1, z1)
    left, right, mid = lax.optimization_barrier((left, right, mid))
    result, = call(
        last_kernel, [((32, 32, 256), F32)],
        [((20, 96, 256), F32), ((640, 768), BF), ((640, 768), BF), ((32, 32, 256), F32),
         ((16, 48, 128), F32), ((32, 96, 128), F32), ((11, 96, 128), F32), ((18, 32, 128), F32),
         ((32, 32, 128), F32), ((32, 32, 256), F32)],
        1, 16, 2 * 10**9, 6 * 10**6, name="last", sems=4, far=True,
    )(taps, before, after, left, right, y0, z0h, z0l, inner, l2x, left2, right2, y2, z2, up1, mid)
    return result


def solution(mesh):
    return jax.shard_map(
        body,
        mesh=mesh,
        in_specs=(P("gx", "gy", None), P()),
        out_specs=P("gx", "gy", None),
        check_vma=False,
    )
```

```python
import jax
import jax.numpy as jnp
from jax import lax
from jax.experimental import pallas as pl
from jax.experimental.pallas import tpu as pltpu
from jax.sharding import PartitionSpec as P

SPLINE = (0.125, 0.5, 0.75, 0.5, 0.125)
RADIUS = 10
TAPS = 21
BF = jnp.bfloat16
F32 = jnp.float32
VMEM_LIMIT = 48 * 1024 * 1024


def halves(x):
    high = x.astype(BF)
    return high, (x - high.astype(F32)).astype(BF)


def dot(a, b):
    return jnp.dot(a, b, preferred_element_type=F32)


def spline_sum(read, center, low, high):
    total = None
    for k in range(-2, 3):
        if low <= 2 * center + k <= high:
            term = SPLINE[k + 2] * read(2 * center + k)
            total = term if total is None else total + term
    return total


def matrices_kernel(taps, y0, y1, y2, z0h, z0l, z1, z2, up1):
    def iota(shape, dim):
        return lax.broadcasted_iota(jnp.int32, shape, dim)

    def pick(level, member, offsets):
        table = jnp.zeros(offsets.shape, F32)
        for k in range(TAPS):
            table = jnp.where(offsets == k, taps[level, member, k], table)
        return table

    def cycle(level, member, length):
        offsets = (iota((length, length), 0) - iota((length, length), 1) + RADIUS) & (length - 1)
        return pick(level, member, offsets)

    def spread(lanes, width, pieces):
        cols = lanes
        for _ in range(2):
            cols = jnp.where(cols >= width, cols - width, cols)
        place = jnp.full(lanes.shape, -99, jnp.int32)
        for begin, end, position in pieces:
            place = jnp.where((cols >= begin) & (cols < end), cols - begin + position, place)
        return place

    def put(out, rows, table, width):
        high, low = halves(table)
        out[rows] = jnp.where(iota(table.shape, 1) < 2 * width, high.astype(F32), low.astype(F32)).astype(BF)

    def block(out, base, table, count):
        high, low = halves(table)
        zero = jnp.zeros((128, 128), BF)
        if count < 128:
            for at in (base, base + 128):
                out[pl.ds(at + count, 128 - count)] = jnp.zeros((128 - count, 256), BF)
        out[pl.ds(base, count), pl.ds(0, 128)] = high
        out[pl.ds(base, count), pl.ds(128, 128)] = low
        out[pl.ds(base + 128, count), pl.ds(0, 128)] = high
        out[pl.ds(base + 128, count), pl.ds(128, 128)] = zero[:count]

    def product(weights, table):
        high, low = halves(table)
        return dot(weights, high) + dot(weights, low)

    place0 = spread(iota((32, 192), 1), 64, ((0, 32, 0), (32, 42, -10), (48, 58, 32))) - iota((32, 192), 0) + RADIUS
    place1 = spread(iota((32, 144), 1), 48, ((0, 12, -11), (12, 30, -1), (30, 42, 15)))
    place1 = place1 - (iota((32, 144), 0) - 1) + RADIUS
    place2 = spread(iota((32, 144), 1), 48, ((0, 11, -1), (16, 27, -9), (27, 38, 7), (38, 43, -11), (43, 48, 15)))
    place2 = place2 - (iota((32, 144), 0) - 1) + RADIUS
    columns = iota((32, 32), 1) - 1
    lift1 = jnp.where(columns < 17, spline_of(iota((32, 32), 0) - 2 * columns), 0.0).astype(BF)
    lift2 = jnp.where(columns < 10, spline_of(iota((32, 32), 0) - 1 - 2 * columns), 0.0).astype(BF)
    lift2 = dot(lift1, lift2).astype(BF)
    up2 = cyclic_iota((64, 128), 0, 1, 128).astype(BF)
    up1[pl.ds(0, 128)] = cyclic_iota((128, 256), 0, 1, 256).astype(BF)
    up1[pl.ds(128, 128)] = cyclic_iota((128, 256), 0, 1, 256).astype(BF)
    for member in range(3):
        rows = pl.ds(32 * member, 32)
        put(y0, rows, pick(0, member, place0), 64)
        put(y1, rows, product(lift1, pick(1, member, place1)), 48)
        put(y2, rows, product(lift2, pick(2, member, place2)), 48)
        high, low = halves(cycle(0, member, 256))
        z0h[pl.ds(256 * member, 256)] = high
        z0l[pl.ds(256 * member, 256)] = low
        block(z1, 256 * member, cycle(1, member, 128), 128)
        high, low = halves(cycle(2, member, 64))
        block(z2, 256 * member, dot(high, up2) + dot(low, up2), 64)


def spline_iota(shape, offset, coarse_dim, fine_dim, keep=None):
    fine = lax.broadcasted_iota(jnp.int32, shape, fine_dim)
    coarse = lax.broadcasted_iota(jnp.int32, shape, coarse_dim)
    delta = fine - 2 * coarse + offset
    if keep is not None:
        delta = jnp.where(coarse < keep, delta, 99)
    return spline_of(delta)


def spline_of(delta):
    far = jnp.abs(delta)
    return jnp.where(far == 0, 0.75, jnp.where(far == 1, 0.5, jnp.where(far == 2, 0.125, 0.0)))


def cyclic_iota(shape, coarse_dim, fine_dim, fine_len):
    fine = lax.broadcasted_iota(jnp.int32, shape, fine_dim)
    coarse = lax.broadcasted_iota(jnp.int32, shape, coarse_dim)
    return spline_of(((fine - 2 * coarse + 2) & (fine_len - 1)) - 2)


def restrict_kernel(charges, l1, l2, up1, down1, last, first, face_up, face_down, s1, s2, c, sems):
    copies = []
    for q in range(4):
        rows = pl.ds(8 * q, 8)
        copies.append(pltpu.make_async_copy(charges.at[rows], c.at[rows], sems.at[q]))
        copies[q].start()
    ry = spline_iota((24, 32), 2, 0, 1, 18).astype(BF)
    for i in range(-1, 17):
        if i in (-1, 3, 7, 11):
            copies[(i + 1) // 4].wait()
        high, low = halves(spline_sum(lambda r: c[r], i, 0, 31))
        s1[i + 1] = dot(ry, high) + dot(ry, low)
    for i in range(32):
        face_up[pl.ds(10 * i, 10)] = c[i, 22:32]
        face_down[pl.ds(10 * i, 10)] = c[i, 0:10]
    face_up[pl.ds(320, 8)] = jnp.zeros((8, 256), F32)
    face_down[pl.ds(320, 8)] = jnp.zeros((8, 256), F32)
    for r in range(10):
        last[pl.ds(32 * r, 32)] = c[22 + r]
        first[pl.ds(32 * r, 32)] = c[r]
    rz = cyclic_iota((256, 128), 1, 0, 256).astype(BF)
    high, low = halves(s1[...].reshape(18 * 24, 256))
    l1[...] = (dot(high, rz) + dot(low, rz)).reshape(18, 24, 128)
    ry2 = spline_iota((16, 24), 1, 0, 1, 11).astype(BF)
    for i in range(-1, 10):
        high, low = halves(spline_sum(lambda r: l1[r + 1], i, -1, 16))
        s2[i + 1] = dot(ry2, high) + dot(ry2, low)
    s2[11] = jnp.zeros((16, 128), F32)
    near = s2[pl.ds(0, 6)].reshape(96, 128)
    far = s2[pl.ds(6, 6)].reshape(96, 128)
    lanes = lax.broadcasted_iota(jnp.int32, (128, 128), 1)
    both = spline_of(((lax.broadcasted_iota(jnp.int32, (128, 128), 0) - 2 * (lanes & 63) + 2) & 127) - 2)
    total = jnp.zeros((96, 128), F32)
    for part, upper in ((near, False), (far, True)):
        weights = jnp.where((lanes >= 64) == upper, both, 0.0).astype(BF)
        high, low = halves(part)
        total = total + dot(high, weights) + dot(low, weights)
    total = total.reshape(6, 16, 128)
    l2[...] = total
    up1[pl.ds(64, 8)] = jnp.zeros((8, 128), F32)
    down1[pl.ds(64, 8)] = jnp.zeros((8, 128), F32)
    for j in range(6):
        up1[pl.ds(11 * j, 11)] = total[j, :11]
        down1[pl.ds(11 * j, 11)] = total[j, :11]
    for r in range(12):
        up1[pl.ds(72 + 18 * r, 18)] = l1[6 + r, :18]
        down1[pl.ds(72 + 18 * r, 18)] = l1[r, :18]


def paired(base, count, j):
    return (pl.ds(base + count * (j // 2), count), pl.ds(128 * (j % 2), 128))


def face_x_kernel(last, first, left, right, up, down):
    up[pl.ds(0, 320)] = last[...]
    down[pl.ds(0, 320)] = first[...]
    lower = lax.broadcasted_iota(jnp.int32, (11, 128), 1) < 64
    for p in range(3):
        even = 2 * p
        odd = min(even + 1, 4)
        a = left[pl.ds(11 * even, 11)]
        b = left[pl.ds(11 * odd, 11)]
        up[paired(320, 11, p)] = jnp.where(lower, pltpu.roll(a, 64, 1), b)
        a = right[pl.ds(11 * even, 11)]
        b = right[pl.ds(11 * odd, 11)]
        down[paired(320, 11, p)] = jnp.where(lower, a, pltpu.roll(b, 64, 1))


def gather_fine_kernel(l1, left, right, l1x, up, down):
    for i in range(38):
        if i < 12:
            l1x[i, :18] = left[pl.ds(72 + 18 * i, 18)]
            l1x[i, pl.ds(18, 6)] = jnp.zeros((6, 128), F32)
        elif i >= 26:
            l1x[i, :18] = right[pl.ds(72 + 18 * (i - 26), 18)]
            l1x[i, pl.ds(18, 6)] = jnp.zeros((6, 128), F32)
        if 10 <= i < 12 or 26 <= i < 28:
            l1x[i] = l1x[i] + l1[i - 10]
        elif 12 <= i < 26:
            l1x[i] = l1[i - 10]
    for i in range(38):
        up[pl.ds(12 * i, 12)] = l1x[i, 6:18]
        down[pl.ds(12 * i, 12)] = l1x[i, 0:12]


def gather_top_kernel(before, after, l2, left, right, l2x, up, down, up2, down2):
    for i in range(20):
        row = before[pl.ds(32 * i, 32)] if i < 10 else after[pl.ds(32 * (i - 10), 32)]
        up[pl.ds(10 * i, 10)] = row[22:32]
        down[pl.ds(10 * i, 10)] = row[0:10]
    up[pl.ds(200, 8)] = jnp.zeros((8, 256), F32)
    down[pl.ds(200, 8)] = jnp.zeros((8, 256), F32)
    lanes = lax.broadcasted_iota(jnp.int32, (11, 128), 1)
    lower = lanes < 64
    rolled = lambda x: pltpu.roll(x, 64, 1)
    for j in range(16):
        low = []
        high = []
        if j < 5:
            slab = before[paired(320, 11, j // 2)]
            low.append(slab if j % 2 == 0 else rolled(slab))
        if 2 <= j < 8:
            low.append(left[pl.ds(11 * (j - 2), 11)])
        if 8 <= j < 13:
            low.append(rolled(left[pl.ds(11 * (j - 8), 11)]))
        if j >= 10:
            low.append(l2[j - 10, :11])
        if j < 5:
            high.append(l2[j, :11])
        if 2 <= j < 8:
            high.append(rolled(right[pl.ds(11 * (j - 2), 11)]))
        if 8 <= j < 13:
            high.append(right[pl.ds(11 * (j - 8), 11)])
        if 10 <= j < 15:
            slab = after[paired(320, 11, (j - 10) // 2)]
            high.append(rolled(slab) if j % 2 == 0 else slab)
        row = jnp.where(lower, sum(low, jnp.zeros((11, 128), F32)), sum(high, jnp.zeros((11, 128), F32)))
        l2x[j, :11] = row
        l2x[j, pl.ds(11, 5)] = jnp.zeros((5, 128), F32)
        up[paired(208, 11, j)] = row
        down[paired(208, 11, j)] = row
        up2[pl.ds(5 * j, 5)] = row[6:11]
        down2[pl.ds(5 * j, 5)] = row[0:5]


def correlate_x(taps, level, v, w, count, many):
    @pl.loop(0, 12)
    def _(g):
        member = g // 4
        rows = pl.ds(pl.multiple_of(8 * g, 8), 8)
        scale = [taps[level, member, k] for k in range(TAPS)]
        for base in range(0, count, many):
            sums = [None] * many
            for i in range(base, base + many + TAPS - 1):
                value = v[i, rows]
                for m in range(many):
                    k = i - base - m
                    if 0 <= k < TAPS:
                        term = scale[k] * value
                        sums[m] = term if sums[m] is None else sums[m] + term
            for m in range(many):
                w[base + m, rows] = sums[m]


def correlate_z(w, count, table):
    total = jnp.zeros((count * 32, 256), F32)
    for member in range(3):
        high, low = halves(w[:, pl.ds(32 * member, 32)].reshape(count * 32, 128))
        total = total + dot(jnp.concatenate([high, low], 1), table[pl.ds(256 * member, 256)])
    return (total[:, :128] + total[:, 128:]).reshape(count, 32, 128)


def fine_level_kernel(taps, l1x, left, right, y1, z1, mid, f1, v1, w1):
    for i in range(38):
        f1[i, pl.ds(0, 12)] = left[pl.ds(12 * i, 12)]
        f1[i, pl.ds(12, 18)] = l1x[i, :18]
        f1[i, pl.ds(30, 12)] = right[pl.ds(12 * i, 12)]
        f1[i, pl.ds(42, 6)] = jnp.zeros((6, 128), F32)

    @pl.loop(0, 38, unroll=19)
    def _(i):
        high, low = halves(f1[i])
        v1[i] = dot(y1[...], jnp.concatenate([high, low, high], 0))

    correlate_x(taps, 1, v1, w1, 18, 9)
    mid[...] = correlate_z(w1, 18, z1)


def upper_kernel(taps, l2x, left, right, left2, right2, y2, z2, up1, mid_in, direct, out,
                 f2, v2, w2, mid, fine, done, sems):
    for j in range(16):
        f2[j, pl.ds(0, 16)] = l2x[j]
        f2[j, pl.ds(16, 11)] = left[paired(208, 11, j)]
        f2[j, pl.ds(27, 11)] = right[paired(208, 11, j)]
        f2[j, pl.ds(38, 5)] = left2[pl.ds(5 * j, 5)]
        f2[j, pl.ds(43, 5)] = right2[pl.ds(5 * j, 5)]

    @pl.loop(0, 16, unroll=16)
    def _(j):
        high, low = halves(f2[j])
        v = dot(y2[...], jnp.concatenate([high, low, high], 0))
        v2[j] = v
        v2[16 + j] = pltpu.roll(v, 64, 1)

    correlate_x(taps, 2, v2, w2, 11, 11)
    v2[pl.ds(0, 11), pl.ds(0, 32)] = correlate_z(w2, 11, z2)
    top = lambda i: v2[i + 1, pl.ds(0, 32)]
    for a in range(-1, 9):
        if a >= 0:
            mid[2 * a + 1] = mid_in[2 * a + 1] + (0.75 * top(a) + 0.125 * (top(a - 1) + top(a + 1)))
        if a < 8:
            mid[2 * a + 2] = mid_in[2 * a + 2] + 0.5 * (top(a) + top(a + 1))
    for a in range(16):
        fine[2 * a] = 0.75 * mid[a + 1] + 0.125 * (mid[a] + mid[a + 2])
        fine[2 * a + 1] = 0.5 * (mid[a + 1] + mid[a + 2])
    copies = []
    for q in range(4):
        rows = pl.ds(8 * q, 8)
        high, low = halves(fine[rows].reshape(256, 128))
        done[rows] = direct[rows] + dot(jnp.concatenate([high, low], 1), up1[...]).reshape(8, 32, 256)
        copies.append(pltpu.make_async_copy(done.at[rows], out.at[rows], sems.at[q]))
        copies[q].start()
    for copy in copies:
        copy.wait()


def section(table, own, left, right, base, at):
    b = left[pl.ds(base, 48)][10 * at:10 * at + 16]
    a = right[pl.ds(base, 48)][10 * at:10 * at + 16]
    high, low = halves(jnp.concatenate([own, b, a], 0))
    return dot(table[...], jnp.concatenate([high, low, high], 0))


def inner_kernel(taps, c, left, right, y0, z0h, z0l, out, v, wh, wl):
    @pl.loop(0, 8, unroll=4)
    def _(q):
        base = pl.multiple_of(40 * q, 8)
        for at in range(4):
            i = 4 * q + at
            v[i] = section(y0, c[i], left, right, base, at)

    @pl.loop(0, 4)
    def _(g):
        for member in range(3):
            rows = pl.ds(pl.multiple_of(32 * member + 8 * g, 8), 8)
            scale = [taps[0, member, k] for k in range(TAPS)]
            for h in range(2):
                lanes = pl.ds(128 * h, 128)
                for base in range(0, 32, 8):
                    sums = [None] * 8
                    for i in range(max(base - RADIUS, 0), min(base + 8 + RADIUS, 32)):
                        value = v[i, rows, lanes]
                        for m in range(8):
                            k = i - base - m + RADIUS
                            if 0 <= k < TAPS:
                                term = scale[k] * value
                                sums[m] = term if sums[m] is None else sums[m] + term
                    for m in range(0, 8, 2):
                        high, low = halves(jnp.concatenate([sums[m], sums[m + 1]], 0))
                        at = (pl.ds(8 * (base + m), 16), pl.ds(256 * member + 128 * h, 128))
                        wh[at] = high
                        wl[at] = low
        cols = pl.ds(pl.multiple_of(8 * g, 8), 8)
        total = dot(wh[...], z0h[...]) + dot(wl[...], z0h[...]) + dot(wh[...], z0l[...])
        out[:, cols] = total.reshape(32, 8, 256)


def finest_kernel(taps, before, after, left, right, y0, z0h, z0l, inner, out, v, wh, wl):
    for i in range(20):
        own = before[pl.ds(32 * i, 32)] if i < 10 else after[pl.ds(32 * (i - 10), 32)]
        b = left[pl.ds(10 * i, 16)]
        a = right[pl.ds(10 * i, 16)]
        high, low = halves(jnp.concatenate([own, b, a], 0))
        v[i] = dot(y0[...], jnp.concatenate([high, low, high], 0))

    @pl.loop(0, 4)
    def _(g):
        for member in range(3):
            rows = pl.ds(pl.multiple_of(32 * member + 8 * g, 8), 8)
            scale = [taps[0, member, k] for k in range(TAPS)]
            for h in range(2):
                lanes = pl.ds(128 * h, 128)
                sums = [None] * 20
                for r in range(20):
                    value = v[r, rows, lanes]
                    for m in range(10):
                        k = r - m if r < 10 else 20 + r - 10 - m
                        at = m if r < 10 else 10 + m
                        if r < 10 and m > r or r >= 10 and m < r - 10:
                            continue
                        term = scale[k] * value
                        sums[at] = term if sums[at] is None else sums[at] + term
                for m in range(0, 20, 2):
                    high, low = halves(jnp.concatenate([sums[m], sums[m + 1]], 0))
                    at = (pl.ds(pl.multiple_of(160 * g, 32) + 8 * m, 16), pl.ds(256 * member + 128 * h, 128))
                    wh[at] = high
                    wl[at] = low

    total = dot(wh[...], z0h[...]) + dot(wl[...], z0h[...]) + dot(wh[...], z0l[...])
    for g in range(4):
        cols = pl.ds(8 * g, 8)
        piece = total[160 * g:160 * g + 160].reshape(20, 8, 256)
        out[pl.ds(0, 10), cols] = inner[pl.ds(0, 10), cols] + piece[:10]
        out[pl.ds(10, 12), cols] = inner[pl.ds(10, 12), cols]
        out[pl.ds(22, 10), cols] = inner[pl.ds(22, 10), cols] + piece[10:]


def call(kernel, outs, scratch=(), scalars=0, count=0, flops=0, moved=0, name=None, sems=0, far=False, near=True, limit=VMEM_LIMIT):
    vmem = pl.BlockSpec(memory_space=pltpu.VMEM)
    smem = pl.BlockSpec(memory_space=pltpu.SMEM)
    hbm = pl.BlockSpec(memory_space=pltpu.HBM)
    shapes = [jax.ShapeDtypeStruct(*o) for o in outs]
    return pl.pallas_call(
        kernel,
        out_shape=shapes,
        in_specs=[smem] * scalars + [vmem if near else hbm] * (count - scalars),
        out_specs=[hbm if far else vmem] * len(shapes),
        scratch_shapes=[pltpu.VMEM(*s) for s in scratch] + [pltpu.SemaphoreType.DMA((sems,))] * (sems > 0),
        compiler_params=pltpu.CompilerParams(vmem_limit_bytes=limit),
        cost_estimate=pl.CostEstimate(flops=flops, bytes_accessed=moved, transcendentals=0),
        name=name,
    )


def shift(x, axis, by):
    n = lax.axis_size(axis)
    return lax.ppermute(x, axis, [(i, (i + by) % n) for i in range(n)])


def body(charges, kernel_taps):
    taps = kernel_taps
    l1, l2, s_up, s_down, last, first, o_up, o_down = call(
        restrict_kernel,
        [((18, 24, 128), F32), ((6, 16, 128), F32), ((288, 128), F32), ((288, 128), F32),
         ((320, 256), F32), ((320, 256), F32), ((328, 256), F32), ((328, 256), F32)],
        [((18, 24, 256), F32), ((12, 16, 128), F32), ((32, 32, 256), F32)],
        0, 1, 10**8, 2 * 10**6, name="restrict", sems=4, near=False, limit=60 * 1024 * 1024,
    )(charges)
    x_left = shift(s_up, "gx", 1)
    x_right = shift(s_down, "gx", -1)
    taps, l1 = lax.optimization_barrier((taps, l1))
    y0, y1, y2, z0h, z0l, z1, z2, up1 = call(
        matrices_kernel,
        [((96, 192), BF), ((96, 144), BF), ((96, 144), BF), ((768, 256), BF), ((768, 256), BF),
         ((768, 256), BF), ((768, 256), BF), ((256, 256), BF)],
        [], 1, 1, 10**8, 4 * 10**6, name="matrices",
    )(taps)
    own_left = shift(o_up, "gy", 1)
    own_right = shift(o_down, "gy", -1)
    x_left, x_right, y0 = lax.optimization_barrier((x_left, x_right, y0))
    c_up, c_down = call(
        face_x_kernel, [((344, 256), F32), ((344, 256), F32)], [], 0, 4, 2 * 10**10, 2 * 10**6, name="face_x",
    )(last, first, x_left, x_right)
    before = shift(c_up, "gx", 1)
    after = shift(c_down, "gx", -1)
    x_left, x_right, c_up = lax.optimization_barrier((x_left, x_right, c_up))
    l1x, g_up, g_down = call(
        gather_fine_kernel, [((38, 24, 128), F32), ((456, 128), F32), ((456, 128), F32)],
        [], 0, 3, 2 * 10**10, 2 * 10**6, name="gather_fine",
    )(l1, x_left, x_right)
    fine_left = shift(g_up, "gy", 1)
    fine_right = shift(g_down, "gy", -1)
    y0, g_up, g_down = lax.optimization_barrier((y0, g_up, g_down))
    inner, = call(
        inner_kernel, [((32, 32, 256), F32)],
        [((32, 96, 256), F32), ((256, 768), BF), ((256, 768), BF)], 1, 7, 2 * 10**9, 6 * 10**6, name="inner",
    )(taps, charges, own_left, own_right, y0, z0h, z0l)
    before, after, inner, fine_left, fine_right = lax.optimization_barrier(
        (before, after, inner, fine_left, fine_right)
    )
    l2x, f_up, f_down, t_up, t_down = call(
        gather_top_kernel,
        [((16, 16, 128), F32), ((296, 256), F32), ((296, 256), F32), ((80, 128), F32), ((80, 128), F32)],
        [], 0, 5, 10**6, 5 * 10**6, name="gather_top",
    )(before, after, l2, x_left, x_right)
    left = shift(f_up, "gy", 1)
    right = shift(f_down, "gy", -1)
    left2 = shift(t_up, "gy", 2)
    right2 = shift(t_down, "gy", -2)
    l1x, f_up, f_down = lax.optimization_barrier((l1x, f_up, f_down))
    mid, = call(
        fine_level_kernel, [((18, 32, 128), F32)],
        [((38, 48, 128), F32), ((38, 96, 128), F32), ((18, 96, 128), F32)],
        1, 6, 4 * 10**8, 4 * 10**6, name="fine_level",
    )(taps, l1x, fine_left, fine_right, y1, z1)
    left, right, mid = lax.optimization_barrier((left, right, mid))
    direct, = call(
        finest_kernel, [((32, 32, 256), F32)],
        [((20, 96, 256), F32), ((640, 768), BF), ((640, 768), BF)],
        1, 9, 2 * 10**9, 6 * 10**6, name="finest",
    )(taps, before, after, left, right, y0, z0h, z0l, inner)
    result, = call(
        upper_kernel, [((32, 32, 256), F32)],
        [((16, 48, 128), F32), ((32, 96, 128), F32), ((11, 96, 128), F32), ((18, 32, 128), F32),
         ((32, 32, 128), F32), ((32, 32, 256), F32)],
        1, 11, 4 * 10**8, 4 * 10**6, name="upper", sems=4, far=True,
    )(taps, l2x, left, right, left2, right2, y2, z2, up1, mid, direct)
    return result


def solution(mesh):
    return jax.shard_map(
        body,
        mesh=mesh,
        in_specs=(P("gx", "gy", None), P()),
        out_specs=P("gx", "gy", None),
        check_vma=False,
    )
```

```python
import jax
import jax.numpy as jnp
from jax import lax
from jax.experimental import pallas as pl
from jax.experimental.pallas import tpu as pltpu
from jax.sharding import PartitionSpec as P

SPLINE = (0.125, 0.5, 0.75, 0.5, 0.125)
RADIUS = 10
TAPS = 21
BF = jnp.bfloat16
F32 = jnp.float32
VMEM_LIMIT = 48 * 1024 * 1024


def halves(x):
    high = x.astype(BF)
    return high, (x - high.astype(F32)).astype(BF)


def dot(a, b):
    return jnp.dot(a, b, preferred_element_type=F32)


def spline_sum(read, center, low, high):
    total = None
    for k in range(-2, 3):
        if low <= 2 * center + k <= high:
            term = SPLINE[k + 2] * read(2 * center + k)
            total = term if total is None else total + term
    return total


def matrices_kernel(taps, y0, y1, y2, z0h, z0l, z1, z2, up1):
    def iota(shape, dim):
        return lax.broadcasted_iota(jnp.int32, shape, dim)

    def pick(level, member, offsets):
        table = jnp.zeros(offsets.shape, F32)
        for k in range(TAPS):
            table = jnp.where(offsets == k, taps[level, member, k], table)
        return table

    def cycle(level, member, length):
        offsets = (iota((length, length), 0) - iota((length, length), 1) + RADIUS) & (length - 1)
        return pick(level, member, offsets)

    def spread(lanes, width, pieces):
        cols = lanes
        for _ in range(2):
            cols = jnp.where(cols >= width, cols - width, cols)
        place = jnp.full(lanes.shape, -99, jnp.int32)
        for begin, end, position in pieces:
            place = jnp.where((cols >= begin) & (cols < end), cols - begin + position, place)
        return place

    def put(out, rows, table, width):
        high, low = halves(table)
        out[rows] = jnp.where(iota(table.shape, 1) < 2 * width, high.astype(F32), low.astype(F32)).astype(BF)

    def block(out, base, table, count):
        high, low = halves(table)
        zero = jnp.zeros((128, 128), BF)
        if count < 128:
            for at in (base, base + 128):
                out[pl.ds(at + count, 128 - count)] = jnp.zeros((128 - count, 256), BF)
        out[pl.ds(base, count), pl.ds(0, 128)] = high
        out[pl.ds(base, count), pl.ds(128, 128)] = low
        out[pl.ds(base + 128, count), pl.ds(0, 128)] = high
        out[pl.ds(base + 128, count), pl.ds(128, 128)] = zero[:count]

    def product(weights, table):
        high, low = halves(table)
        return dot(weights, high) + dot(weights, low)

    place0 = spread(iota((32, 192), 1), 64, ((0, 32, 0), (32, 42, -10), (48, 58, 32))) - iota((32, 192), 0) + RADIUS
    place1 = spread(iota((32, 144), 1), 48, ((0, 12, -11), (12, 30, -1), (30, 42, 15)))
    place1 = place1 - (iota((32, 144), 0) - 1) + RADIUS
    place2 = spread(iota((32, 144), 1), 48, ((0, 11, -1), (16, 27, -9), (27, 38, 7), (38, 43, -11), (43, 48, 15)))
    place2 = place2 - (iota((32, 144), 0) - 1) + RADIUS
    columns = iota((32, 32), 1) - 1
    lift1 = jnp.where(columns < 17, spline_of(iota((32, 32), 0) - 2 * columns), 0.0).astype(BF)
    lift2 = jnp.where(columns < 10, spline_of(iota((32, 32), 0) - 1 - 2 * columns), 0.0).astype(BF)
    lift2 = dot(lift1, lift2).astype(BF)
    up2 = cyclic_iota((64, 128), 0, 1, 128).astype(BF)
    up1[pl.ds(0, 128)] = cyclic_iota((128, 256), 0, 1, 256).astype(BF)
    up1[pl.ds(128, 128)] = cyclic_iota((128, 256), 0, 1, 256).astype(BF)
    for member in range(3):
        rows = pl.ds(32 * member, 32)
        put(y0, rows, pick(0, member, place0), 64)
        put(y1, rows, product(lift1, pick(1, member, place1)), 48)
        put(y2, rows, product(lift2, pick(2, member, place2)), 48)
        high, low = halves(cycle(0, member, 256))
        z0h[pl.ds(256 * member, 256)] = high
        z0l[pl.ds(256 * member, 256)] = low
        block(z1, 256 * member, cycle(1, member, 128), 128)
        high, low = halves(cycle(2, member, 64))
        block(z2, 256 * member, dot(high, up2) + dot(low, up2), 64)


def spline_iota(shape, offset, coarse_dim, fine_dim, keep=None):
    fine = lax.broadcasted_iota(jnp.int32, shape, fine_dim)
    coarse = lax.broadcasted_iota(jnp.int32, shape, coarse_dim)
    delta = fine - 2 * coarse + offset
    if keep is not None:
        delta = jnp.where(coarse < keep, delta, 99)
    return spline_of(delta)


def spline_of(delta):
    far = jnp.abs(delta)
    return jnp.where(far == 0, 0.75, jnp.where(far == 1, 0.5, jnp.where(far == 2, 0.125, 0.0)))


def cyclic_iota(shape, coarse_dim, fine_dim, fine_len):
    fine = lax.broadcasted_iota(jnp.int32, shape, fine_dim)
    coarse = lax.broadcasted_iota(jnp.int32, shape, coarse_dim)
    return spline_of(((fine - 2 * coarse + 2) & (fine_len - 1)) - 2)


def restrict_kernel(c, l1, l2, up1, down1, last, first, face_up, face_down, s1, s2):
    ry = spline_iota((24, 32), 2, 0, 1, 18).astype(BF)
    for i in range(-1, 17):
        high, low = halves(spline_sum(lambda r: c[r], i, 0, 31))
        s1[i + 1] = dot(ry, high) + dot(ry, low)
    for i in range(32):
        face_up[pl.ds(10 * i, 10)] = c[i, 22:32]
        face_down[pl.ds(10 * i, 10)] = c[i, 0:10]
    face_up[pl.ds(320, 8)] = jnp.zeros((8, 256), F32)
    face_down[pl.ds(320, 8)] = jnp.zeros((8, 256), F32)
    for r in range(10):
        last[pl.ds(32 * r, 32)] = c[22 + r]
        first[pl.ds(32 * r, 32)] = c[r]
    rz = cyclic_iota((256, 128), 1, 0, 256).astype(BF)
    high, low = halves(s1[...].reshape(18 * 24, 256))
    l1[...] = (dot(high, rz) + dot(low, rz)).reshape(18, 24, 128)
    ry2 = spline_iota((16, 24), 1, 0, 1, 11).astype(BF)
    for i in range(-1, 10):
        high, low = halves(spline_sum(lambda r: l1[r + 1], i, -1, 16))
        s2[i + 1] = dot(ry2, high) + dot(ry2, low)
    s2[11] = jnp.zeros((16, 128), F32)
    near = s2[pl.ds(0, 6)].reshape(96, 128)
    far = s2[pl.ds(6, 6)].reshape(96, 128)
    lanes = lax.broadcasted_iota(jnp.int32, (128, 128), 1)
    both = spline_of(((lax.broadcasted_iota(jnp.int32, (128, 128), 0) - 2 * (lanes & 63) + 2) & 127) - 2)
    total = jnp.zeros((96, 128), F32)
    for part, upper in ((near, False), (far, True)):
        weights = jnp.where((lanes >= 64) == upper, both, 0.0).astype(BF)
        high, low = halves(part)
        total = total + dot(high, weights) + dot(low, weights)
    total = total.reshape(6, 16, 128)
    l2[...] = total
    up1[pl.ds(64, 8)] = jnp.zeros((8, 128), F32)
    down1[pl.ds(64, 8)] = jnp.zeros((8, 128), F32)
    for j in range(6):
        up1[pl.ds(11 * j, 11)] = total[j, :11]
        down1[pl.ds(11 * j, 11)] = total[j, :11]
    for r in range(12):
        up1[pl.ds(72 + 18 * r, 18)] = l1[6 + r, :18]
        down1[pl.ds(72 + 18 * r, 18)] = l1[r, :18]


def paired(base, count, j):
    return (pl.ds(base + count * (j // 2), count), pl.ds(128 * (j % 2), 128))


def face_x_kernel(last, first, left, right, up, down):
    up[pl.ds(0, 320)] = last[...]
    down[pl.ds(0, 320)] = first[...]
    lower = lax.broadcasted_iota(jnp.int32, (11, 128), 1) < 64
    for p in range(3):
        even = 2 * p
        odd = min(even + 1, 4)
        a = left[pl.ds(11 * even, 11)]
        b = left[pl.ds(11 * odd, 11)]
        up[paired(320, 11, p)] = jnp.where(lower, pltpu.roll(a, 64, 1), b)
        a = right[pl.ds(11 * even, 11)]
        b = right[pl.ds(11 * odd, 11)]
        down[paired(320, 11, p)] = jnp.where(lower, a, pltpu.roll(b, 64, 1))


def gather_fine_kernel(l1, left, right, l1x, up, down):
    for i in range(38):
        if i < 12:
            l1x[i, :18] = left[pl.ds(72 + 18 * i, 18)]
            l1x[i, pl.ds(18, 6)] = jnp.zeros((6, 128), F32)
        elif i >= 26:
            l1x[i, :18] = right[pl.ds(72 + 18 * (i - 26), 18)]
            l1x[i, pl.ds(18, 6)] = jnp.zeros((6, 128), F32)
        if 10 <= i < 12 or 26 <= i < 28:
            l1x[i] = l1x[i] + l1[i - 10]
        elif 12 <= i < 26:
            l1x[i] = l1[i - 10]
    for i in range(38):
        up[pl.ds(12 * i, 12)] = l1x[i, 6:18]
        down[pl.ds(12 * i, 12)] = l1x[i, 0:12]


def gather_top_kernel(before, after, l2, left, right, l2x, up, down, up2, down2):
    for i in range(20):
        row = before[pl.ds(32 * i, 32)] if i < 10 else after[pl.ds(32 * (i - 10), 32)]
        up[pl.ds(10 * i, 10)] = row[22:32]
        down[pl.ds(10 * i, 10)] = row[0:10]
    up[pl.ds(200, 8)] = jnp.zeros((8, 256), F32)
    down[pl.ds(200, 8)] = jnp.zeros((8, 256), F32)
    lanes = lax.broadcasted_iota(jnp.int32, (11, 128), 1)
    lower = lanes < 64
    rolled = lambda x: pltpu.roll(x, 64, 1)
    for j in range(16):
        low = []
        high = []
        if j < 5:
            slab = before[paired(320, 11, j // 2)]
            low.append(slab if j % 2 == 0 else rolled(slab))
        if 2 <= j < 8:
            low.append(left[pl.ds(11 * (j - 2), 11)])
        if 8 <= j < 13:
            low.append(rolled(left[pl.ds(11 * (j - 8), 11)]))
        if j >= 10:
            low.append(l2[j - 10, :11])
        if j < 5:
            high.append(l2[j, :11])
        if 2 <= j < 8:
            high.append(rolled(right[pl.ds(11 * (j - 2), 11)]))
        if 8 <= j < 13:
            high.append(right[pl.ds(11 * (j - 8), 11)])
        if 10 <= j < 15:
            slab = after[paired(320, 11, (j - 10) // 2)]
            high.append(rolled(slab) if j % 2 == 0 else slab)
        row = jnp.where(lower, sum(low, jnp.zeros((11, 128), F32)), sum(high, jnp.zeros((11, 128), F32)))
        l2x[j, :11] = row
        l2x[j, pl.ds(11, 5)] = jnp.zeros((5, 128), F32)
        up[paired(208, 11, j)] = row
        down[paired(208, 11, j)] = row
        up2[pl.ds(5 * j, 5)] = row[6:11]
        down2[pl.ds(5 * j, 5)] = row[0:5]


def correlate_x(taps, level, v, w, count, many):
    @pl.loop(0, 12, unroll=4)
    def _(g):
        member = g // 4
        rows = pl.ds(pl.multiple_of(8 * g, 8), 8)
        scale = [taps[level, member, k] for k in range(TAPS)]
        for base in range(0, count, many):
            sums = [None] * many
            for i in range(base, base + many + TAPS - 1):
                value = v[i, rows]
                for m in range(many):
                    k = i - base - m
                    if 0 <= k < TAPS:
                        term = scale[k] * value
                        sums[m] = term if sums[m] is None else sums[m] + term
            for m in range(many):
                w[base + m, rows] = sums[m]


def correlate_z(w, count, table):
    total = jnp.zeros((count * 32, 256), F32)
    for member in range(3):
        high, low = halves(w[:, pl.ds(32 * member, 32)].reshape(count * 32, 128))
        total = total + dot(jnp.concatenate([high, low], 1), table[pl.ds(256 * member, 256)])
    return (total[:, :128] + total[:, 128:]).reshape(count, 32, 128)


def fine_level_kernel(taps, l1x, left, right, y1, z1, mid, f1, v1, w1):
    for i in range(38):
        f1[i, pl.ds(0, 12)] = left[pl.ds(12 * i, 12)]
        f1[i, pl.ds(12, 18)] = l1x[i, :18]
        f1[i, pl.ds(30, 12)] = right[pl.ds(12 * i, 12)]
        f1[i, pl.ds(42, 6)] = jnp.zeros((6, 128), F32)

    @pl.loop(0, 38, unroll=19)
    def _(i):
        high, low = halves(f1[i])
        v1[i] = dot(y1[...], jnp.concatenate([high, low, high], 0))

    correlate_x(taps, 1, v1, w1, 18, 9)
    mid[...] = correlate_z(w1, 18, z1)


def upper_kernel(taps, l2x, left, right, left2, right2, y2, z2, up1, mid_in, direct, out,
                 f2, v2, w2, mid, fine, done, sems):
    for j in range(16):
        f2[j, pl.ds(0, 16)] = l2x[j]
        f2[j, pl.ds(16, 11)] = left[paired(208, 11, j)]
        f2[j, pl.ds(27, 11)] = right[paired(208, 11, j)]
        f2[j, pl.ds(38, 5)] = left2[pl.ds(5 * j, 5)]
        f2[j, pl.ds(43, 5)] = right2[pl.ds(5 * j, 5)]

    @pl.loop(0, 16, unroll=16)
    def _(j):
        high, low = halves(f2[j])
        v = dot(y2[...], jnp.concatenate([high, low, high], 0))
        v2[j] = v
        v2[16 + j] = pltpu.roll(v, 64, 1)

    correlate_x(taps, 2, v2, w2, 11, 11)
    v2[pl.ds(0, 11), pl.ds(0, 32)] = correlate_z(w2, 11, z2)
    top = lambda i: v2[i + 1, pl.ds(0, 32)]
    for a in range(-1, 9):
        if a >= 0:
            mid[2 * a + 1] = mid_in[2 * a + 1] + (0.75 * top(a) + 0.125 * (top(a - 1) + top(a + 1)))
        if a < 8:
            mid[2 * a + 2] = mid_in[2 * a + 2] + 0.5 * (top(a) + top(a + 1))
    for a in range(16):
        fine[2 * a] = 0.75 * mid[a + 1] + 0.125 * (mid[a] + mid[a + 2])
        fine[2 * a + 1] = 0.5 * (mid[a + 1] + mid[a + 2])
    copies = []
    for q in range(4):
        rows = pl.ds(8 * q, 8)
        high, low = halves(fine[rows].reshape(256, 128))
        done[rows] = direct[rows] + dot(jnp.concatenate([high, low], 1), up1[...]).reshape(8, 32, 256)
        copies.append(pltpu.make_async_copy(done.at[rows], out.at[rows], sems.at[q]))
        copies[q].start()
    for copy in copies:
        copy.wait()


def section(table, own, left, right, base, at):
    b = left[pl.ds(base, 48)][10 * at:10 * at + 16]
    a = right[pl.ds(base, 48)][10 * at:10 * at + 16]
    high, low = halves(jnp.concatenate([own, b, a], 0))
    return dot(table[...], jnp.concatenate([high, low, high], 0))


def inner_kernel(taps, c, left, right, y0, z0h, z0l, out, v, wh, wl):
    @pl.loop(0, 8, unroll=4)
    def _(q):
        base = pl.multiple_of(40 * q, 8)
        for at in range(4):
            i = 4 * q + at
            v[i] = section(y0, c[i], left, right, base, at)

    @pl.loop(0, 4)
    def _(g):
        for member in range(3):
            rows = pl.ds(pl.multiple_of(32 * member + 8 * g, 8), 8)
            scale = [taps[0, member, k] for k in range(TAPS)]
            for h in range(2):
                lanes = pl.ds(128 * h, 128)
                for base in range(0, 32, 8):
                    sums = [None] * 8
                    for i in range(max(base - RADIUS, 0), min(base + 8 + RADIUS, 32)):
                        value = v[i, rows, lanes]
                        for m in range(8):
                            k = i - base - m + RADIUS
                            if 0 <= k < TAPS:
                                term = scale[k] * value
                                sums[m] = term if sums[m] is None else sums[m] + term
                    for m in range(0, 8, 2):
                        high, low = halves(jnp.concatenate([sums[m], sums[m + 1]], 0))
                        at = (pl.ds(8 * (base + m), 16), pl.ds(256 * member + 128 * h, 128))
                        wh[at] = high
                        wl[at] = low
        cols = pl.ds(pl.multiple_of(8 * g, 8), 8)
        total = dot(wh[...], z0h[...]) + dot(wl[...], z0h[...]) + dot(wh[...], z0l[...])
        out[:, cols] = total.reshape(32, 8, 256)


def finest_kernel(taps, before, after, left, right, y0, z0h, z0l, inner, out, v, wh, wl):
    for i in range(20):
        own = before[pl.ds(32 * i, 32)] if i < 10 else after[pl.ds(32 * (i - 10), 32)]
        b = left[pl.ds(10 * i, 16)]
        a = right[pl.ds(10 * i, 16)]
        high, low = halves(jnp.concatenate([own, b, a], 0))
        v[i] = dot(y0[...], jnp.concatenate([high, low, high], 0))

    @pl.loop(0, 4)
    def _(g):
        for member in range(3):
            rows = pl.ds(pl.multiple_of(32 * member + 8 * g, 8), 8)
            scale = [taps[0, member, k] for k in range(TAPS)]
            for h in range(2):
                lanes = pl.ds(128 * h, 128)
                sums = [None] * 20
                for r in range(20):
                    value = v[r, rows, lanes]
                    for m in range(10):
                        k = r - m if r < 10 else 20 + r - 10 - m
                        at = m if r < 10 else 10 + m
                        if r < 10 and m > r or r >= 10 and m < r - 10:
                            continue
                        term = scale[k] * value
                        sums[at] = term if sums[at] is None else sums[at] + term
                for m in range(0, 20, 2):
                    high, low = halves(jnp.concatenate([sums[m], sums[m + 1]], 0))
                    at = (pl.ds(pl.multiple_of(160 * g, 32) + 8 * m, 16), pl.ds(256 * member + 128 * h, 128))
                    wh[at] = high
                    wl[at] = low

    total = dot(wh[...], z0h[...]) + dot(wl[...], z0h[...]) + dot(wh[...], z0l[...])
    for g in range(4):
        cols = pl.ds(8 * g, 8)
        piece = total[160 * g:160 * g + 160].reshape(20, 8, 256)
        out[pl.ds(0, 10), cols] = inner[pl.ds(0, 10), cols] + piece[:10]
        out[pl.ds(10, 12), cols] = inner[pl.ds(10, 12), cols]
        out[pl.ds(22, 10), cols] = inner[pl.ds(22, 10), cols] + piece[10:]


def call(kernel, outs, scratch=(), scalars=0, count=0, flops=0, moved=0, name=None, sems=0, far=False):
    vmem = pl.BlockSpec(memory_space=pltpu.VMEM)
    smem = pl.BlockSpec(memory_space=pltpu.SMEM)
    hbm = pl.BlockSpec(memory_space=pltpu.HBM)
    shapes = [jax.ShapeDtypeStruct(*o) for o in outs]
    return pl.pallas_call(
        kernel,
        out_shape=shapes,
        in_specs=[smem] * scalars + [vmem] * (count - scalars),
        out_specs=[hbm if far else vmem] * len(shapes),
        scratch_shapes=[pltpu.VMEM(*s) for s in scratch] + [pltpu.SemaphoreType.DMA((sems,))] * (sems > 0),
        compiler_params=pltpu.CompilerParams(vmem_limit_bytes=VMEM_LIMIT),
        cost_estimate=pl.CostEstimate(flops=flops, bytes_accessed=moved, transcendentals=0),
        name=name,
    )


def shift(x, axis, by):
    n = lax.axis_size(axis)
    return lax.ppermute(x, axis, [(i, (i + by) % n) for i in range(n)])


def body(charges, kernel_taps):
    taps = kernel_taps
    l1, l2, s_up, s_down, last, first, o_up, o_down = call(
        restrict_kernel,
        [((18, 24, 128), F32), ((6, 16, 128), F32), ((288, 128), F32), ((288, 128), F32),
         ((320, 256), F32), ((320, 256), F32), ((328, 256), F32), ((328, 256), F32)],
        [((18, 24, 256), F32), ((12, 16, 128), F32)], 0, 1, 10**8, 2 * 10**6, name="restrict",
    )(charges)
    x_left = shift(s_up, "gx", 1)
    x_right = shift(s_down, "gx", -1)
    taps, l1 = lax.optimization_barrier((taps, l1))
    y0, y1, y2, z0h, z0l, z1, z2, up1 = call(
        matrices_kernel,
        [((96, 192), BF), ((96, 144), BF), ((96, 144), BF), ((768, 256), BF), ((768, 256), BF),
         ((768, 256), BF), ((768, 256), BF), ((256, 256), BF)],
        [], 1, 1, 10**8, 4 * 10**6, name="matrices",
    )(taps)
    own_left = shift(o_up, "gy", 1)
    own_right = shift(o_down, "gy", -1)
    x_left, x_right, y0 = lax.optimization_barrier((x_left, x_right, y0))
    c_up, c_down = call(
        face_x_kernel, [((344, 256), F32), ((344, 256), F32)], [], 0, 4, 2 * 10**10, 2 * 10**6, name="face_x",
    )(last, first, x_left, x_right)
    before = shift(c_up, "gx", 1)
    after = shift(c_down, "gx", -1)
    x_left, x_right, c_up = lax.optimization_barrier((x_left, x_right, c_up))
    l1x, g_up, g_down = call(
        gather_fine_kernel, [((38, 24, 128), F32), ((456, 128), F32), ((456, 128), F32)],
        [], 0, 3, 2 * 10**10, 2 * 10**6, name="gather_fine",
    )(l1, x_left, x_right)
    fine_left = shift(g_up, "gy", 1)
    fine_right = shift(g_down, "gy", -1)
    y0, g_up, g_down = lax.optimization_barrier((y0, g_up, g_down))
    inner, = call(
        inner_kernel, [((32, 32, 256), F32)],
        [((32, 96, 256), F32), ((256, 768), BF), ((256, 768), BF)], 1, 7, 2 * 10**9, 6 * 10**6, name="inner",
    )(taps, charges, own_left, own_right, y0, z0h, z0l)
    before, after, inner, fine_left, fine_right = lax.optimization_barrier(
        (before, after, inner, fine_left, fine_right)
    )
    l2x, f_up, f_down, t_up, t_down = call(
        gather_top_kernel,
        [((16, 16, 128), F32), ((296, 256), F32), ((296, 256), F32), ((80, 128), F32), ((80, 128), F32)],
        [], 0, 5, 10**6, 5 * 10**6, name="gather_top",
    )(before, after, l2, x_left, x_right)
    left = shift(f_up, "gy", 1)
    right = shift(f_down, "gy", -1)
    left2 = shift(t_up, "gy", 2)
    right2 = shift(t_down, "gy", -2)
    l1x, f_up, f_down = lax.optimization_barrier((l1x, f_up, f_down))
    mid, = call(
        fine_level_kernel, [((18, 32, 128), F32)],
        [((38, 48, 128), F32), ((38, 96, 128), F32), ((18, 96, 128), F32)],
        1, 6, 4 * 10**8, 4 * 10**6, name="fine_level",
    )(taps, l1x, fine_left, fine_right, y1, z1)
    left, right, mid = lax.optimization_barrier((left, right, mid))
    direct, = call(
        finest_kernel, [((32, 32, 256), F32)],
        [((20, 96, 256), F32), ((640, 768), BF), ((640, 768), BF)],
        1, 9, 2 * 10**9, 6 * 10**6, name="finest",
    )(taps, before, after, left, right, y0, z0h, z0l, inner)
    result, = call(
        upper_kernel, [((32, 32, 256), F32)],
        [((16, 48, 128), F32), ((32, 96, 128), F32), ((11, 96, 128), F32), ((18, 32, 128), F32),
         ((32, 32, 128), F32), ((32, 32, 256), F32)],
        1, 11, 4 * 10**8, 4 * 10**6, name="upper", sems=4, far=True,
    )(taps, l2x, left, right, left2, right2, y2, z2, up1, mid, direct)
    return result


def solution(mesh):
    return jax.shard_map(
        body,
        mesh=mesh,
        in_specs=(P("gx", "gy", None), P()),
        out_specs=P("gx", "gy", None),
        check_vma=False,
    )
```

```python
import jax
import jax.numpy as jnp
from jax import lax
from jax.experimental import pallas as pl
from jax.experimental.pallas import tpu as pltpu
from jax.sharding import PartitionSpec as P

SPLINE = (0.125, 0.5, 0.75, 0.5, 0.125)
RADIUS = 10
TAPS = 21
BF = jnp.bfloat16
F32 = jnp.float32
VMEM_LIMIT = 48 * 1024 * 1024


def halves(x):
    high = x.astype(BF)
    return high, (x - high.astype(F32)).astype(BF)


def dot(a, b):
    return jnp.dot(a, b, preferred_element_type=F32)


def spline_sum(read, center, low, high):
    total = None
    for k in range(-2, 3):
        if low <= 2 * center + k <= high:
            term = SPLINE[k + 2] * read(2 * center + k)
            total = term if total is None else total + term
    return total


def matrices_kernel(taps, y0, y1, y2, z0h, z0l, z1, z2, up1):
    def iota(shape, dim):
        return lax.broadcasted_iota(jnp.int32, shape, dim)

    def pick(level, member, offsets):
        table = jnp.zeros(offsets.shape, F32)
        for k in range(TAPS):
            table = jnp.where(offsets == k, taps[level, member, k], table)
        return table

    def cycle(level, member, length):
        offsets = (iota((length, length), 0) - iota((length, length), 1) + RADIUS) & (length - 1)
        return pick(level, member, offsets)

    def spread(lanes, width, pieces):
        cols = lanes
        for _ in range(2):
            cols = jnp.where(cols >= width, cols - width, cols)
        place = jnp.full(lanes.shape, -99, jnp.int32)
        for begin, end, position in pieces:
            place = jnp.where((cols >= begin) & (cols < end), cols - begin + position, place)
        return place

    def put(out, rows, table, width):
        high, low = halves(table)
        out[rows] = jnp.where(iota(table.shape, 1) < 2 * width, high.astype(F32), low.astype(F32)).astype(BF)

    def block(out, base, table, count):
        high, low = halves(table)
        zero = jnp.zeros((128, 128), BF)
        if count < 128:
            for at in (base, base + 128):
                out[pl.ds(at + count, 128 - count)] = jnp.zeros((128 - count, 256), BF)
        out[pl.ds(base, count), pl.ds(0, 128)] = high
        out[pl.ds(base, count), pl.ds(128, 128)] = low
        out[pl.ds(base + 128, count), pl.ds(0, 128)] = high
        out[pl.ds(base + 128, count), pl.ds(128, 128)] = zero[:count]

    def product(weights, table):
        high, low = halves(table)
        return dot(weights, high) + dot(weights, low)

    place0 = spread(iota((32, 192), 1), 64, ((0, 32, 0), (32, 42, -10), (48, 58, 32))) - iota((32, 192), 0) + RADIUS
    place1 = spread(iota((32, 144), 1), 48, ((0, 12, -11), (12, 30, -1), (30, 42, 15)))
    place1 = place1 - (iota((32, 144), 0) - 1) + RADIUS
    place2 = spread(iota((32, 144), 1), 48, ((0, 11, -1), (16, 27, -9), (27, 38, 7), (38, 43, -11), (43, 48, 15)))
    place2 = place2 - (iota((32, 144), 0) - 1) + RADIUS
    columns = iota((32, 32), 1) - 1
    lift1 = jnp.where(columns < 17, spline_of(iota((32, 32), 0) - 2 * columns), 0.0).astype(BF)
    lift2 = jnp.where(columns < 10, spline_of(iota((32, 32), 0) - 1 - 2 * columns), 0.0).astype(BF)
    lift2 = dot(lift1, lift2).astype(BF)
    up2 = cyclic_iota((64, 128), 0, 1, 128).astype(BF)
    up1[pl.ds(0, 128)] = cyclic_iota((128, 256), 0, 1, 256).astype(BF)
    up1[pl.ds(128, 128)] = cyclic_iota((128, 256), 0, 1, 256).astype(BF)
    for member in range(3):
        rows = pl.ds(32 * member, 32)
        put(y0, rows, pick(0, member, place0), 64)
        put(y1, rows, product(lift1, pick(1, member, place1)), 48)
        put(y2, rows, product(lift2, pick(2, member, place2)), 48)
        high, low = halves(cycle(0, member, 256))
        z0h[pl.ds(256 * member, 256)] = high
        z0l[pl.ds(256 * member, 256)] = low
        block(z1, 256 * member, cycle(1, member, 128), 128)
        high, low = halves(cycle(2, member, 64))
        block(z2, 256 * member, dot(high, up2) + dot(low, up2), 64)


def spline_iota(shape, offset, coarse_dim, fine_dim, keep=None):
    fine = lax.broadcasted_iota(jnp.int32, shape, fine_dim)
    coarse = lax.broadcasted_iota(jnp.int32, shape, coarse_dim)
    delta = fine - 2 * coarse + offset
    if keep is not None:
        delta = jnp.where(coarse < keep, delta, 99)
    return spline_of(delta)


def spline_of(delta):
    far = jnp.abs(delta)
    return jnp.where(far == 0, 0.75, jnp.where(far == 1, 0.5, jnp.where(far == 2, 0.125, 0.0)))


def cyclic_iota(shape, coarse_dim, fine_dim, fine_len):
    fine = lax.broadcasted_iota(jnp.int32, shape, fine_dim)
    coarse = lax.broadcasted_iota(jnp.int32, shape, coarse_dim)
    return spline_of(((fine - 2 * coarse + 2) & (fine_len - 1)) - 2)


def restrict_kernel(c, l1, l2, up1, down1, last, first, face_up, face_down, s1, s2):
    ry = spline_iota((24, 32), 2, 0, 1, 18).astype(BF)
    for i in range(-1, 17):
        high, low = halves(spline_sum(lambda r: c[r], i, 0, 31))
        s1[i + 1] = dot(ry, high) + dot(ry, low)
    for i in range(32):
        face_up[pl.ds(10 * i, 10)] = c[i, 22:32]
        face_down[pl.ds(10 * i, 10)] = c[i, 0:10]
    face_up[pl.ds(320, 8)] = jnp.zeros((8, 256), F32)
    face_down[pl.ds(320, 8)] = jnp.zeros((8, 256), F32)
    for r in range(10):
        last[pl.ds(32 * r, 32)] = c[22 + r]
        first[pl.ds(32 * r, 32)] = c[r]
    rz = cyclic_iota((256, 128), 1, 0, 256).astype(BF)
    high, low = halves(s1[...].reshape(18 * 24, 256))
    l1[...] = (dot(high, rz) + dot(low, rz)).reshape(18, 24, 128)
    ry2 = spline_iota((16, 24), 1, 0, 1, 11).astype(BF)
    for i in range(-1, 10):
        high, low = halves(spline_sum(lambda r: l1[r + 1], i, -1, 16))
        s2[i + 1] = dot(ry2, high) + dot(ry2, low)
    s2[11] = jnp.zeros((16, 128), F32)
    near = s2[pl.ds(0, 6)].reshape(96, 128)
    far = s2[pl.ds(6, 6)].reshape(96, 128)
    lanes = lax.broadcasted_iota(jnp.int32, (128, 128), 1)
    both = spline_of(((lax.broadcasted_iota(jnp.int32, (128, 128), 0) - 2 * (lanes & 63) + 2) & 127) - 2)
    total = jnp.zeros((96, 128), F32)
    for part, upper in ((near, False), (far, True)):
        weights = jnp.where((lanes >= 64) == upper, both, 0.0).astype(BF)
        high, low = halves(part)
        total = total + dot(high, weights) + dot(low, weights)
    total = total.reshape(6, 16, 128)
    l2[...] = total
    up1[pl.ds(64, 8)] = jnp.zeros((8, 128), F32)
    down1[pl.ds(64, 8)] = jnp.zeros((8, 128), F32)
    for j in range(6):
        up1[pl.ds(11 * j, 11)] = total[j, :11]
        down1[pl.ds(11 * j, 11)] = total[j, :11]
    for r in range(12):
        up1[pl.ds(72 + 18 * r, 18)] = l1[6 + r, :18]
        down1[pl.ds(72 + 18 * r, 18)] = l1[r, :18]


def paired(base, count, j):
    return (pl.ds(base + count * (j // 2), count), pl.ds(128 * (j % 2), 128))


def face_x_kernel(last, first, left, right, up, down):
    up[pl.ds(0, 320)] = last[...]
    down[pl.ds(0, 320)] = first[...]
    lower = lax.broadcasted_iota(jnp.int32, (11, 128), 1) < 64
    for p in range(3):
        even = 2 * p
        odd = min(even + 1, 4)
        a = left[pl.ds(11 * even, 11)]
        b = left[pl.ds(11 * odd, 11)]
        up[paired(320, 11, p)] = jnp.where(lower, pltpu.roll(a, 64, 1), b)
        a = right[pl.ds(11 * even, 11)]
        b = right[pl.ds(11 * odd, 11)]
        down[paired(320, 11, p)] = jnp.where(lower, a, pltpu.roll(b, 64, 1))


def gather_fine_kernel(l1, left, right, l1x, up, down):
    for i in range(38):
        if i < 12:
            l1x[i, :18] = left[pl.ds(72 + 18 * i, 18)]
            l1x[i, pl.ds(18, 6)] = jnp.zeros((6, 128), F32)
        elif i >= 26:
            l1x[i, :18] = right[pl.ds(72 + 18 * (i - 26), 18)]
            l1x[i, pl.ds(18, 6)] = jnp.zeros((6, 128), F32)
        if 10 <= i < 12 or 26 <= i < 28:
            l1x[i] = l1x[i] + l1[i - 10]
        elif 12 <= i < 26:
            l1x[i] = l1[i - 10]
    for i in range(38):
        up[pl.ds(12 * i, 12)] = l1x[i, 6:18]
        down[pl.ds(12 * i, 12)] = l1x[i, 0:12]


def gather_top_kernel(before, after, l2, left, right, l2x, up, down, up2, down2):
    for i in range(20):
        row = before[pl.ds(32 * i, 32)] if i < 10 else after[pl.ds(32 * (i - 10), 32)]
        up[pl.ds(10 * i, 10)] = row[22:32]
        down[pl.ds(10 * i, 10)] = row[0:10]
    up[pl.ds(200, 8)] = jnp.zeros((8, 256), F32)
    down[pl.ds(200, 8)] = jnp.zeros((8, 256), F32)
    lanes = lax.broadcasted_iota(jnp.int32, (11, 128), 1)
    lower = lanes < 64
    rolled = lambda x: pltpu.roll(x, 64, 1)
    for j in range(16):
        low = []
        high = []
        if j < 5:
            slab = before[paired(320, 11, j // 2)]
            low.append(slab if j % 2 == 0 else rolled(slab))
        if 2 <= j < 8:
            low.append(left[pl.ds(11 * (j - 2), 11)])
        if 8 <= j < 13:
            low.append(rolled(left[pl.ds(11 * (j - 8), 11)]))
        if j >= 10:
            low.append(l2[j - 10, :11])
        if j < 5:
            high.append(l2[j, :11])
        if 2 <= j < 8:
            high.append(rolled(right[pl.ds(11 * (j - 2), 11)]))
        if 8 <= j < 13:
            high.append(right[pl.ds(11 * (j - 8), 11)])
        if 10 <= j < 15:
            slab = after[paired(320, 11, (j - 10) // 2)]
            high.append(rolled(slab) if j % 2 == 0 else slab)
        row = jnp.where(lower, sum(low, jnp.zeros((11, 128), F32)), sum(high, jnp.zeros((11, 128), F32)))
        l2x[j, :11] = row
        l2x[j, pl.ds(11, 5)] = jnp.zeros((5, 128), F32)
        up[paired(208, 11, j)] = row
        down[paired(208, 11, j)] = row
        up2[pl.ds(5 * j, 5)] = row[6:11]
        down2[pl.ds(5 * j, 5)] = row[0:5]


def correlate_x(taps, level, v, w, count, many):
    @pl.loop(0, 12, unroll=12)
    def _(g):
        member = g // 4
        rows = pl.ds(pl.multiple_of(8 * g, 8), 8)
        scale = [taps[level, member, k] for k in range(TAPS)]
        for base in range(0, count, many):
            sums = [None] * many
            for i in range(base, base + many + TAPS - 1):
                value = v[i, rows]
                for m in range(many):
                    k = i - base - m
                    if 0 <= k < TAPS:
                        term = scale[k] * value
                        sums[m] = term if sums[m] is None else sums[m] + term
            for m in range(many):
                w[base + m, rows] = sums[m]


def correlate_z(w, count, table):
    total = jnp.zeros((count * 32, 256), F32)
    for member in range(3):
        high, low = halves(w[:, pl.ds(32 * member, 32)].reshape(count * 32, 128))
        total = total + dot(jnp.concatenate([high, low], 1), table[pl.ds(256 * member, 256)])
    return (total[:, :128] + total[:, 128:]).reshape(count, 32, 128)


def fine_level_kernel(taps, l1x, left, right, y1, z1, mid, f1, v1, w1):
    for i in range(38):
        f1[i, pl.ds(0, 12)] = left[pl.ds(12 * i, 12)]
        f1[i, pl.ds(12, 18)] = l1x[i, :18]
        f1[i, pl.ds(30, 12)] = right[pl.ds(12 * i, 12)]
        f1[i, pl.ds(42, 6)] = jnp.zeros((6, 128), F32)

    @pl.loop(0, 38, unroll=19)
    def _(i):
        high, low = halves(f1[i])
        v1[i] = dot(y1[...], jnp.concatenate([high, low, high], 0))

    correlate_x(taps, 1, v1, w1, 18, 9)
    mid[...] = correlate_z(w1, 18, z1)


def upper_kernel(taps, l2x, left, right, left2, right2, y2, z2, up1, mid_in, direct, out,
                 f2, v2, w2, mid, fine, done, sems):
    for j in range(16):
        f2[j, pl.ds(0, 16)] = l2x[j]
        f2[j, pl.ds(16, 11)] = left[paired(208, 11, j)]
        f2[j, pl.ds(27, 11)] = right[paired(208, 11, j)]
        f2[j, pl.ds(38, 5)] = left2[pl.ds(5 * j, 5)]
        f2[j, pl.ds(43, 5)] = right2[pl.ds(5 * j, 5)]

    @pl.loop(0, 16, unroll=16)
    def _(j):
        high, low = halves(f2[j])
        v = dot(y2[...], jnp.concatenate([high, low, high], 0))
        v2[j] = v
        v2[16 + j] = pltpu.roll(v, 64, 1)

    correlate_x(taps, 2, v2, w2, 11, 11)
    v2[pl.ds(0, 11), pl.ds(0, 32)] = correlate_z(w2, 11, z2)
    top = lambda i: v2[i + 1, pl.ds(0, 32)]
    for a in range(-1, 9):
        if a >= 0:
            mid[2 * a + 1] = mid_in[2 * a + 1] + (0.75 * top(a) + 0.125 * (top(a - 1) + top(a + 1)))
        if a < 8:
            mid[2 * a + 2] = mid_in[2 * a + 2] + 0.5 * (top(a) + top(a + 1))
    for a in range(16):
        fine[2 * a] = 0.75 * mid[a + 1] + 0.125 * (mid[a] + mid[a + 2])
        fine[2 * a + 1] = 0.5 * (mid[a + 1] + mid[a + 2])
    copies = []
    for q in range(4):
        rows = pl.ds(8 * q, 8)
        high, low = halves(fine[rows].reshape(256, 128))
        done[rows] = direct[rows] + dot(jnp.concatenate([high, low], 1), up1[...]).reshape(8, 32, 256)
        copies.append(pltpu.make_async_copy(done.at[rows], out.at[rows], sems.at[q]))
        copies[q].start()
    for copy in copies:
        copy.wait()


def section(table, own, left, right, base, at):
    b = left[pl.ds(base, 48)][10 * at:10 * at + 16]
    a = right[pl.ds(base, 48)][10 * at:10 * at + 16]
    high, low = halves(jnp.concatenate([own, b, a], 0))
    return dot(table[...], jnp.concatenate([high, low, high], 0))


def inner_kernel(taps, c, left, right, y0, z0h, z0l, out, v, wh, wl):
    @pl.loop(0, 8, unroll=4)
    def _(q):
        base = pl.multiple_of(40 * q, 8)
        for at in range(4):
            i = 4 * q + at
            v[i] = section(y0, c[i], left, right, base, at)

    @pl.loop(0, 4)
    def _(g):
        for member in range(3):
            rows = pl.ds(pl.multiple_of(32 * member + 8 * g, 8), 8)
            scale = [taps[0, member, k] for k in range(TAPS)]
            for h in range(2):
                lanes = pl.ds(128 * h, 128)
                for base in range(0, 32, 8):
                    sums = [None] * 8
                    for i in range(max(base - RADIUS, 0), min(base + 8 + RADIUS, 32)):
                        value = v[i, rows, lanes]
                        for m in range(8):
                            k = i - base - m + RADIUS
                            if 0 <= k < TAPS:
                                term = scale[k] * value
                                sums[m] = term if sums[m] is None else sums[m] + term
                    for m in range(0, 8, 2):
                        high, low = halves(jnp.concatenate([sums[m], sums[m + 1]], 0))
                        at = (pl.ds(8 * (base + m), 16), pl.ds(256 * member + 128 * h, 128))
                        wh[at] = high
                        wl[at] = low
        cols = pl.ds(pl.multiple_of(8 * g, 8), 8)
        total = dot(wh[...], z0h[...]) + dot(wl[...], z0h[...]) + dot(wh[...], z0l[...])
        out[:, cols] = total.reshape(32, 8, 256)


def finest_kernel(taps, before, after, left, right, y0, z0h, z0l, inner, out, v, wh, wl):
    for i in range(20):
        own = before[pl.ds(32 * i, 32)] if i < 10 else after[pl.ds(32 * (i - 10), 32)]
        b = left[pl.ds(10 * i, 16)]
        a = right[pl.ds(10 * i, 16)]
        high, low = halves(jnp.concatenate([own, b, a], 0))
        v[i] = dot(y0[...], jnp.concatenate([high, low, high], 0))

    @pl.loop(0, 4, unroll=4)
    def _(g):
        for member in range(3):
            rows = pl.ds(pl.multiple_of(32 * member + 8 * g, 8), 8)
            scale = [taps[0, member, k] for k in range(TAPS)]
            for h in range(2):
                lanes = pl.ds(128 * h, 128)
                sums = [None] * 20
                for r in range(20):
                    value = v[r, rows, lanes]
                    for m in range(10):
                        k = r - m if r < 10 else 20 + r - 10 - m
                        at = m if r < 10 else 10 + m
                        if r < 10 and m > r or r >= 10 and m < r - 10:
                            continue
                        term = scale[k] * value
                        sums[at] = term if sums[at] is None else sums[at] + term
                for m in range(0, 20, 2):
                    high, low = halves(jnp.concatenate([sums[m], sums[m + 1]], 0))
                    at = (pl.ds(pl.multiple_of(160 * g, 32) + 8 * m, 16), pl.ds(256 * member + 128 * h, 128))
                    wh[at] = high
                    wl[at] = low

    total = dot(wh[...], z0h[...]) + dot(wl[...], z0h[...]) + dot(wh[...], z0l[...])
    for g in range(4):
        cols = pl.ds(8 * g, 8)
        piece = total[160 * g:160 * g + 160].reshape(20, 8, 256)
        out[pl.ds(0, 10), cols] = inner[pl.ds(0, 10), cols] + piece[:10]
        out[pl.ds(10, 12), cols] = inner[pl.ds(10, 12), cols]
        out[pl.ds(22, 10), cols] = inner[pl.ds(22, 10), cols] + piece[10:]


def call(kernel, outs, scratch=(), scalars=0, count=0, flops=0, moved=0, name=None, sems=0, far=False):
    vmem = pl.BlockSpec(memory_space=pltpu.VMEM)
    smem = pl.BlockSpec(memory_space=pltpu.SMEM)
    hbm = pl.BlockSpec(memory_space=pltpu.HBM)
    shapes = [jax.ShapeDtypeStruct(*o) for o in outs]
    return pl.pallas_call(
        kernel,
        out_shape=shapes,
        in_specs=[smem] * scalars + [vmem] * (count - scalars),
        out_specs=[hbm if far else vmem] * len(shapes),
        scratch_shapes=[pltpu.VMEM(*s) for s in scratch] + [pltpu.SemaphoreType.DMA((sems,))] * (sems > 0),
        compiler_params=pltpu.CompilerParams(vmem_limit_bytes=VMEM_LIMIT),
        cost_estimate=pl.CostEstimate(flops=flops, bytes_accessed=moved, transcendentals=0),
        name=name,
    )


def shift(x, axis, by):
    n = lax.axis_size(axis)
    return lax.ppermute(x, axis, [(i, (i + by) % n) for i in range(n)])


def body(charges, kernel_taps):
    taps = kernel_taps
    l1, l2, s_up, s_down, last, first, o_up, o_down = call(
        restrict_kernel,
        [((18, 24, 128), F32), ((6, 16, 128), F32), ((288, 128), F32), ((288, 128), F32),
         ((320, 256), F32), ((320, 256), F32), ((328, 256), F32), ((328, 256), F32)],
        [((18, 24, 256), F32), ((12, 16, 128), F32)], 0, 1, 10**8, 2 * 10**6, name="restrict",
    )(charges)
    x_left = shift(s_up, "gx", 1)
    x_right = shift(s_down, "gx", -1)
    taps, l1 = lax.optimization_barrier((taps, l1))
    y0, y1, y2, z0h, z0l, z1, z2, up1 = call(
        matrices_kernel,
        [((96, 192), BF), ((96, 144), BF), ((96, 144), BF), ((768, 256), BF), ((768, 256), BF),
         ((768, 256), BF), ((768, 256), BF), ((256, 256), BF)],
        [], 1, 1, 10**8, 4 * 10**6, name="matrices",
    )(taps)
    own_left = shift(o_up, "gy", 1)
    own_right = shift(o_down, "gy", -1)
    x_left, x_right, y0 = lax.optimization_barrier((x_left, x_right, y0))
    c_up, c_down = call(
        face_x_kernel, [((344, 256), F32), ((344, 256), F32)], [], 0, 4, 2 * 10**10, 2 * 10**6, name="face_x",
    )(last, first, x_left, x_right)
    before = shift(c_up, "gx", 1)
    after = shift(c_down, "gx", -1)
    x_left, x_right, c_up = lax.optimization_barrier((x_left, x_right, c_up))
    l1x, g_up, g_down = call(
        gather_fine_kernel, [((38, 24, 128), F32), ((456, 128), F32), ((456, 128), F32)],
        [], 0, 3, 2 * 10**10, 2 * 10**6, name="gather_fine",
    )(l1, x_left, x_right)
    fine_left = shift(g_up, "gy", 1)
    fine_right = shift(g_down, "gy", -1)
    y0, g_up, g_down = lax.optimization_barrier((y0, g_up, g_down))
    inner, = call(
        inner_kernel, [((32, 32, 256), F32)],
        [((32, 96, 256), F32), ((256, 768), BF), ((256, 768), BF)], 1, 7, 2 * 10**9, 6 * 10**6, name="inner",
    )(taps, charges, own_left, own_right, y0, z0h, z0l)
    before, after, inner, fine_left, fine_right = lax.optimization_barrier(
        (before, after, inner, fine_left, fine_right)
    )
    l2x, f_up, f_down, t_up, t_down = call(
        gather_top_kernel,
        [((16, 16, 128), F32), ((296, 256), F32), ((296, 256), F32), ((80, 128), F32), ((80, 128), F32)],
        [], 0, 5, 10**6, 5 * 10**6, name="gather_top",
    )(before, after, l2, x_left, x_right)
    left = shift(f_up, "gy", 1)
    right = shift(f_down, "gy", -1)
    left2 = shift(t_up, "gy", 2)
    right2 = shift(t_down, "gy", -2)
    l1x, f_up, f_down = lax.optimization_barrier((l1x, f_up, f_down))
    mid, = call(
        fine_level_kernel, [((18, 32, 128), F32)],
        [((38, 48, 128), F32), ((38, 96, 128), F32), ((18, 96, 128), F32)],
        1, 6, 4 * 10**8, 4 * 10**6, name="fine_level",
    )(taps, l1x, fine_left, fine_right, y1, z1)
    left, right, mid = lax.optimization_barrier((left, right, mid))
    direct, = call(
        finest_kernel, [((32, 32, 256), F32)],
        [((20, 96, 256), F32), ((640, 768), BF), ((640, 768), BF)],
        1, 9, 2 * 10**9, 6 * 10**6, name="finest",
    )(taps, before, after, left, right, y0, z0h, z0l, inner)
    result, = call(
        upper_kernel, [((32, 32, 256), F32)],
        [((16, 48, 128), F32), ((32, 96, 128), F32), ((11, 96, 128), F32), ((18, 32, 128), F32),
         ((32, 32, 128), F32), ((32, 32, 256), F32)],
        1, 11, 4 * 10**8, 4 * 10**6, name="upper", sems=4, far=True,
    )(taps, l2x, left, right, left2, right2, y2, z2, up1, mid, direct)
    return result


def solution(mesh):
    return jax.shard_map(
        body,
        mesh=mesh,
        in_specs=(P("gx", "gy", None), P()),
        out_specs=P("gx", "gy", None),
        check_vma=False,
    )
```

```python
import jax
import jax.numpy as jnp
from jax import lax
from jax.experimental import pallas as pl
from jax.experimental.pallas import tpu as pltpu
from jax.sharding import PartitionSpec as P

SPLINE = (0.125, 0.5, 0.75, 0.5, 0.125)
RADIUS = 10
TAPS = 21
BF = jnp.bfloat16
F32 = jnp.float32
VMEM_LIMIT = 48 * 1024 * 1024


def halves(x):
    high = x.astype(BF)
    return high, (x - high.astype(F32)).astype(BF)


def dot(a, b):
    return jnp.dot(a, b, preferred_element_type=F32)


def spline_sum(read, center, low, high):
    total = None
    for k in range(-2, 3):
        if low <= 2 * center + k <= high:
            term = SPLINE[k + 2] * read(2 * center + k)
            total = term if total is None else total + term
    return total


def matrices_kernel(taps, y0, y1, y2, z0h, z0l, z1, z2, up1):
    def iota(shape, dim):
        return lax.broadcasted_iota(jnp.int32, shape, dim)

    def pick(level, member, offsets):
        table = jnp.zeros(offsets.shape, F32)
        for k in range(TAPS):
            table = jnp.where(offsets == k, taps[level, member, k], table)
        return table

    def cycle(level, member, length):
        offsets = (iota((length, length), 0) - iota((length, length), 1) + RADIUS) & (length - 1)
        return pick(level, member, offsets)

    def spread(lanes, width, pieces):
        cols = lanes
        for _ in range(2):
            cols = jnp.where(cols >= width, cols - width, cols)
        place = jnp.full(lanes.shape, -99, jnp.int32)
        for begin, end, position in pieces:
            place = jnp.where((cols >= begin) & (cols < end), cols - begin + position, place)
        return place

    def put(out, rows, table, width):
        high, low = halves(table)
        out[rows] = jnp.where(iota(table.shape, 1) < 2 * width, high.astype(F32), low.astype(F32)).astype(BF)

    def block(out, base, table, count):
        high, low = halves(table)
        zero = jnp.zeros((128, 128), BF)
        if count < 128:
            for at in (base, base + 128):
                out[pl.ds(at + count, 128 - count)] = jnp.zeros((128 - count, 256), BF)
        out[pl.ds(base, count), pl.ds(0, 128)] = high
        out[pl.ds(base, count), pl.ds(128, 128)] = low
        out[pl.ds(base + 128, count), pl.ds(0, 128)] = high
        out[pl.ds(base + 128, count), pl.ds(128, 128)] = zero[:count]

    def product(weights, table):
        high, low = halves(table)
        return dot(weights, high) + dot(weights, low)

    place0 = spread(iota((32, 192), 1), 64, ((0, 32, 0), (32, 42, -10), (48, 58, 32))) - iota((32, 192), 0) + RADIUS
    place1 = spread(iota((32, 144), 1), 48, ((0, 12, -11), (12, 30, -1), (30, 42, 15)))
    place1 = place1 - (iota((32, 144), 0) - 1) + RADIUS
    place2 = spread(iota((32, 144), 1), 48, ((0, 11, -1), (16, 27, -9), (27, 38, 7), (38, 43, -11), (43, 48, 15)))
    place2 = place2 - (iota((32, 144), 0) - 1) + RADIUS
    columns = iota((32, 32), 1) - 1
    lift1 = jnp.where(columns < 17, spline_of(iota((32, 32), 0) - 2 * columns), 0.0).astype(BF)
    lift2 = jnp.where(columns < 10, spline_of(iota((32, 32), 0) - 1 - 2 * columns), 0.0).astype(BF)
    lift2 = dot(lift1, lift2).astype(BF)
    up2 = cyclic_iota((64, 128), 0, 1, 128).astype(BF)
    up1[pl.ds(0, 128)] = cyclic_iota((128, 256), 0, 1, 256).astype(BF)
    up1[pl.ds(128, 128)] = cyclic_iota((128, 256), 0, 1, 256).astype(BF)
    for member in range(3):
        rows = pl.ds(32 * member, 32)
        put(y0, rows, pick(0, member, place0), 64)
        put(y1, rows, product(lift1, pick(1, member, place1)), 48)
        put(y2, rows, product(lift2, pick(2, member, place2)), 48)
        high, low = halves(cycle(0, member, 256))
        z0h[pl.ds(256 * member, 256)] = high
        z0l[pl.ds(256 * member, 256)] = low
        block(z1, 256 * member, cycle(1, member, 128), 128)
        high, low = halves(cycle(2, member, 64))
        block(z2, 256 * member, dot(high, up2) + dot(low, up2), 64)


def spline_iota(shape, offset, coarse_dim, fine_dim, keep=None):
    fine = lax.broadcasted_iota(jnp.int32, shape, fine_dim)
    coarse = lax.broadcasted_iota(jnp.int32, shape, coarse_dim)
    delta = fine - 2 * coarse + offset
    if keep is not None:
        delta = jnp.where(coarse < keep, delta, 99)
    return spline_of(delta)


def spline_of(delta):
    far = jnp.abs(delta)
    return jnp.where(far == 0, 0.75, jnp.where(far == 1, 0.5, jnp.where(far == 2, 0.125, 0.0)))


def cyclic_iota(shape, coarse_dim, fine_dim, fine_len):
    fine = lax.broadcasted_iota(jnp.int32, shape, fine_dim)
    coarse = lax.broadcasted_iota(jnp.int32, shape, coarse_dim)
    return spline_of(((fine - 2 * coarse + 2) & (fine_len - 1)) - 2)


def restrict_kernel(c, l1, l2, up1, down1, last, first, face_up, face_down, s1, s2):
    ry = spline_iota((24, 32), 2, 0, 1, 18).astype(BF)
    for i in range(-1, 17):
        high, low = halves(spline_sum(lambda r: c[r], i, 0, 31))
        s1[i + 1] = dot(ry, high) + dot(ry, low)
    for i in range(32):
        face_up[pl.ds(10 * i, 10)] = c[i, 22:32]
        face_down[pl.ds(10 * i, 10)] = c[i, 0:10]
    face_up[pl.ds(320, 8)] = jnp.zeros((8, 256), F32)
    face_down[pl.ds(320, 8)] = jnp.zeros((8, 256), F32)
    for r in range(10):
        last[pl.ds(32 * r, 32)] = c[22 + r]
        first[pl.ds(32 * r, 32)] = c[r]
    rz = cyclic_iota((256, 128), 1, 0, 256).astype(BF)
    high, low = halves(s1[...].reshape(18 * 24, 256))
    l1[...] = (dot(high, rz) + dot(low, rz)).reshape(18, 24, 128)
    ry2 = spline_iota((16, 24), 1, 0, 1, 11).astype(BF)
    for i in range(-1, 10):
        high, low = halves(spline_sum(lambda r: l1[r + 1], i, -1, 16))
        s2[i + 1] = dot(ry2, high) + dot(ry2, low)
    s2[11] = jnp.zeros((16, 128), F32)
    near = s2[pl.ds(0, 6)].reshape(96, 128)
    far = s2[pl.ds(6, 6)].reshape(96, 128)
    lanes = lax.broadcasted_iota(jnp.int32, (128, 128), 1)
    both = spline_of(((lax.broadcasted_iota(jnp.int32, (128, 128), 0) - 2 * (lanes & 63) + 2) & 127) - 2)
    total = jnp.zeros((96, 128), F32)
    for part, upper in ((near, False), (far, True)):
        weights = jnp.where((lanes >= 64) == upper, both, 0.0).astype(BF)
        high, low = halves(part)
        total = total + dot(high, weights) + dot(low, weights)
    total = total.reshape(6, 16, 128)
    l2[...] = total
    up1[pl.ds(64, 8)] = jnp.zeros((8, 128), F32)
    down1[pl.ds(64, 8)] = jnp.zeros((8, 128), F32)
    for j in range(6):
        up1[pl.ds(11 * j, 11)] = total[j, :11]
        down1[pl.ds(11 * j, 11)] = total[j, :11]
    for r in range(12):
        up1[pl.ds(72 + 18 * r, 18)] = l1[6 + r, :18]
        down1[pl.ds(72 + 18 * r, 18)] = l1[r, :18]


def paired(base, count, j):
    return (pl.ds(base + count * (j // 2), count), pl.ds(128 * (j % 2), 128))


def face_x_kernel(last, first, left, right, up, down):
    up[pl.ds(0, 320)] = last[...]
    down[pl.ds(0, 320)] = first[...]
    lower = lax.broadcasted_iota(jnp.int32, (11, 128), 1) < 64
    for p in range(3):
        even = 2 * p
        odd = min(even + 1, 4)
        a = left[pl.ds(11 * even, 11)]
        b = left[pl.ds(11 * odd, 11)]
        up[paired(320, 11, p)] = jnp.where(lower, pltpu.roll(a, 64, 1), b)
        a = right[pl.ds(11 * even, 11)]
        b = right[pl.ds(11 * odd, 11)]
        down[paired(320, 11, p)] = jnp.where(lower, a, pltpu.roll(b, 64, 1))


def gather_fine_kernel(l1, left, right, l1x, up, down):
    for i in range(38):
        if i < 12:
            l1x[i, :18] = left[pl.ds(72 + 18 * i, 18)]
            l1x[i, pl.ds(18, 6)] = jnp.zeros((6, 128), F32)
        elif i >= 26:
            l1x[i, :18] = right[pl.ds(72 + 18 * (i - 26), 18)]
            l1x[i, pl.ds(18, 6)] = jnp.zeros((6, 128), F32)
        if 10 <= i < 12 or 26 <= i < 28:
            l1x[i] = l1x[i] + l1[i - 10]
        elif 12 <= i < 26:
            l1x[i] = l1[i - 10]
    for i in range(38):
        up[pl.ds(12 * i, 12)] = l1x[i, 6:18]
        down[pl.ds(12 * i, 12)] = l1x[i, 0:12]


def gather_top_kernel(before, after, l2, left, right, l2x, up, down, up2, down2):
    for i in range(20):
        row = before[pl.ds(32 * i, 32)] if i < 10 else after[pl.ds(32 * (i - 10), 32)]
        up[pl.ds(10 * i, 10)] = row[22:32]
        down[pl.ds(10 * i, 10)] = row[0:10]
    up[pl.ds(200, 8)] = jnp.zeros((8, 256), F32)
    down[pl.ds(200, 8)] = jnp.zeros((8, 256), F32)
    lanes = lax.broadcasted_iota(jnp.int32, (11, 128), 1)
    lower = lanes < 64
    rolled = lambda x: pltpu.roll(x, 64, 1)
    for j in range(16):
        low = []
        high = []
        if j < 5:
            slab = before[paired(320, 11, j // 2)]
            low.append(slab if j % 2 == 0 else rolled(slab))
        if 2 <= j < 8:
            low.append(left[pl.ds(11 * (j - 2), 11)])
        if 8 <= j < 13:
            low.append(rolled(left[pl.ds(11 * (j - 8), 11)]))
        if j >= 10:
            low.append(l2[j - 10, :11])
        if j < 5:
            high.append(l2[j, :11])
        if 2 <= j < 8:
            high.append(rolled(right[pl.ds(11 * (j - 2), 11)]))
        if 8 <= j < 13:
            high.append(right[pl.ds(11 * (j - 8), 11)])
        if 10 <= j < 15:
            slab = after[paired(320, 11, (j - 10) // 2)]
            high.append(rolled(slab) if j % 2 == 0 else slab)
        row = jnp.where(lower, sum(low, jnp.zeros((11, 128), F32)), sum(high, jnp.zeros((11, 128), F32)))
        l2x[j, :11] = row
        l2x[j, pl.ds(11, 5)] = jnp.zeros((5, 128), F32)
        up[paired(208, 11, j)] = row
        down[paired(208, 11, j)] = row
        up2[pl.ds(5 * j, 5)] = row[6:11]
        down2[pl.ds(5 * j, 5)] = row[0:5]


def correlate_x(taps, level, v, w, count, many):
    @pl.loop(0, 12, unroll=4 if level == 1 else 12)
    def _(g):
        member = g // 4
        rows = pl.ds(pl.multiple_of(8 * g, 8), 8)
        scale = [taps[level, member, k] for k in range(TAPS)]
        for base in range(0, count, many):
            sums = [None] * many
            for i in range(base, base + many + TAPS - 1):
                value = v[i, rows]
                for m in range(many):
                    k = i - base - m
                    if 0 <= k < TAPS:
                        term = scale[k] * value
                        sums[m] = term if sums[m] is None else sums[m] + term
            for m in range(many):
                w[base + m, rows] = sums[m]


def correlate_z(w, count, table):
    total = jnp.zeros((count * 32, 256), F32)
    for member in range(3):
        high, low = halves(w[:, pl.ds(32 * member, 32)].reshape(count * 32, 128))
        total = total + dot(jnp.concatenate([high, low], 1), table[pl.ds(256 * member, 256)])
    return (total[:, :128] + total[:, 128:]).reshape(count, 32, 128)


def fine_level_kernel(taps, l1x, left, right, y1, z1, mid, f1, v1, w1):
    for i in range(38):
        f1[i, pl.ds(0, 12)] = left[pl.ds(12 * i, 12)]
        f1[i, pl.ds(12, 18)] = l1x[i, :18]
        f1[i, pl.ds(30, 12)] = right[pl.ds(12 * i, 12)]
        f1[i, pl.ds(42, 6)] = jnp.zeros((6, 128), F32)

    @pl.loop(0, 38, unroll=19)
    def _(i):
        high, low = halves(f1[i])
        v1[i] = dot(y1[...], jnp.concatenate([high, low, high], 0))

    correlate_x(taps, 1, v1, w1, 18, 9)
    mid[...] = correlate_z(w1, 18, z1)


def upper_kernel(taps, l2x, left, right, left2, right2, y2, z2, up1, mid_in, direct, out,
                 f2, v2, w2, mid, fine, done, sems):
    for j in range(16):
        f2[j, pl.ds(0, 16)] = l2x[j]
        f2[j, pl.ds(16, 11)] = left[paired(208, 11, j)]
        f2[j, pl.ds(27, 11)] = right[paired(208, 11, j)]
        f2[j, pl.ds(38, 5)] = left2[pl.ds(5 * j, 5)]
        f2[j, pl.ds(43, 5)] = right2[pl.ds(5 * j, 5)]

    @pl.loop(0, 16, unroll=16)
    def _(j):
        high, low = halves(f2[j])
        v = dot(y2[...], jnp.concatenate([high, low, high], 0))
        v2[j] = v
        v2[16 + j] = pltpu.roll(v, 64, 1)

    correlate_x(taps, 2, v2, w2, 11, 11)
    v2[pl.ds(0, 11), pl.ds(0, 32)] = correlate_z(w2, 11, z2)
    top = lambda i: v2[i + 1, pl.ds(0, 32)]
    for a in range(-1, 9):
        if a >= 0:
            mid[2 * a + 1] = mid_in[2 * a + 1] + (0.75 * top(a) + 0.125 * (top(a - 1) + top(a + 1)))
        if a < 8:
            mid[2 * a + 2] = mid_in[2 * a + 2] + 0.5 * (top(a) + top(a + 1))
    for a in range(16):
        fine[2 * a] = 0.75 * mid[a + 1] + 0.125 * (mid[a] + mid[a + 2])
        fine[2 * a + 1] = 0.5 * (mid[a + 1] + mid[a + 2])
    copies = []
    for q in range(4):
        rows = pl.ds(8 * q, 8)
        high, low = halves(fine[rows].reshape(256, 128))
        done[rows] = direct[rows] + dot(jnp.concatenate([high, low], 1), up1[...]).reshape(8, 32, 256)
        copies.append(pltpu.make_async_copy(done.at[rows], out.at[rows], sems.at[q]))
        copies[q].start()
    for copy in copies:
        copy.wait()


def section(table, own, left, right, base, at):
    b = left[pl.ds(base, 48)][10 * at:10 * at + 16]
    a = right[pl.ds(base, 48)][10 * at:10 * at + 16]
    high, low = halves(jnp.concatenate([own, b, a], 0))
    return dot(table[...], jnp.concatenate([high, low, high], 0))


def inner_kernel(taps, c, left, right, y0, z0h, z0l, out, v, wh, wl):
    @pl.loop(0, 8, unroll=4)
    def _(q):
        base = pl.multiple_of(40 * q, 8)
        for at in range(4):
            i = 4 * q + at
            v[i] = section(y0, c[i], left, right, base, at)

    @pl.loop(0, 4)
    def _(g):
        for member in range(3):
            rows = pl.ds(pl.multiple_of(32 * member + 8 * g, 8), 8)
            scale = [taps[0, member, k] for k in range(TAPS)]
            for h in range(2):
                lanes = pl.ds(128 * h, 128)
                for base in range(0, 32, 8):
                    sums = [None] * 8
                    for i in range(max(base - RADIUS, 0), min(base + 8 + RADIUS, 32)):
                        value = v[i, rows, lanes]
                        for m in range(8):
                            k = i - base - m + RADIUS
                            if 0 <= k < TAPS:
                                term = scale[k] * value
                                sums[m] = term if sums[m] is None else sums[m] + term
                    for m in range(0, 8, 2):
                        high, low = halves(jnp.concatenate([sums[m], sums[m + 1]], 0))
                        at = (pl.ds(8 * (base + m), 16), pl.ds(256 * member + 128 * h, 128))
                        wh[at] = high
                        wl[at] = low
        cols = pl.ds(pl.multiple_of(8 * g, 8), 8)
        total = dot(wh[...], z0h[...]) + dot(wl[...], z0h[...]) + dot(wh[...], z0l[...])
        out[:, cols] = total.reshape(32, 8, 256)


def finest_kernel(taps, before, after, left, right, y0, z0h, z0l, inner, out, v, wh, wl):
    for i in range(20):
        own = before[pl.ds(32 * i, 32)] if i < 10 else after[pl.ds(32 * (i - 10), 32)]
        b = left[pl.ds(10 * i, 16)]
        a = right[pl.ds(10 * i, 16)]
        high, low = halves(jnp.concatenate([own, b, a], 0))
        v[i] = dot(y0[...], jnp.concatenate([high, low, high], 0))

    @pl.loop(0, 4, unroll=4)
    def _(g):
        for member in range(3):
            rows = pl.ds(pl.multiple_of(32 * member + 8 * g, 8), 8)
            scale = [taps[0, member, k] for k in range(TAPS)]
            for h in range(2):
                lanes = pl.ds(128 * h, 128)
                sums = [None] * 20
                for r in range(20):
                    value = v[r, rows, lanes]
                    for m in range(10):
                        k = r - m if r < 10 else 20 + r - 10 - m
                        at = m if r < 10 else 10 + m
                        if r < 10 and m > r or r >= 10 and m < r - 10:
                            continue
                        term = scale[k] * value
                        sums[at] = term if sums[at] is None else sums[at] + term
                for m in range(0, 20, 2):
                    high, low = halves(jnp.concatenate([sums[m], sums[m + 1]], 0))
                    at = (pl.ds(pl.multiple_of(160 * g, 32) + 8 * m, 16), pl.ds(256 * member + 128 * h, 128))
                    wh[at] = high
                    wl[at] = low

    total = dot(wh[...], z0h[...]) + dot(wl[...], z0h[...]) + dot(wh[...], z0l[...])
    for g in range(4):
        cols = pl.ds(8 * g, 8)
        piece = total[160 * g:160 * g + 160].reshape(20, 8, 256)
        out[pl.ds(0, 10), cols] = inner[pl.ds(0, 10), cols] + piece[:10]
        out[pl.ds(10, 12), cols] = inner[pl.ds(10, 12), cols]
        out[pl.ds(22, 10), cols] = inner[pl.ds(22, 10), cols] + piece[10:]


def call(kernel, outs, scratch=(), scalars=0, count=0, flops=0, moved=0, name=None, sems=0, far=False):
    vmem = pl.BlockSpec(memory_space=pltpu.VMEM)
    smem = pl.BlockSpec(memory_space=pltpu.SMEM)
    hbm = pl.BlockSpec(memory_space=pltpu.HBM)
    shapes = [jax.ShapeDtypeStruct(*o) for o in outs]
    return pl.pallas_call(
        kernel,
        out_shape=shapes,
        in_specs=[smem] * scalars + [vmem] * (count - scalars),
        out_specs=[hbm if far else vmem] * len(shapes),
        scratch_shapes=[pltpu.VMEM(*s) for s in scratch] + [pltpu.SemaphoreType.DMA((sems,))] * (sems > 0),
        compiler_params=pltpu.CompilerParams(vmem_limit_bytes=VMEM_LIMIT),
        cost_estimate=pl.CostEstimate(flops=flops, bytes_accessed=moved, transcendentals=0),
        name=name,
    )


def shift(x, axis, by):
    n = lax.axis_size(axis)
    return lax.ppermute(x, axis, [(i, (i + by) % n) for i in range(n)])


def body(charges, kernel_taps):
    taps = kernel_taps
    l1, l2, s_up, s_down, last, first, o_up, o_down = call(
        restrict_kernel,
        [((18, 24, 128), F32), ((6, 16, 128), F32), ((288, 128), F32), ((288, 128), F32),
         ((320, 256), F32), ((320, 256), F32), ((328, 256), F32), ((328, 256), F32)],
        [((18, 24, 256), F32), ((12, 16, 128), F32)], 0, 1, 10**8, 2 * 10**6, name="restrict",
    )(charges)
    x_left = shift(s_up, "gx", 1)
    x_right = shift(s_down, "gx", -1)
    taps, l1 = lax.optimization_barrier((taps, l1))
    y0, y1, y2, z0h, z0l, z1, z2, up1 = call(
        matrices_kernel,
        [((96, 192), BF), ((96, 144), BF), ((96, 144), BF), ((768, 256), BF), ((768, 256), BF),
         ((768, 256), BF), ((768, 256), BF), ((256, 256), BF)],
        [], 1, 1, 10**8, 4 * 10**6, name="matrices",
    )(taps)
    own_left = shift(o_up, "gy", 1)
    own_right = shift(o_down, "gy", -1)
    x_left, x_right, y0 = lax.optimization_barrier((x_left, x_right, y0))
    c_up, c_down = call(
        face_x_kernel, [((344, 256), F32), ((344, 256), F32)], [], 0, 4, 2 * 10**10, 2 * 10**6, name="face_x",
    )(last, first, x_left, x_right)
    before = shift(c_up, "gx", 1)
    after = shift(c_down, "gx", -1)
    x_left, x_right, c_up = lax.optimization_barrier((x_left, x_right, c_up))
    l1x, g_up, g_down = call(
        gather_fine_kernel, [((38, 24, 128), F32), ((456, 128), F32), ((456, 128), F32)],
        [], 0, 3, 2 * 10**10, 2 * 10**6, name="gather_fine",
    )(l1, x_left, x_right)
    fine_left = shift(g_up, "gy", 1)
    fine_right = shift(g_down, "gy", -1)
    y0, g_up, g_down = lax.optimization_barrier((y0, g_up, g_down))
    inner, = call(
        inner_kernel, [((32, 32, 256), F32)],
        [((32, 96, 256), F32), ((256, 768), BF), ((256, 768), BF)], 1, 7, 2 * 10**9, 6 * 10**6, name="inner",
    )(taps, charges, own_left, own_right, y0, z0h, z0l)
    before, after, inner, fine_left, fine_right = lax.optimization_barrier(
        (before, after, inner, fine_left, fine_right)
    )
    l2x, f_up, f_down, t_up, t_down = call(
        gather_top_kernel,
        [((16, 16, 128), F32), ((296, 256), F32), ((296, 256), F32), ((80, 128), F32), ((80, 128), F32)],
        [], 0, 5, 10**6, 5 * 10**6, name="gather_top",
    )(before, after, l2, x_left, x_right)
    left = shift(f_up, "gy", 1)
    right = shift(f_down, "gy", -1)
    left2 = shift(t_up, "gy", 2)
    right2 = shift(t_down, "gy", -2)
    l1x, f_up, f_down = lax.optimization_barrier((l1x, f_up, f_down))
    mid, = call(
        fine_level_kernel, [((18, 32, 128), F32)],
        [((38, 48, 128), F32), ((38, 96, 128), F32), ((18, 96, 128), F32)],
        1, 6, 4 * 10**8, 4 * 10**6, name="fine_level",
    )(taps, l1x, fine_left, fine_right, y1, z1)
    left, right, mid = lax.optimization_barrier((left, right, mid))
    direct, = call(
        finest_kernel, [((32, 32, 256), F32)],
        [((20, 96, 256), F32), ((640, 768), BF), ((640, 768), BF)],
        1, 9, 2 * 10**9, 6 * 10**6, name="finest",
    )(taps, before, after, left, right, y0, z0h, z0l, inner)
    result, = call(
        upper_kernel, [((32, 32, 256), F32)],
        [((16, 48, 128), F32), ((32, 96, 128), F32), ((11, 96, 128), F32), ((18, 32, 128), F32),
         ((32, 32, 128), F32), ((32, 32, 256), F32)],
        1, 11, 4 * 10**8, 4 * 10**6, name="upper", sems=4, far=True,
    )(taps, l2x, left, right, left2, right2, y2, z2, up1, mid, direct)
    return result


def solution(mesh):
    return jax.shard_map(
        body,
        mesh=mesh,
        in_specs=(P("gx", "gy", None), P()),
        out_specs=P("gx", "gy", None),
        check_vma=False,
    )
```

```python
import jax
import jax.numpy as jnp
from jax import lax
from jax.experimental import pallas as pl
from jax.experimental.pallas import tpu as pltpu
from jax.sharding import PartitionSpec as P

SPLINE = (0.125, 0.5, 0.75, 0.5, 0.125)
RADIUS = 10
TAPS = 21
BF = jnp.bfloat16
F32 = jnp.float32
VMEM_LIMIT = 48 * 1024 * 1024


def halves(x):
    high = x.astype(BF)
    return high, (x - high.astype(F32)).astype(BF)


def dot(a, b):
    return jnp.dot(a, b, preferred_element_type=F32)


def spline_sum(read, center, low, high):
    total = None
    for k in range(-2, 3):
        if low <= 2 * center + k <= high:
            term = SPLINE[k + 2] * read(2 * center + k)
            total = term if total is None else total + term
    return total


def matrices_kernel(taps, y0, y1, y2, z0h, z0l, z1, z2, up1):
    def iota(shape, dim):
        return lax.broadcasted_iota(jnp.int32, shape, dim)

    def pick(level, member, offsets):
        table = jnp.zeros(offsets.shape, F32)
        for k in range(TAPS):
            table = jnp.where(offsets == k, taps[level, member, k], table)
        return table

    def cycle(level, member, length):
        offsets = (iota((length, length), 0) - iota((length, length), 1) + RADIUS) & (length - 1)
        return pick(level, member, offsets)

    def spread(lanes, width, pieces):
        cols = lanes
        for _ in range(2):
            cols = jnp.where(cols >= width, cols - width, cols)
        place = jnp.full(lanes.shape, -99, jnp.int32)
        for begin, end, position in pieces:
            place = jnp.where((cols >= begin) & (cols < end), cols - begin + position, place)
        return place

    def put(out, rows, table, width):
        high, low = halves(table)
        out[rows] = jnp.where(iota(table.shape, 1) < 2 * width, high.astype(F32), low.astype(F32)).astype(BF)

    def block(out, base, table, count):
        high, low = halves(table)
        zero = jnp.zeros((128, 128), BF)
        if count < 128:
            for at in (base, base + 128):
                out[pl.ds(at + count, 128 - count)] = jnp.zeros((128 - count, 256), BF)
        out[pl.ds(base, count), pl.ds(0, 128)] = high
        out[pl.ds(base, count), pl.ds(128, 128)] = low
        out[pl.ds(base + 128, count), pl.ds(0, 128)] = high
        out[pl.ds(base + 128, count), pl.ds(128, 128)] = zero[:count]

    def product(weights, table):
        high, low = halves(table)
        return dot(weights, high) + dot(weights, low)

    place0 = spread(iota((32, 192), 1), 64, ((0, 32, 0), (32, 42, -10), (48, 58, 32))) - iota((32, 192), 0) + RADIUS
    place1 = spread(iota((32, 144), 1), 48, ((0, 12, -11), (12, 30, -1), (30, 42, 15)))
    place1 = place1 - (iota((32, 144), 0) - 1) + RADIUS
    place2 = spread(iota((32, 144), 1), 48, ((0, 11, -1), (16, 27, -9), (27, 38, 7), (38, 43, -11), (43, 48, 15)))
    place2 = place2 - (iota((32, 144), 0) - 1) + RADIUS
    columns = iota((32, 32), 1) - 1
    lift1 = jnp.where(columns < 17, spline_of(iota((32, 32), 0) - 2 * columns), 0.0).astype(BF)
    lift2 = jnp.where(columns < 10, spline_of(iota((32, 32), 0) - 1 - 2 * columns), 0.0).astype(BF)
    lift2 = dot(lift1, lift2).astype(BF)
    up2 = cyclic_iota((64, 128), 0, 1, 128).astype(BF)
    up1[pl.ds(0, 128)] = cyclic_iota((128, 256), 0, 1, 256).astype(BF)
    up1[pl.ds(128, 128)] = cyclic_iota((128, 256), 0, 1, 256).astype(BF)
    for member in range(3):
        rows = pl.ds(32 * member, 32)
        put(y0, rows, pick(0, member, place0), 64)
        put(y1, rows, product(lift1, pick(1, member, place1)), 48)
        put(y2, rows, product(lift2, pick(2, member, place2)), 48)
        high, low = halves(cycle(0, member, 256))
        z0h[pl.ds(256 * member, 256)] = high
        z0l[pl.ds(256 * member, 256)] = low
        block(z1, 256 * member, cycle(1, member, 128), 128)
        high, low = halves(cycle(2, member, 64))
        block(z2, 256 * member, dot(high, up2) + dot(low, up2), 64)


def spline_iota(shape, offset, coarse_dim, fine_dim, keep=None):
    fine = lax.broadcasted_iota(jnp.int32, shape, fine_dim)
    coarse = lax.broadcasted_iota(jnp.int32, shape, coarse_dim)
    delta = fine - 2 * coarse + offset
    if keep is not None:
        delta = jnp.where(coarse < keep, delta, 99)
    return spline_of(delta)


def spline_of(delta):
    far = jnp.abs(delta)
    return jnp.where(far == 0, 0.75, jnp.where(far == 1, 0.5, jnp.where(far == 2, 0.125, 0.0)))


def cyclic_iota(shape, coarse_dim, fine_dim, fine_len):
    fine = lax.broadcasted_iota(jnp.int32, shape, fine_dim)
    coarse = lax.broadcasted_iota(jnp.int32, shape, coarse_dim)
    return spline_of(((fine - 2 * coarse + 2) & (fine_len - 1)) - 2)


def restrict_kernel(c, l1, l2, up1, down1, last, first, face_up, face_down, s1, s2):
    ry = spline_iota((24, 32), 2, 0, 1, 18).astype(BF)
    for i in range(-1, 17):
        high, low = halves(spline_sum(lambda r: c[r], i, 0, 31))
        s1[i + 1] = dot(ry, high) + dot(ry, low)
    for i in range(32):
        face_up[pl.ds(10 * i, 10)] = c[i, 22:32]
        face_down[pl.ds(10 * i, 10)] = c[i, 0:10]
    face_up[pl.ds(320, 8)] = jnp.zeros((8, 256), F32)
    face_down[pl.ds(320, 8)] = jnp.zeros((8, 256), F32)
    for r in range(10):
        last[pl.ds(32 * r, 32)] = c[22 + r]
        first[pl.ds(32 * r, 32)] = c[r]
    rz = cyclic_iota((256, 128), 1, 0, 256).astype(BF)
    high, low = halves(s1[...].reshape(18 * 24, 256))
    l1[...] = (dot(high, rz) + dot(low, rz)).reshape(18, 24, 128)
    ry2 = spline_iota((16, 24), 1, 0, 1, 11).astype(BF)
    for i in range(-1, 10):
        high, low = halves(spline_sum(lambda r: l1[r + 1], i, -1, 16))
        s2[i + 1] = dot(ry2, high) + dot(ry2, low)
    s2[11] = jnp.zeros((16, 128), F32)
    near = s2[pl.ds(0, 6)].reshape(96, 128)
    far = s2[pl.ds(6, 6)].reshape(96, 128)
    lanes = lax.broadcasted_iota(jnp.int32, (128, 128), 1)
    both = spline_of(((lax.broadcasted_iota(jnp.int32, (128, 128), 0) - 2 * (lanes & 63) + 2) & 127) - 2)
    total = jnp.zeros((96, 128), F32)
    for part, upper in ((near, False), (far, True)):
        weights = jnp.where((lanes >= 64) == upper, both, 0.0).astype(BF)
        high, low = halves(part)
        total = total + dot(high, weights) + dot(low, weights)
    total = total.reshape(6, 16, 128)
    l2[...] = total
    up1[pl.ds(64, 8)] = jnp.zeros((8, 128), F32)
    down1[pl.ds(64, 8)] = jnp.zeros((8, 128), F32)
    for j in range(6):
        up1[pl.ds(11 * j, 11)] = total[j, :11]
        down1[pl.ds(11 * j, 11)] = total[j, :11]
    for r in range(12):
        up1[pl.ds(72 + 18 * r, 18)] = l1[6 + r, :18]
        down1[pl.ds(72 + 18 * r, 18)] = l1[r, :18]


def paired(base, count, j):
    return (pl.ds(base + count * (j // 2), count), pl.ds(128 * (j % 2), 128))


def face_x_kernel(last, first, left, right, up, down):
    up[pl.ds(0, 320)] = last[...]
    down[pl.ds(0, 320)] = first[...]
    lower = lax.broadcasted_iota(jnp.int32, (11, 128), 1) < 64
    for p in range(3):
        even = 2 * p
        odd = min(even + 1, 4)
        a = left[pl.ds(11 * even, 11)]
        b = left[pl.ds(11 * odd, 11)]
        up[paired(320, 11, p)] = jnp.where(lower, pltpu.roll(a, 64, 1), b)
        a = right[pl.ds(11 * even, 11)]
        b = right[pl.ds(11 * odd, 11)]
        down[paired(320, 11, p)] = jnp.where(lower, a, pltpu.roll(b, 64, 1))


def gather_fine_kernel(l1, left, right, l1x, up, down):
    for i in range(38):
        if i < 12:
            l1x[i, :18] = left[pl.ds(72 + 18 * i, 18)]
            l1x[i, pl.ds(18, 6)] = jnp.zeros((6, 128), F32)
        elif i >= 26:
            l1x[i, :18] = right[pl.ds(72 + 18 * (i - 26), 18)]
            l1x[i, pl.ds(18, 6)] = jnp.zeros((6, 128), F32)
        if 10 <= i < 12 or 26 <= i < 28:
            l1x[i] = l1x[i] + l1[i - 10]
        elif 12 <= i < 26:
            l1x[i] = l1[i - 10]
    for i in range(38):
        up[pl.ds(12 * i, 12)] = l1x[i, 6:18]
        down[pl.ds(12 * i, 12)] = l1x[i, 0:12]


def gather_top_kernel(before, after, l2, left, right, l2x, up, down, up2, down2):
    for i in range(20):
        row = before[pl.ds(32 * i, 32)] if i < 10 else after[pl.ds(32 * (i - 10), 32)]
        up[pl.ds(10 * i, 10)] = row[22:32]
        down[pl.ds(10 * i, 10)] = row[0:10]
    up[pl.ds(200, 8)] = jnp.zeros((8, 256), F32)
    down[pl.ds(200, 8)] = jnp.zeros((8, 256), F32)
    lanes = lax.broadcasted_iota(jnp.int32, (11, 128), 1)
    lower = lanes < 64
    rolled = lambda x: pltpu.roll(x, 64, 1)
    for j in range(16):
        low = []
        high = []
        if j < 5:
            slab = before[paired(320, 11, j // 2)]
            low.append(slab if j % 2 == 0 else rolled(slab))
        if 2 <= j < 8:
            low.append(left[pl.ds(11 * (j - 2), 11)])
        if 8 <= j < 13:
            low.append(rolled(left[pl.ds(11 * (j - 8), 11)]))
        if j >= 10:
            low.append(l2[j - 10, :11])
        if j < 5:
            high.append(l2[j, :11])
        if 2 <= j < 8:
            high.append(rolled(right[pl.ds(11 * (j - 2), 11)]))
        if 8 <= j < 13:
            high.append(right[pl.ds(11 * (j - 8), 11)])
        if 10 <= j < 15:
            slab = after[paired(320, 11, (j - 10) // 2)]
            high.append(rolled(slab) if j % 2 == 0 else slab)
        row = jnp.where(lower, sum(low, jnp.zeros((11, 128), F32)), sum(high, jnp.zeros((11, 128), F32)))
        l2x[j, :11] = row
        l2x[j, pl.ds(11, 5)] = jnp.zeros((5, 128), F32)
        up[paired(208, 11, j)] = row
        down[paired(208, 11, j)] = row
        up2[pl.ds(5 * j, 5)] = row[6:11]
        down2[pl.ds(5 * j, 5)] = row[0:5]


def correlate_x(taps, level, v, w, count, many):
    @pl.loop(0, 12, unroll=4 if level == 1 else 12)
    def _(g):
        member = g // 4
        rows = pl.ds(pl.multiple_of(8 * g, 8), 8)
        scale = [taps[level, member, k] for k in range(TAPS)]
        for base in range(0, count, many):
            sums = [None] * many
            for i in range(base, base + many + TAPS - 1):
                value = v[i, rows]
                for m in range(many):
                    k = i - base - m
                    if 0 <= k < TAPS:
                        term = scale[k] * value
                        sums[m] = term if sums[m] is None else sums[m] + term
            for m in range(many):
                w[base + m, rows] = sums[m]


def correlate_z(w, count, table):
    total = jnp.zeros((count * 32, 256), F32)
    for member in range(3):
        high, low = halves(w[:, pl.ds(32 * member, 32)].reshape(count * 32, 128))
        total = total + dot(jnp.concatenate([high, low], 1), table[pl.ds(256 * member, 256)])
    return (total[:, :128] + total[:, 128:]).reshape(count, 32, 128)


def fine_level_kernel(taps, l1x, left, right, y1, z1, mid, f1, v1, w1):
    for i in range(38):
        f1[i, pl.ds(0, 12)] = left[pl.ds(12 * i, 12)]
        f1[i, pl.ds(12, 18)] = l1x[i, :18]
        f1[i, pl.ds(30, 12)] = right[pl.ds(12 * i, 12)]
        f1[i, pl.ds(42, 6)] = jnp.zeros((6, 128), F32)

    @pl.loop(0, 38, unroll=19)
    def _(i):
        high, low = halves(f1[i])
        v1[i] = dot(y1[...], jnp.concatenate([high, low, high], 0))

    correlate_x(taps, 1, v1, w1, 18, 9)
    mid[...] = correlate_z(w1, 18, z1)


def upper_kernel(taps, l2x, left, right, left2, right2, y2, z2, up1, mid_in, direct, out,
                 f2, v2, w2, mid, fine, done, sems):
    for j in range(16):
        f2[j, pl.ds(0, 16)] = l2x[j]
        f2[j, pl.ds(16, 11)] = left[paired(208, 11, j)]
        f2[j, pl.ds(27, 11)] = right[paired(208, 11, j)]
        f2[j, pl.ds(38, 5)] = left2[pl.ds(5 * j, 5)]
        f2[j, pl.ds(43, 5)] = right2[pl.ds(5 * j, 5)]

    @pl.loop(0, 16, unroll=16)
    def _(j):
        high, low = halves(f2[j])
        v = dot(y2[...], jnp.concatenate([high, low, high], 0))
        v2[j] = v
        v2[16 + j] = pltpu.roll(v, 64, 1)

    correlate_x(taps, 2, v2, w2, 11, 11)
    v2[pl.ds(0, 11), pl.ds(0, 32)] = correlate_z(w2, 11, z2)
    top = lambda i: v2[i + 1, pl.ds(0, 32)]
    for a in range(-1, 9):
        if a >= 0:
            mid[2 * a + 1] = mid_in[2 * a + 1] + (0.75 * top(a) + 0.125 * (top(a - 1) + top(a + 1)))
        if a < 8:
            mid[2 * a + 2] = mid_in[2 * a + 2] + 0.5 * (top(a) + top(a + 1))
    for a in range(16):
        fine[2 * a] = 0.75 * mid[a + 1] + 0.125 * (mid[a] + mid[a + 2])
        fine[2 * a + 1] = 0.5 * (mid[a + 1] + mid[a + 2])
    copies = []
    for q in range(8):
        rows = pl.ds(4 * q, 4)
        high, low = halves(fine[rows].reshape(128, 128))
        done[rows] = direct[rows] + dot(jnp.concatenate([high, low], 1), up1[...]).reshape(4, 32, 256)
        copies.append(pltpu.make_async_copy(done.at[rows], out.at[rows], sems.at[q]))
        copies[q].start()
    for copy in copies:
        copy.wait()


def section(table, own, left, right, base, at):
    b = left[pl.ds(base, 48)][10 * at:10 * at + 16]
    a = right[pl.ds(base, 48)][10 * at:10 * at + 16]
    high, low = halves(jnp.concatenate([own, b, a], 0))
    return dot(table[...], jnp.concatenate([high, low, high], 0))


def inner_kernel(taps, c, left, right, y0, z0h, z0l, out, v, wh, wl):
    @pl.loop(0, 8, unroll=4)
    def _(q):
        base = pl.multiple_of(40 * q, 8)
        for at in range(4):
            i = 4 * q + at
            v[i] = section(y0, c[i], left, right, base, at)

    @pl.loop(0, 4)
    def _(g):
        for member in range(3):
            rows = pl.ds(pl.multiple_of(32 * member + 8 * g, 8), 8)
            scale = [taps[0, member, k] for k in range(TAPS)]
            for h in range(2):
                lanes = pl.ds(128 * h, 128)
                for base in range(0, 32, 8):
                    sums = [None] * 8
                    for i in range(max(base - RADIUS, 0), min(base + 8 + RADIUS, 32)):
                        value = v[i, rows, lanes]
                        for m in range(8):
                            k = i - base - m + RADIUS
                            if 0 <= k < TAPS:
                                term = scale[k] * value
                                sums[m] = term if sums[m] is None else sums[m] + term
                    for m in range(0, 8, 2):
                        high, low = halves(jnp.concatenate([sums[m], sums[m + 1]], 0))
                        at = (pl.ds(8 * (base + m), 16), pl.ds(256 * member + 128 * h, 128))
                        wh[at] = high
                        wl[at] = low
        cols = pl.ds(pl.multiple_of(8 * g, 8), 8)
        total = dot(wh[...], z0h[...]) + dot(wl[...], z0h[...]) + dot(wh[...], z0l[...])
        out[:, cols] = total.reshape(32, 8, 256)


def finest_kernel(taps, before, after, left, right, y0, z0h, z0l, inner, out, v, wh, wl):
    for i in range(20):
        own = before[pl.ds(32 * i, 32)] if i < 10 else after[pl.ds(32 * (i - 10), 32)]
        b = left[pl.ds(10 * i, 16)]
        a = right[pl.ds(10 * i, 16)]
        high, low = halves(jnp.concatenate([own, b, a], 0))
        v[i] = dot(y0[...], jnp.concatenate([high, low, high], 0))

    @pl.loop(0, 4, unroll=4)
    def _(g):
        for member in range(3):
            rows = pl.ds(pl.multiple_of(32 * member + 8 * g, 8), 8)
            scale = [taps[0, member, k] for k in range(TAPS)]
            for h in range(2):
                lanes = pl.ds(128 * h, 128)
                sums = [None] * 20
                for r in range(20):
                    value = v[r, rows, lanes]
                    for m in range(10):
                        k = r - m if r < 10 else 20 + r - 10 - m
                        at = m if r < 10 else 10 + m
                        if r < 10 and m > r or r >= 10 and m < r - 10:
                            continue
                        term = scale[k] * value
                        sums[at] = term if sums[at] is None else sums[at] + term
                for m in range(0, 20, 2):
                    high, low = halves(jnp.concatenate([sums[m], sums[m + 1]], 0))
                    at = (pl.ds(pl.multiple_of(160 * g, 32) + 8 * m, 16), pl.ds(256 * member + 128 * h, 128))
                    wh[at] = high
                    wl[at] = low

    total = dot(wh[...], z0h[...]) + dot(wl[...], z0h[...]) + dot(wh[...], z0l[...])
    for g in range(4):
        cols = pl.ds(8 * g, 8)
        piece = total[160 * g:160 * g + 160].reshape(20, 8, 256)
        out[pl.ds(0, 10), cols] = inner[pl.ds(0, 10), cols] + piece[:10]
        out[pl.ds(10, 12), cols] = inner[pl.ds(10, 12), cols]
        out[pl.ds(22, 10), cols] = inner[pl.ds(22, 10), cols] + piece[10:]


def call(kernel, outs, scratch=(), scalars=0, count=0, flops=0, moved=0, name=None, sems=0, far=False):
    vmem = pl.BlockSpec(memory_space=pltpu.VMEM)
    smem = pl.BlockSpec(memory_space=pltpu.SMEM)
    hbm = pl.BlockSpec(memory_space=pltpu.HBM)
    shapes = [jax.ShapeDtypeStruct(*o) for o in outs]
    return pl.pallas_call(
        kernel,
        out_shape=shapes,
        in_specs=[smem] * scalars + [vmem] * (count - scalars),
        out_specs=[hbm if far else vmem] * len(shapes),
        scratch_shapes=[pltpu.VMEM(*s) for s in scratch] + [pltpu.SemaphoreType.DMA((sems,))] * (sems > 0),
        compiler_params=pltpu.CompilerParams(vmem_limit_bytes=VMEM_LIMIT),
        cost_estimate=pl.CostEstimate(flops=flops, bytes_accessed=moved, transcendentals=0),
        name=name,
    )


def shift(x, axis, by):
    n = lax.axis_size(axis)
    return lax.ppermute(x, axis, [(i, (i + by) % n) for i in range(n)])


def body(charges, kernel_taps):
    taps = kernel_taps
    l1, l2, s_up, s_down, last, first, o_up, o_down = call(
        restrict_kernel,
        [((18, 24, 128), F32), ((6, 16, 128), F32), ((288, 128), F32), ((288, 128), F32),
         ((320, 256), F32), ((320, 256), F32), ((328, 256), F32), ((328, 256), F32)],
        [((18, 24, 256), F32), ((12, 16, 128), F32)], 0, 1, 10**8, 2 * 10**6, name="restrict",
    )(charges)
    x_left = shift(s_up, "gx", 1)
    x_right = shift(s_down, "gx", -1)
    taps, l1 = lax.optimization_barrier((taps, l1))
    y0, y1, y2, z0h, z0l, z1, z2, up1 = call(
        matrices_kernel,
        [((96, 192), BF), ((96, 144), BF), ((96, 144), BF), ((768, 256), BF), ((768, 256), BF),
         ((768, 256), BF), ((768, 256), BF), ((256, 256), BF)],
        [], 1, 1, 10**8, 4 * 10**6, name="matrices",
    )(taps)
    own_left = shift(o_up, "gy", 1)
    own_right = shift(o_down, "gy", -1)
    x_left, x_right, y0 = lax.optimization_barrier((x_left, x_right, y0))
    c_up, c_down = call(
        face_x_kernel, [((344, 256), F32), ((344, 256), F32)], [], 0, 4, 2 * 10**10, 2 * 10**6, name="face_x",
    )(last, first, x_left, x_right)
    before = shift(c_up, "gx", 1)
    after = shift(c_down, "gx", -1)
    x_left, x_right, c_up = lax.optimization_barrier((x_left, x_right, c_up))
    l1x, g_up, g_down = call(
        gather_fine_kernel, [((38, 24, 128), F32), ((456, 128), F32), ((456, 128), F32)],
        [], 0, 3, 2 * 10**10, 2 * 10**6, name="gather_fine",
    )(l1, x_left, x_right)
    fine_left = shift(g_up, "gy", 1)
    fine_right = shift(g_down, "gy", -1)
    y0, g_up, g_down = lax.optimization_barrier((y0, g_up, g_down))
    inner, = call(
        inner_kernel, [((32, 32, 256), F32)],
        [((32, 96, 256), F32), ((256, 768), BF), ((256, 768), BF)], 1, 7, 2 * 10**9, 6 * 10**6, name="inner",
    )(taps, charges, own_left, own_right, y0, z0h, z0l)
    before, after, inner, fine_left, fine_right = lax.optimization_barrier(
        (before, after, inner, fine_left, fine_right)
    )
    l2x, f_up, f_down, t_up, t_down = call(
        gather_top_kernel,
        [((16, 16, 128), F32), ((296, 256), F32), ((296, 256), F32), ((80, 128), F32), ((80, 128), F32)],
        [], 0, 5, 10**6, 5 * 10**6, name="gather_top",
    )(before, after, l2, x_left, x_right)
    left = shift(f_up, "gy", 1)
    right = shift(f_down, "gy", -1)
    left2 = shift(t_up, "gy", 2)
    right2 = shift(t_down, "gy", -2)
    l1x, f_up, f_down = lax.optimization_barrier((l1x, f_up, f_down))
    mid, = call(
        fine_level_kernel, [((18, 32, 128), F32)],
        [((38, 48, 128), F32), ((38, 96, 128), F32), ((18, 96, 128), F32)],
        1, 6, 4 * 10**8, 4 * 10**6, name="fine_level",
    )(taps, l1x, fine_left, fine_right, y1, z1)
    left, right, mid = lax.optimization_barrier((left, right, mid))
    direct, = call(
        finest_kernel, [((32, 32, 256), F32)],
        [((20, 96, 256), F32), ((640, 768), BF), ((640, 768), BF)],
        1, 9, 2 * 10**9, 6 * 10**6, name="finest",
    )(taps, before, after, left, right, y0, z0h, z0l, inner)
    result, = call(
        upper_kernel, [((32, 32, 256), F32)],
        [((16, 48, 128), F32), ((32, 96, 128), F32), ((11, 96, 128), F32), ((18, 32, 128), F32),
         ((32, 32, 128), F32), ((32, 32, 256), F32)],
        1, 11, 4 * 10**8, 4 * 10**6, name="upper", sems=8, far=True,
    )(taps, l2x, left, right, left2, right2, y2, z2, up1, mid, direct)
    return result


def solution(mesh):
    return jax.shard_map(
        body,
        mesh=mesh,
        in_specs=(P("gx", "gy", None), P()),
        out_specs=P("gx", "gy", None),
        check_vma=False,
    )
```
